128 devices in a mesh: tiles: 128 (over x, z, y, core).
Axes of the slice: x: 4, y: 4, z: 4, core: 2. Of those that a mesh axis runs over, the one named last changes fastest.
Arguments:
- water_depth: float32 [512, 128, 128], P('tiles'), may hold values from 0.05 to 2
- velocity: float32 [512, 2, 128, 128], P('tiles'), may hold values from -22 to 22
- aquifer_head: float32 [512, 128, 128], P('tiles'), may hold values from -3 to -0.5
- terrain: float32 [512, 128, 128], P('tiles'), may hold values from -1.5 to 1.5
- leakance: float32 [512, 128, 128], P('tiles'), may hold values from 0.05 to 0.5
- diffusivity: float32 [512, 128, 128], P('tiles'), may hold values from 0.1 to 1
- tile_wet: int32 [512], replicated, may hold values from 0 to 1, as said below
- neighbours: int32 [512, 4], replicated, may hold values from -1 to 511, as said below
- destination: int32 [512], replicated, may hold values from 0 to 511, as said below
Outputs:
- flood_depth: float32 [512, 128, 128], P('tiles')
- flood_discharge: float32 [512, 2, 128, 128], P('tiles')
- water_table: float32 [512, 128, 128], P('tiles')
The draws below stay inside these ranges and needn't reach their ends.
Inputs may be any that keep to these rules, and one draw needn't show every extreme that they name: `tile_wet`: 1 marks a tile that holds water. `neighbours`: slot t lies in row t // 16 of the basin's tile layout, at column t % 16 in even rows and 15 - t % 16 in odd rows. Entry k (west, east, south, north) names the slot of the tile beside it in that direction, or -1 where there is none or where either of the two tiles is dry. The relation is mutual. `destination`: A permutation. Slot s belongs to device s // 4. Tiles move only between neighbouring devices, by swaps: between devices k and k + 1 the same number of tiles pass each way, at most 2, exactly 2 between devices 0 and 1.
All inputs are finite; a program needn't handle non-finite values.
Results may differ from the reference program's by a relative error of at most 0.00002.
Values sent between devices are 32-bit elements; how exact they have to be, the bound alone decides.
A program may use at most 128 MiB of HBM per device.

```python
import math
import jax
import jax.numpy as jnp
from jax import lax

TILE = 128
TPD = 4
W = 16
MOVE = 2
STEPS = 4
TOTAL = 512


def wet_layout(key):
    rows_count = TOTAL // W
    levels = jax.random.randint(jax.random.fold_in(key, 11), (rows_count, 1), 0, 9)
    levels = levels.at[rows_count - 1].set(8)
    levels = levels.at[0].set(8)
    levels = levels.at[1].set(8)
    rolls = jax.random.randint(jax.random.fold_in(key, 12), (rows_count, W), 0, 8)
    grid_wet = (rolls < levels).astype(jnp.int32)
    return grid_wet.at[1, W - 1].set(0)


def layout_cells():
    all_slots = jnp.arange(TOTAL, dtype=jnp.int32)
    row_of = all_slots // W
    column_of = jnp.where(row_of % 2 == 0, all_slots % W, W - 1 - all_slots % W)
    return (row_of, column_of)


def draw_tile_wet(key, part):
    grid_wet = wet_layout(key)
    row_of, column_of = layout_cells()
    return grid_wet[row_of, column_of].astype(jnp.int32)


def draw_neighbours(key, part):
    grid_wet = wet_layout(key)
    rows_count = TOTAL // W
    row_of, column_of = layout_cells()
    other_row = row_of[:, None] + jnp.array([0, 0, -1, 1], jnp.int32)[None, :]
    other_column = column_of[:, None] + jnp.array([-1, 1, 0, 0], jnp.int32)[None, :]
    inside = (other_row >= 0) & (other_row < rows_count) & (other_column >= 0) & (other_column < W)
    safe_row = jnp.clip(other_row, 0, rows_count - 1)
    safe_column = jnp.clip(other_column, 0, W - 1)
    other_tile = safe_row * W + jnp.where(safe_row % 2 == 0, safe_column, W - 1 - safe_column)
    both_wet = (grid_wet[row_of, column_of][:, None] == 1) & (grid_wet[safe_row, safe_column] == 1)
    return jnp.where(inside & both_wet, other_tile, -1).astype(jnp.int32)


def draw_destination(key, part):
    key = jax.random.fold_in(key, 7)
    devices = TOTAL // TPD
    scores = jax.random.randint(jax.random.fold_in(key, 1), (devices, TPD), 0, 1 << 20) * TPD + jnp.arange(TPD, dtype=jnp.int32)[None, :]
    order = jnp.argsort(scores, axis=1).astype(jnp.int32)
    counts = jax.random.randint(jax.random.fold_in(key, 2), (devices,), 0, MOVE + 1)
    counts = counts.at[0].set(MOVE)
    positions = jnp.arange(MOVE, dtype=jnp.int32)
    device_ids = jnp.arange(devices, dtype=jnp.int32)
    valid = (positions[None, :] < counts[:, None]) & (device_ids[:, None] < devices - 1)
    leaving = device_ids[:, None] * TPD + order[:, :MOVE]
    next_ids = (device_ids + 1) % devices
    arriving = next_ids[:, None] * TPD + order[next_ids][:, MOVE:2 * MOVE]
    first = jnp.where(valid, arriving, leaving)
    second = jnp.where(valid, leaving, arriving)
    result = jnp.arange(TOTAL, dtype=jnp.int32)
    result = result.at[leaving.reshape(-1)].set(first.reshape(-1))
    result = result.at[arriving.reshape(-1)].set(second.reshape(-1))
    return result.astype(jnp.int32)


def draw_velocity(key, part):
    grid_wet = wet_layout(key)
    key = jax.random.fold_in(key, 9)
    row_of, column_of = layout_cells()
    wet_flags = grid_wet[row_of, column_of]
    all_slots = jnp.arange(TOTAL, dtype=jnp.int32)
    scores = jax.random.randint(jax.random.fold_in(key, 1), (TOTAL,), 0, 1 << 16) * TOTAL + all_slots
    scores = jnp.where(wet_flags == 1, scores, -1)
    chosen_slots = lax.top_k(scores, 2)[1]
    field_shape = (TOTAL, 2, TILE, TILE)
    unit_field = jax.random.uniform(jax.random.fold_in(key, 2), field_shape, jnp.float32, -1.0, 1.0)
    base_field = jnp.clip(0.3 * jax.random.normal(jax.random.fold_in(key, 3), field_shape, jnp.float32), -1.8, 1.8)
    first_strength = jax.random.uniform(jax.random.fold_in(key, 4), (1,), jnp.float32, 6.0, 10.0)
    strengths = jnp.concatenate([first_strength, jnp.zeros((1,), jnp.float32)])
    boosts = jnp.zeros((TOTAL,), jnp.float32).at[chosen_slots].set(strengths)
    return base_field + boosts[:, None, None, None] * unit_field


def shard_levels(key, dims, split, least, top_value):
    loudness, own = 1.0, jax.random.fold_in(key, 6)
    for dim, shards_of in split:
        heights = jnp.exp(jax.random.uniform(jax.random.fold_in(own, dim), (shards_of,), jnp.float32, least / len(split), top_value / len(split)))
        loudness = loudness * jnp.repeat(heights, dims[dim] // shards_of).reshape([-1 if axis == dim else 1 for axis in range(len(dims))])
    return loudness


def scatter_about(rng, dims, scale, bound, split=(), kind=jnp.bfloat16):
    values = scale * jax.random.normal(rng, dims, jnp.float32)
    if split:
        values = values * shard_levels(rng, dims, split, -0.22, 0.18)
    return jnp.clip(values, -bound, bound).astype(kind)


def setup_inputs(seed: int = 0) -> dict:
    streams_of = jax.random.split(jax.random.key(seed), 10)
    water_depth = jnp.clip(0.05 + 1.95 * jax.random.uniform(streams_of[0], (TOTAL, TILE, TILE), jnp.float32) ** shard_levels(streams_of[0], (TOTAL, TILE, TILE), ((0, 128),), -0.2, 0.2), 0.05, 2.0)
    velocity = draw_velocity(jax.random.fold_in(streams_of[9], 71), 0)
    aquifer_head = jnp.clip(-3.0 + 2.5 * jax.random.uniform(streams_of[2], (TOTAL, TILE, TILE), jnp.float32) ** shard_levels(streams_of[2], (TOTAL, TILE, TILE), ((0, 128),), -0.2, 0.2), -3.0, -0.5)
    terrain = scatter_about(streams_of[3], (TOTAL, TILE, TILE), 0.25, 1.5, ((0, 128),), jnp.float32)
    leakance = jnp.clip(jnp.exp(math.log(0.5) - 2.3025851 * jax.random.uniform(streams_of[4], (TOTAL, TILE, TILE), jnp.float32) ** shard_levels(streams_of[4], (TOTAL, TILE, TILE), ((0, 128),), -0.2, 0.2)), 0.05, 0.5)
    diffusivity = jnp.clip(jnp.exp(math.log(1.0) - 2.3025851 * jax.random.uniform(streams_of[5], (TOTAL, TILE, TILE), jnp.float32) ** shard_levels(streams_of[5], (TOTAL, TILE, TILE), ((0, 128),), -0.2, 0.2)), 0.1, 1.0)
    tile_wet = draw_tile_wet(jax.random.fold_in(streams_of[9], 71), 0)
    neighbours = draw_neighbours(jax.random.fold_in(streams_of[9], 71), 0)
    destination = draw_destination(jax.random.fold_in(streams_of[9], 71), 0)
    return dict(water_depth=water_depth, velocity=velocity, aquifer_head=aquifer_head, terrain=terrain, leakance=leakance, diffusivity=diffusivity, tile_wet=tile_wet, neighbours=neighbours, destination=destination)


GRAVITY = 9.81
SHALLOW = 0.1
COURANT = 0.45
STORAGE = 0.2
WALL_SIGNS = ((1.0, -1.0, 1.0, 1.0, 1.0), (1.0, -1.0, 1.0, 1.0, 1.0), (1.0, 1.0, -1.0, 1.0, 1.0), (1.0, 1.0, -1.0, 1.0, 1.0))
FACING = (1, 0, 3, 2)

def face_flux(depth_left, normal_left, along_left, depth_right, normal_right, along_right):
    floor_left = jnp.maximum(depth_left, SHALLOW)
    floor_right = jnp.maximum(depth_right, SHALLOW)
    speed_left = normal_left / floor_left
    speed_right = normal_right / floor_right
    wave_speed = jnp.maximum(jnp.abs(speed_left) + jnp.sqrt(GRAVITY * floor_left), jnp.abs(speed_right) + jnp.sqrt(GRAVITY * floor_right))
    mass_flux = 0.5 * (normal_left + normal_right) - 0.5 * wave_speed * (depth_right - depth_left)
    push_flux = 0.5 * (normal_left * speed_left + 0.5 * GRAVITY * depth_left * depth_left + normal_right * speed_right + 0.5 * GRAVITY * depth_right * depth_right) - 0.5 * wave_speed * (normal_right - normal_left)
    carry_flux = 0.5 * (along_left * speed_left + along_right * speed_right) - 0.5 * wave_speed * (along_right - along_left)
    return (mass_flux, push_flux, carry_flux)

def east_side(field, ghost):
    return jnp.concatenate([field[:, 1:], ghost[:, None]], axis=1)

def west_side(field, ghost):
    return jnp.concatenate([ghost[:, None], field[:, :-1]], axis=1)

def north_side(field, ghost):
    return jnp.concatenate([field[1:], ghost[None]], axis=0)

def south_side(field, ghost):
    return jnp.concatenate([ghost[None], field[:-1]], axis=0)

def advance(fields_now, ground, leak_rate, spread, ghosts, interval):
    water_now = fields_now[0]
    east_flow = fields_now[1]
    north_flow = fields_now[2]
    head_now = fields_now[3]
    cells = (water_now, east_flow, north_flow, head_now, ground)
    east_cells = [east_side(cells[field_index], ghosts[1, field_index]) for field_index in range(5)]
    north_cells = [north_side(cells[field_index], ghosts[3, field_index]) for field_index in range(5)]
    west_head = west_side(head_now, ghosts[0, 3])
    west_ground = west_side(ground, ghosts[0, 4])
    south_head = south_side(head_now, ghosts[2, 3])
    south_ground = south_side(ground, ghosts[2, 4])
    flux_east = face_flux(water_now, east_flow, north_flow, east_cells[0], east_cells[1], east_cells[2])
    rim_west = face_flux(ghosts[0, 0], ghosts[0, 1], ghosts[0, 2], water_now[:, 0], east_flow[:, 0], north_flow[:, 0])
    flux_west = [jnp.concatenate([rim_west[part_index][:, None], flux_east[part_index][:, :-1]], axis=1) for part_index in range(3)]
    flux_north = face_flux(water_now, north_flow, east_flow, north_cells[0], north_cells[2], north_cells[1])
    rim_south = face_flux(ghosts[2, 0], ghosts[2, 2], ghosts[2, 1], water_now[0], north_flow[0], east_flow[0])
    flux_south = [jnp.concatenate([rim_south[part_index][None], flux_north[part_index][:-1]], axis=0) for part_index in range(3)]
    seepage = leak_rate * (water_now + ground - head_now)
    new_depth = water_now - interval * (flux_east[0] - flux_west[0] + (flux_north[0] - flux_south[0])) - interval * seepage
    new_east = east_flow - interval * (flux_east[1] - flux_west[1] + (flux_north[2] - flux_south[2])) - interval * GRAVITY * water_now * 0.5 * (east_cells[4] - west_ground)
    new_north = north_flow - interval * (flux_east[2] - flux_west[2] + (flux_north[1] - flux_south[1])) - interval * GRAVITY * water_now * 0.5 * (north_cells[4] - south_ground)
    new_head = head_now + interval * (spread * (east_cells[3] + west_head + north_cells[3] + south_head - 4.0 * head_now) + seepage / STORAGE)
    return jnp.stack([new_depth, new_east, new_north, new_head])

def tile_speed(fields_now):
    floor_depth = jnp.maximum(fields_now[..., 0, :, :], SHALLOW)
    cell_speed = jnp.abs(fields_now[..., 1, :, :]) / floor_depth + jnp.abs(fields_now[..., 2, :, :]) / floor_depth + 2.0 * jnp.sqrt(GRAVITY * floor_depth)
    return lax.optimization_barrier(jnp.max(cell_speed, axis=(-2, -1)))

def tile_edges(fields_now):
    return jnp.stack([fields_now[..., :, 0], fields_now[..., :, -1], fields_now[..., 0, :], fields_now[..., -1, :]], axis=-3)

def reference(water_depth, velocity, aquifer_head, terrain, leakance, diffusivity, tile_wet, neighbours, destination):
    all_slots = jnp.arange(TOTAL, dtype=jnp.int32)
    source = jnp.zeros((TOTAL,), jnp.int32).at[destination].set(all_slots)
    discharge = water_depth[:, None] * velocity
    fields_now = jnp.concatenate([water_depth[:, None], discharge, aquifer_head[:, None]], axis=1)[source]
    ground = terrain[source]
    leak_rate = leakance[source]
    spread = diffusivity[source]
    wet_slot = tile_wet[source]
    linked = neighbours[source]
    linked_slots = jnp.where(linked >= 0, destination[jnp.clip(linked, 0, TOTAL - 1)], -1)
    facing = jnp.array(FACING, jnp.int32)[None, :]
    wall_signs = jnp.array(WALL_SIGNS, jnp.float32)[:, :, None]
    lowest = 2.0 * math.sqrt(GRAVITY * SHALLOW)
    for index_step in range(STEPS):
        fastest = jnp.max(jnp.where(wet_slot == 1, tile_speed(fields_now), lowest))
        interval = COURANT / fastest
        rim_rows = jnp.concatenate([tile_edges(fields_now), tile_edges(ground[:, None])], axis=2)
        remote_rims = rim_rows[jnp.clip(linked_slots, 0, TOTAL - 1), facing]
        ghosts = jnp.where((linked_slots >= 0)[:, :, None, None], remote_rims, rim_rows * wall_signs)
        updated = lax.map(lambda bundle: advance(bundle[0], bundle[1], bundle[2], bundle[3], bundle[4], interval), (fields_now, ground, leak_rate, spread, ghosts))
        fields_now = jnp.where((wet_slot == 1)[:, None, None, None], updated, fields_now)
    return (fields_now[:, 0], fields_now[:, 1:3], fields_now[:, 3])
```

```python
import functools
import math

import jax
import jax.numpy as jnp
from jax import lax
from jax.experimental import pallas as pl
from jax.experimental.pallas import tpu as pltpu
from jax.sharding import PartitionSpec as P

MESH = pl.DeviceIdType.MESH
TPD = 4
MOVE = 2
STEPS = 4
TILE = 128
BLOCKS = TILE // 8
GRAVITY = 9.81
ROOT_G = math.sqrt(GRAVITY)
SHALLOW = 0.1
COURANT = 0.45
STORAGE = 0.2
LOWEST = 2.0 * math.sqrt(GRAVITY * SHALLOW)
DEVICES = 128
F32 = jnp.float32


def peers(me):
    core = lax.rem(me, 2)
    y = lax.rem(me // 2, 4)
    z = lax.rem(me // 8, 4)
    x = me // 32
    xs = [lax.rem(x + d, 4) * 32 for d in range(4)]
    zs = [lax.rem(z + d, 4) * 8 for d in range(4)]
    ys = [lax.rem(y + d, 4) * 2 for d in range(4)]
    cs = [core, 1 - core]
    xz = [[a + b for b in zs] for a in xs]
    yc = [[a + b for b in cs] for a in ys]
    found = []
    for dx in range(4):
        for dz in range(4):
            for dy in range(4):
                for dc in range(2):
                    offset = ((dx * 4 + dz) * 4 + dy) * 2 + dc
                    if offset:
                        hops = sum(min(d, 4 - d) for d in (dx, dz, dy))
                        found.append((hops, offset, xz[dx][dz] + yc[dy][dc]))
    found.sort(key=lambda item: -item[0])
    return [(offset, target) for _, offset, target in found]


def derived(h, mx, my):
    s = jnp.maximum(h, SHALLOW)
    r = lax.rsqrt(s)
    inv = r * r
    c = (ROOT_G * s) * r
    return inv, c


def wave(h, n, inv, c):
    u = n * inv
    return u, jnp.abs(u) + c


def face(h1, n1, a1, h2, n2, a2):
    inv1, c1 = derived(h1, n1, a1)
    inv2, c2 = derived(h2, n2, a2)
    u1, w1 = wave(h1, n1, inv1, c1)
    u2, w2 = wave(h2, n2, inv2, c2)
    speed = jnp.maximum(w1, w2)
    half_g = 0.5 * GRAVITY
    mass = (n1 + n2) - speed * (h2 - h1)
    push = (n1 * u1 + half_g * h1 * h1 + n2 * u2 + half_g * h2 * h2) - speed * (n2 - n1)
    carry = (a1 * u1 + a2 * u2) - speed * (a2 - a1)
    return mass, push, carry


def flood_kernel(
    wet_ref, link_ref, dest_ref, depth_in, vel_in, head_in, terr_in, leak_in, diff_in,
    pool_out,
    U, D, R, G, L, S, KX, KY, VEL, mbuf, ew_own, ew_got, ns_own, ns_got, movers,
    in_sem, mx_send, mx_recv, ew_send, ew_recv, ns_send, ns_recv, mv_send, mv_recv, out_sem,
):
    me = lax.axis_index("tiles")
    row = me // 4
    col = lax.rem(me, 4)
    odd = lax.rem(row, 2)
    place = col + odd * (3 - 2 * col)
    base = me * TPD

    def device_at(r, c):
        o = lax.rem(r, 2)
        return r * 4 + c + o * (3 - 2 * c)

    east = device_at(row, lax.rem(place + 1, 4))
    west = device_at(row, lax.rem(place + 3, 4))
    north = device_at(lax.rem(row + 1, 32), place)
    south = device_at(lax.rem(row + 31, 32), place)
    after = lax.rem(me + 1, DEVICES)
    before = lax.rem(me + DEVICES - 1, DEVICES)
    everyone = peers(me)
    slot = [p + odd * (3 - 2 * p) for p in range(TPD)]

    loads = []
    for p in range(TPD):
        t = slot[p]
        loads.append(pltpu.make_async_copy(depth_in.at[t], U.at[p, 0], in_sem.at[0, p]))
        loads.append(pltpu.make_async_copy(vel_in.at[t], VEL.at[p], in_sem.at[1, p]))
        loads.append(pltpu.make_async_copy(head_in.at[t], U.at[p, 3], in_sem.at[2, p]))
        loads.append(pltpu.make_async_copy(terr_in.at[t], G.at[p], in_sem.at[3, p]))
        loads.append(pltpu.make_async_copy(leak_in.at[t], L.at[p], in_sem.at[4, p]))
        loads.append(pltpu.make_async_copy(diff_in.at[t], S.at[p], in_sem.at[5, p]))
    for load in loads:
        load.start()

    barrier = pltpu.get_barrier_semaphore()
    for _, target in everyone:
        pl.semaphore_signal(barrier, inc=1, device_id=(target,), device_id_type=MESH)

    wet = [wet_ref[base + slot[p]] for p in range(TPD)]
    linked = [[link_ref[k, base + slot[p]] for k in range(4)] for p in range(TPD)]
    lane = lax.broadcasted_iota(jnp.int32, (8, TILE), 1)
    sub = lax.broadcasted_iota(jnp.int32, (8, TILE), 0)
    first_lane = lane == 0
    last_lane = lane == TILE - 1
    wall_lane = [jnp.where(linked[p][1] >= 0, -1, TILE - 1) for p in range(TPD - 1)]
    wall_back = [jnp.where(linked[p][0] >= 0, -1, 0) for p in range(TPD)]
    zero = jnp.zeros((8, TILE), F32)

    def rows_of(i):
        return pl.ds(pl.multiple_of(i * 8, 8), 8)

    def pack(i, q, value, acc, edge):
        lane_at = q * BLOCKS + i
        shift = lane_at + (1 if edge else 0)
        return jnp.where(lane == lane_at, pltpu.roll(value, shift, 1), acc)

    for load in loads:
        load.wait()

    def ground_block(i, carry):
        acc_e, acc_w = carry
        blk = rows_of(i)
        acc_e = pack(i, 4, G[TPD - 1, blk, :], acc_e, True)
        acc_w = pack(i, 4, G[0, blk, :], acc_w, False)
        return acc_e, acc_w

    ground_e, ground_w = lax.fori_loop(0, BLOCKS, ground_block, (zero, zero))
    for s in range(STEPS):
        for p in range(TPD):
            ns_own[s, 0, 16 + p : 17 + p, :] = G[p, TILE - 1 : TILE, :]
            ns_own[s, 1, 16 + p : 17 + p, :] = G[p, 0:1, :]
        for k in range(2):
            ns_own[s, k, 20:24, :] = jnp.zeros((4, TILE), F32)

    def sweep(step, dt_of):
        def block(i, carry):
            acc_e, acc_w, top = carry
            blk = rows_of(i)
            top = list(top)
            for p in range(TPD):
                if dt_of is None:
                    h = U[p, 0, blk, :]
                    mx = h * VEL[p, 0, blk, :]
                    my = h * VEL[p, 1, blk, :]
                    hd = U[p, 3, blk, :]
                    U[p, 1, blk, :] = mx
                    U[p, 2, blk, :] = my
                else:
                    new = [U[p, q, blk, :] + dt_of[p] * R[p, q, blk, :] for q in range(4)]
                    for q in range(4):
                        U[p, q, blk, :] = new[q]
                    h, mx, my, hd = new
                inv, c = derived(h, mx, my)
                top[p] = jnp.maximum(top[p], (jnp.abs(mx) + jnp.abs(my)) * inv + 2.0 * c)
                if p == TPD - 1:
                    for q, value in enumerate((h, mx, my, hd)):
                        acc_e = pack(i, q, value, acc_e, True)
                if p == 0:
                    for q, value in enumerate((h, mx, my, hd)):
                        acc_w = pack(i, q, value, acc_w, False)
            return acc_e, acc_w, tuple(top)

        acc_e, acc_w, top = lax.fori_loop(
            0, BLOCKS, block, (ground_e, ground_w, (zero,) * TPD)
        )
        ew_own[step, 0] = acc_e
        ew_own[step, 1] = acc_w
        largest = jnp.full((8, TILE), LOWEST, F32)
        for p in range(TPD):
            largest = jnp.maximum(largest, jnp.where(wet[p] == 1, top[p], LOWEST))
        mbuf[step, 0:1, :] = jnp.max(largest, axis=0, keepdims=True)
        for q in range(4):
            for p in range(TPD):
                at = q * 4 + p
                ns_own[step, 0, at : at + 1, :] = U[p, q, TILE - 1 : TILE, :]
                ns_own[step, 1, at : at + 1, :] = U[p, q, 0:1, :]

    def halos(step):
        return [
            pltpu.make_async_remote_copy(
                ew_own.at[step, 0], ew_got.at[step, 1], ew_send.at[step, 0], ew_recv.at[step, 1],
                device_id=(east,), device_id_type=MESH),
            pltpu.make_async_remote_copy(
                ew_own.at[step, 1], ew_got.at[step, 0], ew_send.at[step, 1], ew_recv.at[step, 0],
                device_id=(west,), device_id_type=MESH),
            pltpu.make_async_remote_copy(
                ns_own.at[step, 0], ns_got.at[step, 1], ns_send.at[step, 0], ns_recv.at[step, 1],
                device_id=(north,), device_id_type=MESH),
            pltpu.make_async_remote_copy(
                ns_own.at[step, 1], ns_got.at[step, 0], ns_send.at[step, 1], ns_recv.at[step, 0],
                device_id=(south,), device_id_type=MESH),
        ]

    def send(step):
        for n, (offset, target) in enumerate(everyone):
            if n == 14:
                for copy in halos(step):
                    copy.start()
            pltpu.make_async_remote_copy(
                mbuf.at[step, 0:1], mbuf.at[step, offset : offset + 1],
                mx_send.at[step], mx_recv.at[step],
                device_id=(target,), device_id_type=MESH).start()

    def all_rows(step, sem):
        rest = mbuf.at[step, 1:DEVICES]
        return pltpu.make_async_copy(rest, rest, sem.at[step])

    def ground_slopes():
        def block(i, below):
            blk = rows_of(i)
            nxt = rows_of(jnp.minimum(i + 1, BLOCKS - 1))
            top_row = jnp.where(i == BLOCKS - 1, 7, -1)
            here = [G[p, blk, :] for p in range(TPD)]
            turned = [pltpu.roll(g, TILE - 1, 1) for g in here]
            back = zero
            new_below = []
            for p in range(TPD):
                g = here[p]
                if p < TPD - 1:
                    de = jnp.where(last_lane, turned[p + 1], turned[p]) - g
                    de = jnp.where(lane == wall_lane[p], 0.0, de)
                else:
                    de = jnp.where(last_lane, 0.0, turned[p] - g)
                round_de = pltpu.roll(de, 1, 1)
                dw = jnp.where(first_lane, back, round_de)
                back = round_de
                KX[p, blk, :] = (0.5 * GRAVITY) * (de + dw)
                up = jnp.where(sub == 7, pltpu.roll(G[p, nxt, :], 7, 0), pltpu.roll(g, 7, 0))
                dn = jnp.where(sub == top_row, 0.0, up - g)
                round_dn = pltpu.roll(dn, 1, 0)
                ds = jnp.where(sub == 0, below[p], round_dn)
                new_below.append(round_dn)
                KY[p, blk, :] = (0.5 * GRAVITY) * (dn + ds)
            return tuple(new_below)

        lax.fori_loop(0, BLOCKS, block, (zero,) * TPD)

    def right_sides():
        def derive(i, _):
            blk = rows_of(i)
            for p in range(TPD):
                h, mx, my = (U[p, q, blk, :] for q in range(3))
                inv, c = derived(h, mx, my)
                u, au = wave(h, mx, inv, c)
                v, av = wave(h, my, inv, c)
                still = (0.5 * GRAVITY) * h * h
                D[p, 0, blk, :] = au
                D[p, 1, blk, :] = av
                D[p, 2, blk, :] = mx * u + still
                D[p, 3, blk, :] = mx * v
                D[p, 4, blk, :] = my * v + still
            return 0

        lax.fori_loop(0, BLOCKS, derive, 0)

        def block(i, below):
            blk = rows_of(i)
            nxt = rows_of(jnp.minimum(i + 1, BLOCKS - 1))
            top_row = jnp.where(i == BLOCKS - 1, 7, -1)
            new_below = []
            after_turned = None
            east_faces = [None] * TPD
            sides = [None] * TPD
            for p in reversed(range(TPD)):
                h, mx, my, hd = (U[p, q, blk, :] for q in range(4))
                au, fxx, fxy = D[p, 0, blk, :], D[p, 2, blk, :], D[p, 3, blk, :]
                own = (h, mx, my, hd, au, fxx, fxy)
                turned = [pltpu.roll(value, TILE - 1, 1) for value in own]
                if after_turned is None:
                    he, me_, ye, de, ae, xe, ce = turned
                else:
                    he, me_, ye, de, ae, xe, ce = (
                        jnp.where(last_lane, b, a) for a, b in zip(turned, after_turned)
                    )
                after_turned = turned
                speed = jnp.maximum(au, ae)
                g0 = (mx + me_) - speed * (he - h)
                g1 = (fxx + xe) - speed * (me_ - mx)
                g2 = (fxy + ce) - speed * (ye - my)
                g3 = de - hd
                step_out = au * mx
                if p == TPD - 1:
                    wall, push = last_lane, 0.0
                else:
                    wall, push = lane == wall_lane[p], 2.0 * (fxx + step_out)
                g0 = jnp.where(wall, 0.0, g0)
                g1 = jnp.where(wall, push, g1)
                g2 = jnp.where(wall, 0.0, g2)
                g3 = jnp.where(wall, 0.0, g3)
                east_faces[p] = (g0, g1, g2, g3)
                sides[p] = 2.0 * (fxx - step_out)
            back = (zero,) * 4
            for p in range(TPD):
                rounds = [pltpu.roll(g, 1, 1) for g in east_faces[p]]
                west_faces = [jnp.where(first_lane, b, a) for a, b in zip(rounds, back)]
                if p > 0:
                    west_faces[1] = jnp.where(lane == wall_back[p], sides[p], west_faces[1])
                back = rounds
                x0, x1, x2, x3 = (e - w for e, w in zip(east_faces[p], west_faces))

                h, mx, my, hd = (U[p, q, blk, :] for q in range(4))
                av, fxy, fyy = D[p, 1, blk, :], D[p, 3, blk, :], D[p, 4, blk, :]
                own = (h, mx, my, hd, av, fxy, fyy)
                ups = (U[p, 0, nxt, :], U[p, 1, nxt, :], U[p, 2, nxt, :], U[p, 3, nxt, :],
                       D[p, 1, nxt, :], D[p, 3, nxt, :], D[p, 4, nxt, :])
                hn, xn, mn, dn, an, cn, yn = (
                    jnp.where(sub == 7, pltpu.roll(b, 7, 0), pltpu.roll(a, 7, 0))
                    for a, b in zip(own, ups)
                )
                speed = jnp.maximum(av, an)
                f0 = (my + mn) - speed * (hn - h)
                f1 = (fyy + yn) - speed * (mn - my)
                f2 = (fxy + cn) - speed * (xn - mx)
                f3 = dn - hd
                faces = [jnp.where(sub == top_row, 0.0, f) for f in (f0, f1, f2, f3)]
                rounds = [pltpu.roll(f, 1, 0) for f in faces]
                lower = [jnp.where(sub == 0, b, a) for a, b in zip(rounds, below[4 * p : 4 * p + 4])]
                new_below.extend(rounds)
                y0, y1, y2, y3 = (n - s for n, s in zip(faces, lower))

                seep = L[p, blk, :] * (h + G[p, blk, :] - hd)
                R[p, 0, blk, :] = -0.5 * (x0 + y0) - seep
                R[p, 1, blk, :] = -0.5 * (x1 + y2) - h * KX[p, blk, :]
                R[p, 2, blk, :] = -0.5 * (x2 + y1) - h * KY[p, blk, :]
                R[p, 3, blk, :] = S[p, blk, :] * (x3 + y3) + seep * (1.0 / STORAGE)
            return tuple(new_below)

        lax.fori_loop(0, BLOCKS, block, (zero,) * (4 * TPD))

    def column_terms(own, got, link, flip_east):
        ghost = jnp.where(link >= 0, got, jnp.where(lane // BLOCKS == 1, -own, own))
        part = lambda packed, q: packed if q == 0 else pltpu.roll(packed, TILE - q * BLOCKS, 1)
        h, n, a, hd, g = (part(own, q) for q in range(5))
        gh, gn, ga, ghd, gg = (part(ghost, q) for q in range(5))
        if flip_east:
            mass, push, carry = face(h, n, a, gh, gn, ga)
            sign = -0.5
        else:
            mass, push, carry = face(gh, gn, ga, h, n, a)
            sign = 0.5
        slope = (0.5 * GRAVITY) * h * ((gg - g) if flip_east else (g - gg))
        return sign * mass, sign * push - slope, sign * carry, ghd - hd

    def row_terms(own, got, k, is_north):
        rows = lax.broadcasted_iota(jnp.int32, (TPD, TILE), 0)
        link = jnp.full((TPD, TILE), linked[0][k], jnp.int32)
        for p in range(1, TPD):
            link = jnp.where(rows == p, linked[p][k], link)
        mine = [own[q * 4 : q * 4 + 4, :] for q in range(5)]
        signs = (1.0, 1.0, -1.0, 1.0, 1.0)
        ghost = [
            jnp.where(link >= 0, got[q * 4 : q * 4 + 4, :], signs[q] * mine[q]) for q in range(5)
        ]
        h, a, n, hd, g = mine
        gh, ga, gn, ghd, gg = ghost
        if is_north:
            mass, push, carry = face(h, n, a, gh, gn, ga)
            sign = -0.5
        else:
            mass, push, carry = face(gh, gn, ga, h, n, a)
            sign = 0.5
        slope = (0.5 * GRAVITY) * h * ((gg - g) if is_north else (g - gg))
        return sign * mass, sign * carry, sign * push - slope, ghd - hd

    def rims(step):
        for copy in halos(step):
            copy.wait_recv()
        for side, p, edge in ((0, TPD - 1, True), (1, 0, False)):
            terms = column_terms(
                ew_own[step, side], ew_got[step, side], linked[p][1 - side], edge
            )
            at_edge = last_lane if edge else first_lane

            def block(i, _):
                blk = rows_of(i)
                shift = (TILE - 1 - i) if edge else lax.rem(TILE - i, TILE)
                for q in range(4):
                    add = pltpu.roll(terms[q], shift, 1)
                    if q == 3:
                        add = add * S[p, blk, :]
                    R[p, q, blk, :] += jnp.where(at_edge, add, 0.0)
                return 0

            lax.fori_loop(0, BLOCKS, block, 0)
        for side, at in ((0, TILE - 1), (1, 0)):
            terms = row_terms(ns_own.at[step, side], ns_got.at[step, side], 3 - side, side == 0)
            for p in range(TPD):
                for q in range(4):
                    add = terms[q][p : p + 1, :]
                    if q == 3:
                        add = add * S[p, at : at + 1, :]
                    R[p, q, at : at + 1, :] += add

    def interval(step):
        all_rows(step, mx_recv).wait()
        top = jnp.max(jnp.max(mbuf[step], axis=0, keepdims=True), axis=1, keepdims=True)
        dt = COURANT / jnp.broadcast_to(top, (8, TILE))
        return [jnp.where(wet[p] == 1, dt, 0.0) for p in range(TPD)]

    sweep(0, None)
    pl.semaphore_wait(barrier, DEVICES - 1)

    def body(step, _):
        send(step)
        right_sides()
        rims(step)
        sweep(step + 1, interval(step))
        return 0

    send(0)
    ground_slopes()
    right_sides()
    rims(0)
    sweep(1, interval(0))
    lax.fori_loop(1, STEPS, body, 0)

    def movers_of(flags):
        count = jnp.int32(0)
        picks = [jnp.int32(0), jnp.int32(0)]
        for t in range(TPD):
            at = t + odd * (3 - 2 * t)
            for j in range(MOVE):
                picks[j] = jnp.where(jnp.logical_and(flags[t], count == j), at, picks[j])
            count = count + flags[t].astype(jnp.int32)
        return picks

    targets_of = [dest_ref[base + t] for t in range(TPD)]
    rightward = movers_of([d >= base + TPD for d in targets_of])
    leftward = movers_of([d < base for d in targets_of])
    keep = pltpu.make_async_copy(U.at[:, 0:4], pool_out.at[0:TPD], out_sem.at[0])
    keep.start()
    sent = []
    for j in range(MOVE):
        for side, picks, target in ((0, rightward, after), (1, leftward, before)):
            for q in range(4):
                movers[side, j, q] = U[picks[j], q]
            copy = pltpu.make_async_remote_copy(
                movers.at[side, j], pool_out.at[TPD + side * MOVE + j],
                mv_send.at[side, j], mv_recv.at[side, j],
                device_id=(target,), device_id_type=MESH)
            copy.start()
            sent.append(copy)
    for step in range(STEPS):
        all_rows(step, mx_send).wait()
        for copy in halos(step):
            copy.wait_send()
    keep.wait()
    for copy in sent:
        copy.wait()


def pick_kernel(dest_ref, pool, depth_out, flow_out, head_out, sem):
    me = lax.axis_index("tiles")
    base = me * TPD
    last = DEVICES - 1

    def odd_of(device):
        return lax.rem(device // 4, 2)

    wanted = [jnp.int32(0)] * TPD
    odd = odd_of(me)
    for t in range(TPD):
        d = dest_ref[base + t]
        at = t + odd * (3 - 2 * t)
        for k in range(TPD):
            wanted[k] = jnp.where(d == base + k, at, wanted[k])
    rank = jnp.int32(0)
    for t in range(TPD):
        d = dest_ref[jnp.maximum(base - TPD, 0) + t]
        came = jnp.logical_and(d >= base, me > 0)
        for k in range(TPD):
            wanted[k] = jnp.where(jnp.logical_and(came, d == base + k), TPD + rank, wanted[k])
        rank = rank + came.astype(jnp.int32)
    rank = jnp.int32(0)
    for t in range(TPD):
        d = dest_ref[jnp.minimum(base + TPD, last * TPD) + t]
        came = jnp.logical_and(d < base + TPD, me < last)
        for k in range(TPD):
            wanted[k] = jnp.where(
                jnp.logical_and(came, d == base + k), TPD + MOVE + rank, wanted[k]
            )
        rank = rank + came.astype(jnp.int32)
    copies = []
    for k in range(TPD):
        w = wanted[k]
        copies.append(pltpu.make_async_copy(pool.at[w, 0], depth_out.at[k], sem.at[0, k]))
        copies.append(pltpu.make_async_copy(pool.at[w, 1:3], flow_out.at[k], sem.at[1, k]))
        copies.append(pltpu.make_async_copy(pool.at[w, 3], head_out.at[k], sem.at[2, k]))
    for copy in copies:
        copy.start()
    for copy in copies:
        copy.wait()


def shards(depth, velocity, head, terrain, leakance, diffusivity, tile_wet, neighbours, destination):
    hbm = pl.BlockSpec(memory_space=pltpu.HBM)
    vmem = pl.BlockSpec(memory_space=pltpu.VMEM)
    smem = pl.BlockSpec(memory_space=pltpu.SMEM)
    vm = lambda *shape: pltpu.VMEM(shape + (TILE,), F32)
    dma = pltpu.SemaphoreType.DMA
    pool = pl.pallas_call(
        flood_kernel,
        out_shape=jax.ShapeDtypeStruct((TPD + 2 * MOVE, 4, TILE, TILE), F32),
        in_specs=[smem] * 3 + [hbm] * 6,
        out_specs=vmem,
        scratch_shapes=[
            vm(TPD, 4, TILE), vm(TPD, 5, TILE), vm(TPD, 4, TILE),
            vm(TPD, TILE), vm(TPD, TILE), vm(TPD, TILE), vm(TPD, TILE), vm(TPD, TILE),
            vm(TPD, 2, TILE), vm(STEPS + 1, DEVICES),
            vm(STEPS + 1, 2, 8), vm(STEPS, 2, 8), vm(STEPS + 1, 2, 24), vm(STEPS, 2, 24),
            vm(2, MOVE, 4, TILE),
            dma((6, TPD)), dma((STEPS,)), dma((STEPS,)),
            dma((STEPS, 2)), dma((STEPS, 2)), dma((STEPS, 2)), dma((STEPS, 2)),
            dma((2, MOVE)), dma((2, MOVE)), dma((1,)),
        ],
        compiler_params=pltpu.CompilerParams(
            collective_id=0, has_side_effects=True, vmem_limit_bytes=60 << 20
        ),
    )(tile_wet, neighbours.T, destination, depth, velocity, head, terrain, leakance, diffusivity)
    tile = jax.ShapeDtypeStruct((TPD, TILE, TILE), F32)
    return pl.pallas_call(
        pick_kernel,
        out_shape=(tile, jax.ShapeDtypeStruct((TPD, 2, TILE, TILE), F32), tile),
        in_specs=[smem, vmem],
        out_specs=(hbm,) * 3,
        scratch_shapes=[dma((3, TPD))],
    )(destination, pool)


def solution(mesh):
    tiles = P("tiles", None, None)
    pair = P("tiles", None, None, None)
    return jax.shard_map(
        shards,
        mesh=mesh,
        in_specs=(tiles, pair, tiles, tiles, tiles, tiles, P(), P(), P()),
        out_specs=(tiles, pair, tiles),
        check_vma=False,
    )
```

```python
import functools
import math

import jax
import jax.numpy as jnp
from jax import lax
from jax.experimental import pallas as pl
from jax.experimental.pallas import tpu as pltpu
from jax.sharding import PartitionSpec as P

MESH = pl.DeviceIdType.MESH
TPD = 4
MOVE = 2
STEPS = 4
TILE = 128
BLOCKS = TILE // 8
GRAVITY = 9.81
ROOT_G = math.sqrt(GRAVITY)
SHALLOW = 0.1
COURANT = 0.45
STORAGE = 0.2
LOWEST = 2.0 * math.sqrt(GRAVITY * SHALLOW)
DEVICES = 128
F32 = jnp.float32


def peers(me):
    core = lax.rem(me, 2)
    y = lax.rem(me // 2, 4)
    z = lax.rem(me // 8, 4)
    x = me // 32
    xs = [lax.rem(x + d, 4) * 32 for d in range(4)]
    zs = [lax.rem(z + d, 4) * 8 for d in range(4)]
    ys = [lax.rem(y + d, 4) * 2 for d in range(4)]
    cs = [core, 1 - core]
    xz = [[a + b for b in zs] for a in xs]
    yc = [[a + b for b in cs] for a in ys]
    found = []
    for dx in range(4):
        for dz in range(4):
            for dy in range(4):
                for dc in range(2):
                    offset = ((dx * 4 + dz) * 4 + dy) * 2 + dc
                    if offset:
                        hops = sum(min(d, 4 - d) for d in (dx, dz, dy))
                        found.append((hops, offset, xz[dx][dz] + yc[dy][dc]))
    found.sort(key=lambda item: -item[0])
    return [(offset, target) for _, offset, target in found]


def derived(h, mx, my):
    s = jnp.maximum(h, SHALLOW)
    r = lax.rsqrt(s)
    inv = r * r
    c = (ROOT_G * s) * r
    return inv, c


def wave(h, n, inv, c):
    u = n * inv
    return u, jnp.abs(u) + c


def face(h1, n1, a1, h2, n2, a2):
    inv1, c1 = derived(h1, n1, a1)
    inv2, c2 = derived(h2, n2, a2)
    u1, w1 = wave(h1, n1, inv1, c1)
    u2, w2 = wave(h2, n2, inv2, c2)
    speed = jnp.maximum(w1, w2)
    half_g = 0.5 * GRAVITY
    mass = (n1 + n2) - speed * (h2 - h1)
    push = (n1 * u1 + half_g * h1 * h1 + n2 * u2 + half_g * h2 * h2) - speed * (n2 - n1)
    carry = (a1 * u1 + a2 * u2) - speed * (a2 - a1)
    return mass, push, carry


def flood_kernel(
    wet_ref, link_ref, dest_ref, depth_in, vel_in, head_in, terr_in, leak_in, diff_in,
    pool_out,
    U, D, R, G, L, S, KX, KY, VEL, mbuf, ew_own, ew_got, ns_own, ns_got, movers,
    in_sem, mx_send, mx_recv, ew_send, ew_recv, ns_send, ns_recv, mv_send, mv_recv, out_sem,
):
    me = lax.axis_index("tiles")
    row = me // 4
    col = lax.rem(me, 4)
    odd = lax.rem(row, 2)
    place = col + odd * (3 - 2 * col)
    base = me * TPD

    def device_at(r, c):
        o = lax.rem(r, 2)
        return r * 4 + c + o * (3 - 2 * c)

    east = device_at(row, lax.rem(place + 1, 4))
    west = device_at(row, lax.rem(place + 3, 4))
    north = device_at(lax.rem(row + 1, 32), place)
    south = device_at(lax.rem(row + 31, 32), place)
    after = lax.rem(me + 1, DEVICES)
    before = lax.rem(me + DEVICES - 1, DEVICES)
    everyone = peers(me)
    slot = [p + odd * (3 - 2 * p) for p in range(TPD)]

    loads = []
    for p in range(TPD):
        t = slot[p]
        loads.append(pltpu.make_async_copy(depth_in.at[t], U.at[p, 0], in_sem.at[0, p]))
        loads.append(pltpu.make_async_copy(vel_in.at[t], VEL.at[p], in_sem.at[1, p]))
        loads.append(pltpu.make_async_copy(head_in.at[t], U.at[p, 3], in_sem.at[2, p]))
        loads.append(pltpu.make_async_copy(terr_in.at[t], G.at[p], in_sem.at[3, p]))
        loads.append(pltpu.make_async_copy(leak_in.at[t], L.at[p], in_sem.at[4, p]))
        loads.append(pltpu.make_async_copy(diff_in.at[t], S.at[p], in_sem.at[5, p]))
    for load in loads:
        load.start()

    barrier = pltpu.get_barrier_semaphore()
    for _, target in everyone:
        pl.semaphore_signal(barrier, inc=1, device_id=(target,), device_id_type=MESH)

    wet = [wet_ref[base + slot[p]] for p in range(TPD)]
    linked = [[link_ref[k, base + slot[p]] for k in range(4)] for p in range(TPD)]
    lane = lax.broadcasted_iota(jnp.int32, (8, TILE), 1)
    sub = lax.broadcasted_iota(jnp.int32, (8, TILE), 0)
    first_lane = lane == 0
    last_lane = lane == TILE - 1
    wall_lane = [jnp.where(linked[p][1] >= 0, -1, TILE - 1) for p in range(TPD - 1)]
    wall_back = [jnp.where(linked[p][0] >= 0, -1, 0) for p in range(TPD)]
    zero = jnp.zeros((8, TILE), F32)

    def rows_of(i):
        return pl.ds(i * 8 if isinstance(i, int) else pl.multiple_of(i * 8, 8), 8)

    def pack(i, q, value, acc, edge):
        lane_at = q * BLOCKS + i
        shift = (lane_at + (1 if edge else 0)) % TILE
        return jnp.where(lane == lane_at, pltpu.roll(value, shift, 1), acc)

    for load in loads:
        load.wait()

    def ground_block(i, carry):
        acc_e, acc_w = carry
        blk = rows_of(i)
        acc_e = pack(i, 4, G[TPD - 1, blk, :], acc_e, True)
        acc_w = pack(i, 4, G[0, blk, :], acc_w, False)
        return acc_e, acc_w

    ground_e = ground_w = zero
    for i in range(BLOCKS):
        ground_e, ground_w = ground_block(i, (ground_e, ground_w))
    for s in range(STEPS):
        for p in range(TPD):
            ns_own[s, 0, 16 + p : 17 + p, :] = G[p, TILE - 1 : TILE, :]
            ns_own[s, 1, 16 + p : 17 + p, :] = G[p, 0:1, :]
        for k in range(2):
            ns_own[s, k, 20:24, :] = jnp.zeros((4, TILE), F32)

    def sweep(step, dt_of):
        def block(i, carry):
            acc_e, acc_w, top = carry
            blk = rows_of(i)
            top = list(top)
            for p in range(TPD):
                if dt_of is None:
                    h = U[p, 0, blk, :]
                    mx = h * VEL[p, 0, blk, :]
                    my = h * VEL[p, 1, blk, :]
                    hd = U[p, 3, blk, :]
                    U[p, 1, blk, :] = mx
                    U[p, 2, blk, :] = my
                else:
                    new = [U[p, q, blk, :] + dt_of[p] * R[p, q, blk, :] for q in range(4)]
                    for q in range(4):
                        U[p, q, blk, :] = new[q]
                    h, mx, my, hd = new
                inv, c = derived(h, mx, my)
                top[p] = jnp.maximum(top[p], (jnp.abs(mx) + jnp.abs(my)) * inv + 2.0 * c)
                if p == TPD - 1:
                    for q, value in enumerate((h, mx, my, hd)):
                        acc_e = pack(i, q, value, acc_e, True)
                if p == 0:
                    for q, value in enumerate((h, mx, my, hd)):
                        acc_w = pack(i, q, value, acc_w, False)
            return acc_e, acc_w, tuple(top)

        state = (ground_e, ground_w, (zero,) * TPD)
        for i in range(BLOCKS):
            state = block(i, state)
        acc_e, acc_w, top = state
        ew_own[step, 0] = acc_e
        ew_own[step, 1] = acc_w
        largest = jnp.full((8, TILE), LOWEST, F32)
        for p in range(TPD):
            largest = jnp.maximum(largest, jnp.where(wet[p] == 1, top[p], LOWEST))
        mbuf[step, 0:1, :] = jnp.max(largest, axis=0, keepdims=True)
        for q in range(4):
            for p in range(TPD):
                at = q * 4 + p
                ns_own[step, 0, at : at + 1, :] = U[p, q, TILE - 1 : TILE, :]
                ns_own[step, 1, at : at + 1, :] = U[p, q, 0:1, :]

    def halos(step):
        return [
            pltpu.make_async_remote_copy(
                ew_own.at[step, 0], ew_got.at[step, 1], ew_send.at[step, 0], ew_recv.at[step, 1],
                device_id=(east,), device_id_type=MESH),
            pltpu.make_async_remote_copy(
                ew_own.at[step, 1], ew_got.at[step, 0], ew_send.at[step, 1], ew_recv.at[step, 0],
                device_id=(west,), device_id_type=MESH),
            pltpu.make_async_remote_copy(
                ns_own.at[step, 0], ns_got.at[step, 1], ns_send.at[step, 0], ns_recv.at[step, 1],
                device_id=(north,), device_id_type=MESH),
            pltpu.make_async_remote_copy(
                ns_own.at[step, 1], ns_got.at[step, 0], ns_send.at[step, 1], ns_recv.at[step, 0],
                device_id=(south,), device_id_type=MESH),
        ]

    def send(step):
        for n, (offset, target) in enumerate(everyone):
            if n == 2:
                for copy in halos(step):
                    copy.start()
            pltpu.make_async_remote_copy(
                mbuf.at[step, 0:1], mbuf.at[step, offset : offset + 1],
                mx_send.at[step], mx_recv.at[step],
                device_id=(target,), device_id_type=MESH).start()

    def all_rows(step, sem):
        rest = mbuf.at[step, 1:DEVICES]
        return pltpu.make_async_copy(rest, rest, sem.at[step])

    def ground_slopes():
        def block(i, below):
            blk = rows_of(i)
            nxt = rows_of(jnp.minimum(i + 1, BLOCKS - 1))
            top_row = jnp.where(i == BLOCKS - 1, 7, -1)
            here = [G[p, blk, :] for p in range(TPD)]
            turned = [pltpu.roll(g, TILE - 1, 1) for g in here]
            back = zero
            new_below = []
            for p in range(TPD):
                g = here[p]
                if p < TPD - 1:
                    de = jnp.where(last_lane, turned[p + 1], turned[p]) - g
                    de = jnp.where(lane == wall_lane[p], 0.0, de)
                else:
                    de = jnp.where(last_lane, 0.0, turned[p] - g)
                round_de = pltpu.roll(de, 1, 1)
                dw = jnp.where(first_lane, back, round_de)
                back = round_de
                KX[p, blk, :] = (0.5 * GRAVITY) * (de + dw)
                up = jnp.where(sub == 7, pltpu.roll(G[p, nxt, :], 7, 0), pltpu.roll(g, 7, 0))
                dn = jnp.where(sub == top_row, 0.0, up - g)
                round_dn = pltpu.roll(dn, 1, 0)
                ds = jnp.where(sub == 0, below[p], round_dn)
                new_below.append(round_dn)
                KY[p, blk, :] = (0.5 * GRAVITY) * (dn + ds)
            return tuple(new_below)

        lax.fori_loop(0, BLOCKS, block, (zero,) * TPD)

    def right_sides():
        def derive(i, _):
            blk = rows_of(i)
            for p in range(TPD):
                h, mx, my = (U[p, q, blk, :] for q in range(3))
                inv, c = derived(h, mx, my)
                u, au = wave(h, mx, inv, c)
                v, av = wave(h, my, inv, c)
                still = (0.5 * GRAVITY) * h * h
                D[p, 0, blk, :] = au
                D[p, 1, blk, :] = av
                D[p, 2, blk, :] = mx * u + still
                D[p, 3, blk, :] = mx * v
                D[p, 4, blk, :] = my * v + still
            return 0

        lax.fori_loop(0, BLOCKS, derive, 0, unroll=4)

        def block(i, below):
            blk = rows_of(i)
            nxt = rows_of(jnp.minimum(i + 1, BLOCKS - 1))
            top_row = jnp.where(i == BLOCKS - 1, 7, -1)
            new_below = []
            after_turned = None
            east_faces = [None] * TPD
            sides = [None] * TPD
            for p in reversed(range(TPD)):
                h, mx, my, hd = (U[p, q, blk, :] for q in range(4))
                au, fxx, fxy = D[p, 0, blk, :], D[p, 2, blk, :], D[p, 3, blk, :]
                own = (h, mx, my, hd, au, fxx, fxy)
                turned = [pltpu.roll(value, TILE - 1, 1) for value in own]
                if after_turned is None:
                    he, me_, ye, de, ae, xe, ce = turned
                else:
                    he, me_, ye, de, ae, xe, ce = (
                        jnp.where(last_lane, b, a) for a, b in zip(turned, after_turned)
                    )
                after_turned = turned
                speed = jnp.maximum(au, ae)
                g0 = (mx + me_) - speed * (he - h)
                g1 = (fxx + xe) - speed * (me_ - mx)
                g2 = (fxy + ce) - speed * (ye - my)
                g3 = de - hd
                step_out = au * mx
                if p == TPD - 1:
                    wall, push = last_lane, 0.0
                else:
                    wall, push = lane == wall_lane[p], 2.0 * (fxx + step_out)
                g0 = jnp.where(wall, 0.0, g0)
                g1 = jnp.where(wall, push, g1)
                g2 = jnp.where(wall, 0.0, g2)
                g3 = jnp.where(wall, 0.0, g3)
                east_faces[p] = (g0, g1, g2, g3)
                sides[p] = 2.0 * (fxx - step_out)
            back = (zero,) * 4
            for p in range(TPD):
                rounds = [pltpu.roll(g, 1, 1) for g in east_faces[p]]
                west_faces = [jnp.where(first_lane, b, a) for a, b in zip(rounds, back)]
                if p > 0:
                    west_faces[1] = jnp.where(lane == wall_back[p], sides[p], west_faces[1])
                back = rounds
                x0, x1, x2, x3 = (e - w for e, w in zip(east_faces[p], west_faces))

                h, mx, my, hd = (U[p, q, blk, :] for q in range(4))
                av, fxy, fyy = D[p, 1, blk, :], D[p, 3, blk, :], D[p, 4, blk, :]
                own = (h, mx, my, hd, av, fxy, fyy)
                ups = (U[p, 0, nxt, :], U[p, 1, nxt, :], U[p, 2, nxt, :], U[p, 3, nxt, :],
                       D[p, 1, nxt, :], D[p, 3, nxt, :], D[p, 4, nxt, :])
                hn, xn, mn, dn, an, cn, yn = (
                    jnp.where(sub == 7, pltpu.roll(b, 7, 0), pltpu.roll(a, 7, 0))
                    for a, b in zip(own, ups)
                )
                speed = jnp.maximum(av, an)
                f0 = (my + mn) - speed * (hn - h)
                f1 = (fyy + yn) - speed * (mn - my)
                f2 = (fxy + cn) - speed * (xn - mx)
                f3 = dn - hd
                faces = [jnp.where(sub == top_row, 0.0, f) for f in (f0, f1, f2, f3)]
                rounds = [pltpu.roll(f, 1, 0) for f in faces]
                lower = [jnp.where(sub == 0, b, a) for a, b in zip(rounds, below[4 * p : 4 * p + 4])]
                new_below.extend(rounds)
                y0, y1, y2, y3 = (n - s for n, s in zip(faces, lower))

                seep = L[p, blk, :] * (h + G[p, blk, :] - hd)
                R[p, 0, blk, :] = -0.5 * (x0 + y0) - seep
                R[p, 1, blk, :] = -0.5 * (x1 + y2) - h * KX[p, blk, :]
                R[p, 2, blk, :] = -0.5 * (x2 + y1) - h * KY[p, blk, :]
                R[p, 3, blk, :] = S[p, blk, :] * (x3 + y3) + seep * (1.0 / STORAGE)
            return tuple(new_below)

        lax.fori_loop(0, BLOCKS, block, (zero,) * (4 * TPD), unroll=2)

    def column_terms(own, got, link, flip_east):
        ghost = jnp.where(link >= 0, got, jnp.where(lane // BLOCKS == 1, -own, own))
        part = lambda packed, q: packed if q == 0 else pltpu.roll(packed, TILE - q * BLOCKS, 1)
        h, n, a, hd, g = (part(own, q) for q in range(5))
        gh, gn, ga, ghd, gg = (part(ghost, q) for q in range(5))
        if flip_east:
            mass, push, carry = face(h, n, a, gh, gn, ga)
            sign = -0.5
        else:
            mass, push, carry = face(gh, gn, ga, h, n, a)
            sign = 0.5
        slope = (0.5 * GRAVITY) * h * ((gg - g) if flip_east else (g - gg))
        return sign * mass, sign * push - slope, sign * carry, ghd - hd

    def row_terms(own, got, k, is_north):
        rows = lax.broadcasted_iota(jnp.int32, (TPD, TILE), 0)
        link = jnp.full((TPD, TILE), linked[0][k], jnp.int32)
        for p in range(1, TPD):
            link = jnp.where(rows == p, linked[p][k], link)
        mine = [own[q * 4 : q * 4 + 4, :] for q in range(5)]
        signs = (1.0, 1.0, -1.0, 1.0, 1.0)
        ghost = [
            jnp.where(link >= 0, got[q * 4 : q * 4 + 4, :], signs[q] * mine[q]) for q in range(5)
        ]
        h, a, n, hd, g = mine
        gh, ga, gn, ghd, gg = ghost
        if is_north:
            mass, push, carry = face(h, n, a, gh, gn, ga)
            sign = -0.5
        else:
            mass, push, carry = face(gh, gn, ga, h, n, a)
            sign = 0.5
        slope = (0.5 * GRAVITY) * h * ((gg - g) if is_north else (g - gg))
        return sign * mass, sign * carry, sign * push - slope, ghd - hd

    def rims(step):
        for copy in halos(step):
            copy.wait_recv()
        for side, p, edge in ((0, TPD - 1, True), (1, 0, False)):
            terms = column_terms(
                ew_own[step, side], ew_got[step, side], linked[p][1 - side], edge
            )
            at_edge = last_lane if edge else first_lane

            for i in range(BLOCKS):
                blk = rows_of(i)
                shift = (TILE - 1 - i) if edge else (TILE - i) % TILE
                for q in range(4):
                    add = pltpu.roll(terms[q], shift, 1)
                    if q == 3:
                        add = add * S[p, blk, :]
                    R[p, q, blk, :] += jnp.where(at_edge, add, 0.0)
        for side, at in ((0, TILE - 1), (1, 0)):
            terms = row_terms(ns_own.at[step, side], ns_got.at[step, side], 3 - side, side == 0)
            for p in range(TPD):
                for q in range(4):
                    add = terms[q][p : p + 1, :]
                    if q == 3:
                        add = add * S[p, at : at + 1, :]
                    R[p, q, at : at + 1, :] += add

    def interval(step):
        all_rows(step, mx_recv).wait()
        top = jnp.max(jnp.max(mbuf[step], axis=0, keepdims=True), axis=1, keepdims=True)
        dt = COURANT / jnp.broadcast_to(top, (8, TILE))
        return [jnp.where(wet[p] == 1, dt, 0.0) for p in range(TPD)]

    sweep(0, None)
    ground_slopes()
    pl.semaphore_wait(barrier, DEVICES - 1)

    def body(step, _):
        send(step)
        right_sides()
        rims(step)
        sweep(step + 1, interval(step))
        return 0

    lax.fori_loop(0, STEPS, body, 0)

    def movers_of(flags):
        count = jnp.int32(0)
        picks = [jnp.int32(0), jnp.int32(0)]
        for t in range(TPD):
            at = t + odd * (3 - 2 * t)
            for j in range(MOVE):
                picks[j] = jnp.where(jnp.logical_and(flags[t], count == j), at, picks[j])
            count = count + flags[t].astype(jnp.int32)
        return picks

    targets_of = [dest_ref[base + t] for t in range(TPD)]
    rightward = movers_of([d >= base + TPD for d in targets_of])
    leftward = movers_of([d < base for d in targets_of])
    keep = pltpu.make_async_copy(U.at[:, 0:4], pool_out.at[0:TPD], out_sem.at[0])
    keep.start()
    sent = []
    for j in range(MOVE):
        for side, picks, target in ((0, rightward, after), (1, leftward, before)):
            for q in range(4):
                movers[side, j, q] = U[picks[j], q]
            copy = pltpu.make_async_remote_copy(
                movers.at[side, j], pool_out.at[TPD + side * MOVE + j],
                mv_send.at[side, j], mv_recv.at[side, j],
                device_id=(target,), device_id_type=MESH)
            copy.start()
            sent.append(copy)
    for step in range(STEPS):
        all_rows(step, mx_send).wait()
        for copy in halos(step):
            copy.wait_send()
    keep.wait()
    for copy in sent:
        copy.wait()


def pick_kernel(dest_ref, pool, depth_out, flow_out, head_out, held, in_sem, sem):
    me = lax.axis_index("tiles")
    base = me * TPD
    last = DEVICES - 1

    def odd_of(device):
        return lax.rem(device // 4, 2)

    wanted = [jnp.int32(0)] * TPD
    odd = odd_of(me)
    for t in range(TPD):
        d = dest_ref[base + t]
        at = t + odd * (3 - 2 * t)
        for k in range(TPD):
            wanted[k] = jnp.where(d == base + k, at, wanted[k])
    rank = jnp.int32(0)
    for t in range(TPD):
        d = dest_ref[jnp.maximum(base - TPD, 0) + t]
        came = jnp.logical_and(d >= base, me > 0)
        for k in range(TPD):
            wanted[k] = jnp.where(jnp.logical_and(came, d == base + k), TPD + rank, wanted[k])
        rank = rank + came.astype(jnp.int32)
    rank = jnp.int32(0)
    for t in range(TPD):
        d = dest_ref[jnp.minimum(base + TPD, last * TPD) + t]
        came = jnp.logical_and(d < base + TPD, me < last)
        for k in range(TPD):
            wanted[k] = jnp.where(
                jnp.logical_and(came, d == base + k), TPD + MOVE + rank, wanted[k]
            )
        rank = rank + came.astype(jnp.int32)
    fetches = [pltpu.make_async_copy(pool.at[wanted[k]], held.at[k], in_sem.at[k]) for k in range(TPD)]
    for fetch in fetches:
        fetch.start()
    copies = []
    for k in range(TPD):
        fetches[k].wait()
        for n, (part, out) in enumerate(
            ((held.at[k, 0], depth_out), (held.at[k, 1:3], flow_out), (held.at[k, 3], head_out))
        ):
            copy = pltpu.make_async_copy(part, out.at[k], sem.at[n, k])
            copy.start()
            copies.append(copy)
    for copy in copies:
        copy.wait()


def shards(depth, velocity, head, terrain, leakance, diffusivity, tile_wet, neighbours, destination):
    hbm = pl.BlockSpec(memory_space=pltpu.HBM)
    smem = pl.BlockSpec(memory_space=pltpu.SMEM)
    vm = lambda *shape: pltpu.VMEM(shape + (TILE,), F32)
    dma = pltpu.SemaphoreType.DMA
    pool = pl.pallas_call(
        flood_kernel,
        out_shape=jax.ShapeDtypeStruct((TPD + 2 * MOVE, 4, TILE, TILE), F32),
        in_specs=[smem] * 3 + [hbm] * 6,
        out_specs=hbm,
        scratch_shapes=[
            vm(TPD, 4, TILE), vm(TPD, 5, TILE), vm(TPD, 4, TILE),
            vm(TPD, TILE), vm(TPD, TILE), vm(TPD, TILE), vm(TPD, TILE), vm(TPD, TILE),
            vm(TPD, 2, TILE), vm(STEPS + 1, DEVICES),
            vm(STEPS + 1, 2, 8), vm(STEPS, 2, 8), vm(STEPS + 1, 2, 24), vm(STEPS, 2, 24),
            vm(2, MOVE, 4, TILE),
            dma((6, TPD)), dma((STEPS,)), dma((STEPS,)),
            dma((STEPS, 2)), dma((STEPS, 2)), dma((STEPS, 2)), dma((STEPS, 2)),
            dma((2, MOVE)), dma((2, MOVE)), dma((1,)),
        ],
        compiler_params=pltpu.CompilerParams(
            collective_id=0, has_side_effects=True, vmem_limit_bytes=60 << 20
        ),
    )(tile_wet, neighbours.T, destination, depth, velocity, head, terrain, leakance, diffusivity)
    tile = jax.ShapeDtypeStruct((TPD, TILE, TILE), F32)
    return pl.pallas_call(
        pick_kernel,
        out_shape=(tile, jax.ShapeDtypeStruct((TPD, 2, TILE, TILE), F32), tile),
        in_specs=[smem, hbm],
        out_specs=(hbm,) * 3,
        scratch_shapes=[vm(TPD, 4, TILE), dma((TPD,)), dma((3, TPD))],
    )(destination, pool)


def solution(mesh):
    tiles = P("tiles", None, None)
    pair = P("tiles", None, None, None)
    return jax.shard_map(
        shards,
        mesh=mesh,
        in_specs=(tiles, pair, tiles, tiles, tiles, tiles, P(), P(), P()),
        out_specs=(tiles, pair, tiles),
        check_vma=False,
    )
```

```python
import functools
import math

import jax
import jax.numpy as jnp
from jax import lax
from jax.experimental import pallas as pl
from jax.experimental.pallas import tpu as pltpu
from jax.sharding import PartitionSpec as P

MESH = pl.DeviceIdType.MESH
TPD = 4
MOVE = 2
STEPS = 4
TILE = 128
BLOCKS = TILE // 8
GRAVITY = 9.81
ROOT_G = math.sqrt(GRAVITY)
SHALLOW = 0.1
COURANT = 0.45
STORAGE = 0.2
LOWEST = 2.0 * math.sqrt(GRAVITY * SHALLOW)
DEVICES = 128
F32 = jnp.float32


def peers(me):
    core = lax.rem(me, 2)
    y = lax.rem(me // 2, 4)
    z = lax.rem(me // 8, 4)
    x = me // 32
    xs = [lax.rem(x + d, 4) * 32 for d in range(4)]
    zs = [lax.rem(z + d, 4) * 8 for d in range(4)]
    ys = [lax.rem(y + d, 4) * 2 for d in range(4)]
    cs = [core, 1 - core]
    xz = [[a + b for b in zs] for a in xs]
    yc = [[a + b for b in cs] for a in ys]
    found = []
    for dx in range(4):
        for dz in range(4):
            for dy in range(4):
                for dc in range(2):
                    offset = ((dx * 4 + dz) * 4 + dy) * 2 + dc
                    if offset:
                        hops = sum(min(d, 4 - d) for d in (dx, dz, dy))
                        found.append((hops, offset, xz[dx][dz] + yc[dy][dc]))
    found.sort(key=lambda item: -item[0])
    return [(offset, target) for _, offset, target in found]


def derived(h, mx, my):
    s = jnp.maximum(h, SHALLOW)
    r = lax.rsqrt(s)
    inv = r * r
    c = (ROOT_G * s) * r
    return inv, c


def wave(h, n, inv, c):
    u = n * inv
    return u, jnp.abs(u) + c


def face(h1, n1, a1, h2, n2, a2):
    inv1, c1 = derived(h1, n1, a1)
    inv2, c2 = derived(h2, n2, a2)
    u1, w1 = wave(h1, n1, inv1, c1)
    u2, w2 = wave(h2, n2, inv2, c2)
    speed = jnp.maximum(w1, w2)
    half_g = 0.5 * GRAVITY
    mass = (n1 + n2) - speed * (h2 - h1)
    push = (n1 * u1 + half_g * h1 * h1 + n2 * u2 + half_g * h2 * h2) - speed * (n2 - n1)
    carry = (a1 * u1 + a2 * u2) - speed * (a2 - a1)
    return mass, push, carry


def flood_kernel(
    wet_ref, link_ref, dest_ref, depth_in, vel_in, head_in, terr_in, leak_in, diff_in,
    tiles_out,
    U, D, R, G, L, S, KX, KY, VEL, mbuf, ew_own, ew_got, ns_own, ns_got,
    movers, mover_ground, arrived_ground, DA, line_own, line_got, made,
    in_sem, mx_send, mx_recv, ew_send, ew_recv, ns_send, ns_recv, mv_send, mv_recv,
    mg_send, mg_recv, ln_send, ln_recv, out_sem,
):
    me = lax.axis_index("tiles")
    row = me // 4
    col = lax.rem(me, 4)
    odd = lax.rem(row, 2)
    place = col + odd * (3 - 2 * col)
    base = me * TPD

    def device_at(r, c):
        o = lax.rem(r, 2)
        return r * 4 + c + o * (3 - 2 * c)

    east = device_at(row, lax.rem(place + 1, 4))
    west = device_at(row, lax.rem(place + 3, 4))
    north = device_at(lax.rem(row + 1, 32), place)
    south = device_at(lax.rem(row + 31, 32), place)
    after = lax.rem(me + 1, DEVICES)
    before = lax.rem(me + DEVICES - 1, DEVICES)
    everyone = peers(me)
    slot = [p + odd * (3 - 2 * p) for p in range(TPD)]

    loads = []
    for n, (array, place_of) in enumerate((
        (depth_in, lambda p: U.at[p, 0]), (vel_in, lambda p: VEL.at[p]),
        (head_in, lambda p: U.at[p, 3]), (terr_in, lambda p: G.at[p]),
        (leak_in, lambda p: L.at[p]), (diff_in, lambda p: S.at[p]),
    )):
        for p in range(TPD):
            loads.append(pltpu.make_async_copy(array.at[slot[p]], place_of(p), in_sem.at[n, p]))
    early, late = loads[: 4 * TPD], loads[4 * TPD :]

    barrier = pltpu.get_barrier_semaphore()

    def announce(some):
        for _, target in some:
            pl.semaphore_signal(barrier, inc=1, device_id=(target,), device_id_type=MESH)

    for load in early:
        load.start()
    announce(everyone)
    for load in late:
        load.start()

    wet = [wet_ref[base + slot[p]] for p in range(TPD)]
    linked = [[link_ref[k, base + slot[p]] for k in range(4)] for p in range(TPD)]
    lane = lax.broadcasted_iota(jnp.int32, (8, TILE), 1)
    sub = lax.broadcasted_iota(jnp.int32, (8, TILE), 0)
    first_lane = lane == 0
    last_lane = lane == TILE - 1
    wall_lane = [jnp.where(linked[p][1] >= 0, -1, TILE - 1) for p in range(TPD - 1)]
    wall_back = [jnp.where(linked[p][0] >= 0, -1, 0) for p in range(TPD)]
    zero = jnp.zeros((8, TILE), F32)

    def rows_of(i):
        return pl.ds(i * 8 if isinstance(i, int) else pl.multiple_of(i * 8, 8), 8)

    def pack(i, q, value, acc, edge):
        lane_at = q * BLOCKS + i
        shift = (lane_at + (1 if edge else 0)) % TILE
        return jnp.where(lane == lane_at, pltpu.roll(value, shift, 1), acc)

    for load in early:
        load.wait()

    def ground_block(i, carry):
        acc_e, acc_w = carry
        blk = rows_of(i)
        acc_e = pack(i, 4, G[TPD - 1, blk, :], acc_e, True)
        acc_w = pack(i, 4, G[0, blk, :], acc_w, False)
        return acc_e, acc_w

    ground_e = ground_w = zero
    for i in range(BLOCKS):
        ground_e, ground_w = ground_block(i, (ground_e, ground_w))
    for s in range(STEPS):
        for p in range(TPD):
            ns_own[s, 0, 16 + p : 17 + p, :] = G[p, TILE - 1 : TILE, :]
            ns_own[s, 1, 16 + p : 17 + p, :] = G[p, 0:1, :]
        for k in range(2):
            ns_own[s, k, 20:24, :] = jnp.zeros((4, TILE), F32)

    def sweep(step, dt_of):
        def block(i, carry):
            acc_e, acc_w, top = carry
            blk = rows_of(i)
            top = list(top)
            for p in range(TPD):
                if dt_of is None:
                    h = U[p, 0, blk, :]
                    mx = h * VEL[p, 0, blk, :]
                    my = h * VEL[p, 1, blk, :]
                    hd = U[p, 3, blk, :]
                    U[p, 1, blk, :] = mx
                    U[p, 2, blk, :] = my
                else:
                    new = [U[p, q, blk, :] + dt_of[p] * R[p, q, blk, :] for q in range(4)]
                    for q in range(4):
                        U[p, q, blk, :] = new[q]
                    h, mx, my, hd = new
                inv, c = derived(h, mx, my)
                top[p] = jnp.maximum(top[p], (jnp.abs(mx) + jnp.abs(my)) * inv + 2.0 * c)
                if p == TPD - 1:
                    for q, value in enumerate((h, mx, my, hd)):
                        acc_e = pack(i, q, value, acc_e, True)
                if p == 0:
                    for q, value in enumerate((h, mx, my, hd)):
                        acc_w = pack(i, q, value, acc_w, False)
            return acc_e, acc_w, tuple(top)

        state = (ground_e, ground_w, (zero,) * TPD)
        for i in range(BLOCKS):
            state = block(i, state)
        acc_e, acc_w, top = state
        ew_own[step, 0] = acc_e
        ew_own[step, 1] = acc_w
        largest = jnp.full((8, TILE), LOWEST, F32)
        for p in range(TPD):
            largest = jnp.maximum(largest, jnp.where(wet[p] == 1, top[p], LOWEST))
        mbuf[step, 0:1, :] = jnp.max(largest, axis=0, keepdims=True)
        for q in range(4):
            for p in range(TPD):
                at = q * 4 + p
                ns_own[step, 0, at : at + 1, :] = U[p, q, TILE - 1 : TILE, :]
                ns_own[step, 1, at : at + 1, :] = U[p, q, 0:1, :]

    def halos(step):
        return [
            pltpu.make_async_remote_copy(
                ew_own.at[step, 0], ew_got.at[step, 1], ew_send.at[step, 0], ew_recv.at[step, 1],
                device_id=(east,), device_id_type=MESH),
            pltpu.make_async_remote_copy(
                ew_own.at[step, 1], ew_got.at[step, 0], ew_send.at[step, 1], ew_recv.at[step, 0],
                device_id=(west,), device_id_type=MESH),
            pltpu.make_async_remote_copy(
                ns_own.at[step, 0], ns_got.at[step, 1], ns_send.at[step, 0], ns_recv.at[step, 1],
                device_id=(north,), device_id_type=MESH),
            pltpu.make_async_remote_copy(
                ns_own.at[step, 1], ns_got.at[step, 0], ns_send.at[step, 1], ns_recv.at[step, 0],
                device_id=(south,), device_id_type=MESH),
        ]

    def send(step):
        for n, (offset, target) in enumerate(everyone):
            if n == 2:
                for copy in halos(step):
                    copy.start()
            pltpu.make_async_remote_copy(
                mbuf.at[step, 0:1], mbuf.at[step, offset : offset + 1],
                mx_send.at[step], mx_recv.at[step],
                device_id=(target,), device_id_type=MESH).start()

    def all_rows(step, sem):
        rest = mbuf.at[step, 1:DEVICES]
        return pltpu.make_async_copy(rest, rest, sem.at[step])

    def ground_slopes():
        def block(i, below):
            blk = rows_of(i)
            nxt = rows_of(jnp.minimum(i + 1, BLOCKS - 1))
            top_row = jnp.where(i == BLOCKS - 1, 7, -1)
            here = [G[p, blk, :] for p in range(TPD)]
            turned = [pltpu.roll(g, TILE - 1, 1) for g in here]
            back = zero
            new_below = []
            for p in range(TPD):
                g = here[p]
                if p < TPD - 1:
                    de = jnp.where(last_lane, turned[p + 1], turned[p]) - g
                    de = jnp.where(lane == wall_lane[p], 0.0, de)
                else:
                    de = jnp.where(last_lane, 0.0, turned[p] - g)
                round_de = pltpu.roll(de, 1, 1)
                dw = jnp.where(first_lane, back, round_de)
                back = round_de
                KX[p, blk, :] = (0.5 * GRAVITY) * (de + dw)
                up = jnp.where(sub == 7, pltpu.roll(G[p, nxt, :], 7, 0), pltpu.roll(g, 7, 0))
                dn = jnp.where(sub == top_row, 0.0, up - g)
                round_dn = pltpu.roll(dn, 1, 0)
                ds = jnp.where(sub == 0, below[p], round_dn)
                new_below.append(round_dn)
                KY[p, blk, :] = (0.5 * GRAVITY) * (dn + ds)
            return tuple(new_below)

        lax.fori_loop(0, BLOCKS, block, (zero,) * TPD)

    def right_sides():
        def derive(i, _):
            blk = rows_of(i)
            for p in range(TPD):
                h, mx, my = (U[p, q, blk, :] for q in range(3))
                inv, c = derived(h, mx, my)
                u, au = wave(h, mx, inv, c)
                v, av = wave(h, my, inv, c)
                still = (0.5 * GRAVITY) * h * h
                D[p, 0, blk, :] = au
                D[p, 1, blk, :] = av
                D[p, 2, blk, :] = mx * u + still
                D[p, 3, blk, :] = mx * v
                D[p, 4, blk, :] = my * v + still
            return 0

        lax.fori_loop(0, BLOCKS, derive, 0, unroll=4)

        def block(i, below):
            blk = rows_of(i)
            nxt = rows_of(jnp.minimum(i + 1, BLOCKS - 1))
            top_row = jnp.where(i == BLOCKS - 1, 7, -1)
            new_below = []
            after_turned = None
            east_faces = [None] * TPD
            sides = [None] * TPD
            for p in reversed(range(TPD)):
                h, mx, my, hd = (U[p, q, blk, :] for q in range(4))
                au, fxx, fxy = D[p, 0, blk, :], D[p, 2, blk, :], D[p, 3, blk, :]
                own = (h, mx, my, hd, au, fxx, fxy)
                turned = [pltpu.roll(value, TILE - 1, 1) for value in own]
                if after_turned is None:
                    he, me_, ye, de, ae, xe, ce = turned
                else:
                    he, me_, ye, de, ae, xe, ce = (
                        jnp.where(last_lane, b, a) for a, b in zip(turned, after_turned)
                    )
                after_turned = turned
                speed = jnp.maximum(au, ae)
                g0 = (mx + me_) - speed * (he - h)
                g1 = (fxx + xe) - speed * (me_ - mx)
                g2 = (fxy + ce) - speed * (ye - my)
                g3 = de - hd
                step_out = au * mx
                if p == TPD - 1:
                    wall, push = last_lane, 0.0
                else:
                    wall, push = lane == wall_lane[p], 2.0 * (fxx + step_out)
                g0 = jnp.where(wall, 0.0, g0)
                g1 = jnp.where(wall, push, g1)
                g2 = jnp.where(wall, 0.0, g2)
                g3 = jnp.where(wall, 0.0, g3)
                east_faces[p] = (g0, g1, g2, g3)
                sides[p] = 2.0 * (fxx - step_out)
            back = (zero,) * 4
            for p in range(TPD):
                rounds = [pltpu.roll(g, 1, 1) for g in east_faces[p]]
                west_faces = [jnp.where(first_lane, b, a) for a, b in zip(rounds, back)]
                if p > 0:
                    west_faces[1] = jnp.where(lane == wall_back[p], sides[p], west_faces[1])
                back = rounds
                x0, x1, x2, x3 = (e - w for e, w in zip(east_faces[p], west_faces))

                h, mx, my, hd = (U[p, q, blk, :] for q in range(4))
                av, fxy, fyy = D[p, 1, blk, :], D[p, 3, blk, :], D[p, 4, blk, :]
                own = (h, mx, my, hd, av, fxy, fyy)
                ups = (U[p, 0, nxt, :], U[p, 1, nxt, :], U[p, 2, nxt, :], U[p, 3, nxt, :],
                       D[p, 1, nxt, :], D[p, 3, nxt, :], D[p, 4, nxt, :])
                hn, xn, mn, dn, an, cn, yn = (
                    jnp.where(sub == 7, pltpu.roll(b, 7, 0), pltpu.roll(a, 7, 0))
                    for a, b in zip(own, ups)
                )
                speed = jnp.maximum(av, an)
                f0 = (my + mn) - speed * (hn - h)
                f1 = (fyy + yn) - speed * (mn - my)
                f2 = (fxy + cn) - speed * (xn - mx)
                f3 = dn - hd
                faces = [jnp.where(sub == top_row, 0.0, f) for f in (f0, f1, f2, f3)]
                rounds = [pltpu.roll(f, 1, 0) for f in faces]
                lower = [jnp.where(sub == 0, b, a) for a, b in zip(rounds, below[4 * p : 4 * p + 4])]
                new_below.extend(rounds)
                y0, y1, y2, y3 = (n - s for n, s in zip(faces, lower))

                seep = L[p, blk, :] * (h + G[p, blk, :] - hd)
                R[p, 0, blk, :] = -0.5 * (x0 + y0) - seep
                R[p, 1, blk, :] = -0.5 * (x1 + y2) - h * KX[p, blk, :]
                R[p, 2, blk, :] = -0.5 * (x2 + y1) - h * KY[p, blk, :]
                R[p, 3, blk, :] = S[p, blk, :] * (x3 + y3) + seep * (1.0 / STORAGE)
            return tuple(new_below)

        lax.fori_loop(0, BLOCKS, block, (zero,) * (4 * TPD), unroll=2)

    def column_terms(own, got, link, flip_east):
        ghost = jnp.where(link >= 0, got, jnp.where(lane // BLOCKS == 1, -own, own))
        part = lambda packed, q: packed if q == 0 else pltpu.roll(packed, TILE - q * BLOCKS, 1)
        h, n, a, hd, g = (part(own, q) for q in range(5))
        gh, gn, ga, ghd, gg = (part(ghost, q) for q in range(5))
        if flip_east:
            mass, push, carry = face(h, n, a, gh, gn, ga)
            sign = -0.5
        else:
            mass, push, carry = face(gh, gn, ga, h, n, a)
            sign = 0.5
        slope = (0.5 * GRAVITY) * h * ((gg - g) if flip_east else (g - gg))
        return sign * mass, sign * push - slope, sign * carry, ghd - hd

    def row_terms(own, got, k, is_north):
        rows = lax.broadcasted_iota(jnp.int32, (TPD, TILE), 0)
        link = jnp.full((TPD, TILE), linked[0][k], jnp.int32)
        for p in range(1, TPD):
            link = jnp.where(rows == p, linked[p][k], link)
        mine = [own[q * 4 : q * 4 + 4, :] for q in range(5)]
        signs = (1.0, 1.0, -1.0, 1.0, 1.0)
        ghost = [
            jnp.where(link >= 0, got[q * 4 : q * 4 + 4, :], signs[q] * mine[q]) for q in range(5)
        ]
        h, a, n, hd, g = mine
        gh, ga, gn, ghd, gg = ghost
        if is_north:
            mass, push, carry = face(h, n, a, gh, gn, ga)
            sign = -0.5
        else:
            mass, push, carry = face(gh, gn, ga, h, n, a)
            sign = 0.5
        slope = (0.5 * GRAVITY) * h * ((gg - g) if is_north else (g - gg))
        return sign * mass, sign * carry, sign * push - slope, ghd - hd

    def rims(step):
        for copy in halos(step):
            copy.wait_recv()
        for side, p, edge in ((0, TPD - 1, True), (1, 0, False)):
            terms = column_terms(
                ew_own[step, side], ew_got[step, side], linked[p][1 - side], edge
            )
            at_edge = last_lane if edge else first_lane

            for i in range(BLOCKS):
                blk = rows_of(i)
                shift = (TILE - 1 - i) if edge else (TILE - i) % TILE
                for q in range(4):
                    add = pltpu.roll(terms[q], shift, 1)
                    if q == 3:
                        add = add * S[p, blk, :]
                    R[p, q, blk, :] += jnp.where(at_edge, add, 0.0)
        for side, at in ((0, TILE - 1), (1, 0)):
            terms = row_terms(ns_own.at[step, side], ns_got.at[step, side], 3 - side, side == 0)
            for p in range(TPD):
                for q in range(4):
                    add = terms[q][p : p + 1, :]
                    if q == 3:
                        add = add * S[p, at : at + 1, :]
                    R[p, q, at : at + 1, :] += add

    def interval(step):
        all_rows(step, mx_recv).wait()
        top = jnp.max(jnp.max(mbuf[step], axis=0, keepdims=True), axis=1, keepdims=True)
        dt = COURANT / jnp.broadcast_to(top, (8, TILE))
        return dt, [jnp.where(wet[p] == 1, dt, 0.0) for p in range(TPD)]

    sweep(0, None)
    pl.semaphore_wait(barrier, DEVICES - 1)

    def ranked(flags, values):
        count = jnp.int32(0)
        picks = [jnp.int32(0)] * MOVE
        for flag, value in zip(flags, values):
            for j in range(MOVE):
                picks[j] = jnp.where(jnp.logical_and(flag, count == j), value, picks[j])
            count = count + flag.astype(jnp.int32)
        return picks

    mine = [dest_ref[base + t] for t in range(TPD)]
    leaving = [
        ranked([d >= base + TPD for d in mine], slot),
        ranked([d < base for d in mine], slot),
    ]
    wanted = [jnp.int32(0)] * TPD
    wanted_wet = [jnp.int32(0)] * TPD

    def offer(flag, goes, tile, tile_wet):
        for k in range(TPD):
            here = jnp.logical_and(flag, goes == base + k)
            wanted[k] = jnp.where(here, tile, wanted[k])
            wanted_wet[k] = jnp.where(here, tile_wet, wanted_wet[k])

    for t in range(TPD):
        offer(mine[t] >= base, mine[t], slot[t], wet_ref[base + t])
    for first_slot, side, reach in ((before * TPD, 0, me > 0), (after * TPD, 1, me < DEVICES - 1)):
        rank = jnp.int32(0)
        for t in range(TPD):
            goes = dest_ref[first_slot + t]
            comes = goes >= base if side == 0 else goes < base + TPD
            comes = jnp.logical_and(reach, comes)
            tile = TPD + side * MOVE + jnp.minimum(rank, MOVE - 1)
            offer(comes, goes, tile, wet_ref[first_slot + t])
            rank = rank + comes.astype(jnp.int32)

    def grounds(kind):
        return [
            pltpu.make_async_remote_copy(
                mover_ground.at[side, kind], arrived_ground.at[side, kind],
                mg_send.at[side, kind], mg_recv.at[side, kind],
                device_id=(target,), device_id_type=MESH)
            for side, target in ((0, after), (1, before))
        ]

    PIECES = ((0, 0, TILE), (1, 0, TILE // 2), (1, TILE // 2, TILE // 2))

    def fields_of(piece):
        j, start, count = PIECES[piece]
        rows = pl.ds(start, count)
        return [
            pltpu.make_async_remote_copy(
                movers.at[side, j, :, rows, :], U.at[TPD + side * MOVE + j, :, rows, :],
                mv_send.at[side, piece], mv_recv.at[side, piece],
                device_id=(target,), device_id_type=MESH)
            for side, target in ((0, after), (1, before))
        ]

    def lines():
        return [
            pltpu.make_async_remote_copy(
                line_own.at[side], line_got.at[side], ln_send.at[side], ln_recv.at[side],
                device_id=(target,), device_id_type=MESH)
            for side, target in ((0, after), (1, before))
        ]

    def outer_lines():
        for side in range(2):
            for j in range(MOVE):
                tile = leaving[side][j]
                acc = zero
                for q in range(4):
                    line_own[side, j, q : q + 1, :] = R[tile, q, TILE - 1 : TILE, :]
                    line_own[side, j, 4 + q : 5 + q, :] = R[tile, q, 0:1, :]
                    for i in range(BLOCKS):
                        value = R[tile, q, rows_of(i), :]
                        at = q * BLOCKS + i
                        acc = jnp.where(lane == at, pltpu.roll(value, at, 1), acc)
                        at += TILE // 2
                        acc = jnp.where(lane == at, pltpu.roll(value, (at + 1) % TILE, 1), acc)
                line_own[side, j, 8:16, :] = acc

    def arrived_sides(j):
        def derive(i, _):
            blk = rows_of(i)
            for side in range(2):
                h, mx, my = (U[TPD + side * MOVE + j, q, blk, :] for q in range(3))
                inv, c = derived(h, mx, my)
                u, au = wave(h, mx, inv, c)
                v, av = wave(h, my, inv, c)
                still = (0.5 * GRAVITY) * h * h
                DA[side, 0, blk, :] = au
                DA[side, 1, blk, :] = av
                DA[side, 2, blk, :] = mx * u + still
                DA[side, 3, blk, :] = mx * v
                DA[side, 4, blk, :] = my * v + still
            return 0


        def block(i, below):
            blk = rows_of(i)
            nxt = rows_of(jnp.minimum(i + 1, BLOCKS - 1))
            new_below = []
            for side in range(2):
                old = below[5 * side : 5 * side + 5]
                h, mx, my, hd = (U[TPD + side * MOVE + j, q, blk, :] for q in range(4))
                g = arrived_ground[side, 0, j, blk, :]
                au, av, fxx, fxy, fyy = (DA[side, n, blk, :] for n in range(5))
                he, me_, ye, de, ae, xe, ce = (
                    pltpu.roll(value, TILE - 1, 1) for value in (h, mx, my, hd, au, fxx, fxy)
                )
                speed = jnp.maximum(au, ae)
                east_faces = (
                    (mx + me_) - speed * (he - h),
                    (fxx + xe) - speed * (me_ - mx),
                    (fxy + ce) - speed * (ye - my),
                    de - hd,
                )
                x0, x1, x2, x3 = (f - pltpu.roll(f, 1, 1) for f in east_faces)
                kx = (0.5 * GRAVITY) * (pltpu.roll(g, TILE - 1, 1) - pltpu.roll(g, 1, 1))
                ups = [U[TPD + side * MOVE + j, q, nxt, :] for q in range(4)]
                ups += [DA[side, n, nxt, :] for n in (1, 3, 4)]
                ups.append(arrived_ground[side, 0, j, nxt, :])
                hn, xn, mn, dn, an, cn, yn, gn = (
                    jnp.where(sub == 7, pltpu.roll(b, 7, 0), pltpu.roll(a, 7, 0))
                    for a, b in zip((h, mx, my, hd, av, fxy, fyy, g), ups)
                )
                speed = jnp.maximum(av, an)
                faces = (
                    (my + mn) - speed * (hn - h),
                    (fyy + yn) - speed * (mn - my),
                    (fxy + cn) - speed * (xn - mx),
                    dn - hd,
                    gn - g,
                )
                rounds = [pltpu.roll(f, 1, 0) for f in faces]
                lower = [jnp.where(sub == 0, b, a) for a, b in zip(rounds, old)]
                new_below.extend(rounds)
                y0, y1, y2, y3 = (n - s for n, s in zip(faces[:4], lower[:4]))
                ky = (0.5 * GRAVITY) * (faces[4] + lower[4])
                seep = arrived_ground[side, 1, j, blk, :] * (h + g - hd)
                R[TPD + side * MOVE + j, 0, blk, :] = -0.5 * (x0 + y0) - seep
                R[TPD + side * MOVE + j, 1, blk, :] = -0.5 * (x1 + y2) - h * kx
                R[TPD + side * MOVE + j, 2, blk, :] = -0.5 * (x2 + y1) - h * ky
                R[TPD + side * MOVE + j, 3, blk, :] = (
                    arrived_ground[side, 2, j, blk, :] * (x3 + y3) + seep * (1.0 / STORAGE)
                )
            return tuple(new_below)

        below = (zero,) * 10
        for piece, (tile, start, count) in enumerate(PIECES):
            if tile != j:
                continue
            for copy in fields_of(piece):
                copy.wait_recv()
            lo, hi = start // 8, (start + count) // 8
            lax.fori_loop(lo, hi, derive, 0, unroll=4)
            first = lo - 1 if lo else 0
            last = hi - 1 if hi < BLOCKS else BLOCKS
            below = lax.fori_loop(first, last, block, below, unroll=2 if (last - first) % 2 == 0 else 3)

    def fill_lines(tile):
        side, j = divmod(tile - TPD, MOVE)
        cols = line_got[side, j, 8:16, :]
        for q in range(4):
            for i in range(BLOCKS):
                blk = rows_of(i)
                rate = R[tile, q, blk, :]
                at = q * BLOCKS + i
                rate = jnp.where(first_lane, pltpu.roll(cols, (TILE - at) % TILE, 1), rate)
                rate = jnp.where(last_lane, pltpu.roll(cols, TILE // 2 - 1 - at, 1), rate)
                if i == 0:
                    rate = jnp.where(sub == 0, line_got[side, j, 4 + q : 5 + q, :], rate)
                if i == BLOCKS - 1:
                    rate = jnp.where(sub == 7, line_got[side, j, q : q + 1, :], rate)
                R[tile, q, blk, :] = rate

    def body(step, _):
        send(step)

        @pl.when(step == 0)
        def _():
            for load in late:
                load.wait()
            ground_slopes()
            for side in range(2):
                for j in range(MOVE):
                    for kind, array in enumerate((G, L, S)):
                        mover_ground[side, kind, j] = array[leaving[side][j]]

        for copy in grounds(step):
            copy.start()
        right_sides()
        rims(step)
        sweep(step + 1, interval(step)[1])
        return 0

    lax.fori_loop(0, STEPS - 1, body, 0)

    final = STEPS - 1
    send(final)
    for j in range(MOVE):
        for q in range(4):
            for i in range(BLOCKS):
                blk = rows_of(i)
                own = [U[p, q, blk, :] for p in range(TPD)]
                for side in range(2):
                    value = own[0]
                    for p in range(1, TPD):
                        value = jnp.where(leaving[side][j] == p, own[p], value)
                    movers[side, j, q, blk, :] = value
        for piece in range(len(PIECES)):
            if PIECES[piece][0] == j:
                for copy in fields_of(piece):
                    copy.start()
    right_sides()
    rims(final)
    outer_lines()
    for copy in lines():
        copy.start()
    for kind in range(3):
        for copy in grounds(kind):
            copy.wait_recv()
    for j in range(MOVE):
        arrived_sides(j)
    for copy in lines():
        copy.wait_recv()
    for tile in range(TPD, TPD + 2 * MOVE):
        fill_lines(tile)
    dt = interval(final)[0]
    keeps = []
    for k in range(TPD):
        tile, tile_wet = wanted[k], wanted_wet[k]
        dt_k = jnp.where(tile_wet == 1, dt, 0.0)
        for q in range(4):
            for i in range(BLOCKS):
                blk = rows_of(i)
                made[k, q, blk, :] = U[tile, q, blk, :] + dt_k * R[tile, q, blk, :]
        keep = pltpu.make_async_copy(made.at[k], tiles_out.at[k], out_sem.at[k])
        keep.start()
        keeps.append(keep)
    for step in range(STEPS):
        all_rows(step, mx_send).wait()
        for copy in halos(step):
            copy.wait_send()
    for kind in range(3):
        for copy in grounds(kind):
            copy.wait_send()
    for piece in range(len(PIECES)):
        for copy in fields_of(piece):
            copy.wait_send()
    for copy in lines():
        copy.wait_send()
    for keep in keeps:
        keep.wait()


def split_kernel(tiles, depth_out, flow_out, head_out, held, in_sem, sem):
    fetches = [
        pltpu.make_async_copy(tiles.at[k], held.at[k], in_sem.at[k]) for k in range(TPD)
    ]
    for fetch in fetches:
        fetch.start()
    copies = []
    for k in range(TPD):
        fetches[k].wait()
        for n, (part, out) in enumerate(
            ((held.at[k, 0], depth_out), (held.at[k, 1:3], flow_out), (held.at[k, 3], head_out))
        ):
            copy = pltpu.make_async_copy(part, out.at[k], sem.at[n, k])
            copy.start()
            copies.append(copy)
    for copy in copies:
        copy.wait()


def shards(depth, velocity, head, terrain, leakance, diffusivity, tile_wet, neighbours, destination):
    hbm = pl.BlockSpec(memory_space=pltpu.HBM)
    smem = pl.BlockSpec(memory_space=pltpu.SMEM)
    vm = lambda *shape: pltpu.VMEM(shape + (TILE,), F32)
    dma = pltpu.SemaphoreType.DMA
    made = pl.pallas_call(
        flood_kernel,
        out_shape=jax.ShapeDtypeStruct((TPD, 4, TILE, TILE), F32),
        in_specs=[smem] * 3 + [hbm] * 6,
        out_specs=hbm,
        scratch_shapes=[
            vm(TPD + 2 * MOVE, 4, TILE), vm(TPD, 5, TILE), vm(TPD + 2 * MOVE, 4, TILE),
            vm(TPD, TILE), vm(TPD, TILE), vm(TPD, TILE), vm(TPD, TILE), vm(TPD, TILE),
            vm(TPD, 2, TILE), vm(STEPS, DEVICES),
            vm(STEPS, 2, 8), vm(STEPS, 2, 8), vm(STEPS, 2, 24), vm(STEPS, 2, 24),
            vm(2, MOVE, 4, TILE), vm(2, 3, MOVE, TILE), vm(2, 3, MOVE, TILE),
            vm(2, 5, TILE), vm(2, MOVE, 16), vm(2, MOVE, 16), vm(TPD, 4, TILE),
            dma((6, TPD)), dma((STEPS,)), dma((STEPS,)),
            dma((STEPS, 2)), dma((STEPS, 2)), dma((STEPS, 2)), dma((STEPS, 2)),
            dma((2, 3)), dma((2, 3)), dma((2, 3)), dma((2, 3)), dma((2,)), dma((2,)),
            dma((TPD,)),
        ],
        compiler_params=pltpu.CompilerParams(
            collective_id=0, has_side_effects=True, vmem_limit_bytes=60 << 20
        ),
    )(tile_wet, neighbours.T, destination, depth, velocity, head, terrain, leakance, diffusivity)
    tile = jax.ShapeDtypeStruct((TPD, TILE, TILE), F32)
    return pl.pallas_call(
        split_kernel,
        out_shape=(tile, jax.ShapeDtypeStruct((TPD, 2, TILE, TILE), F32), tile),
        in_specs=[hbm],
        out_specs=(hbm,) * 3,
        scratch_shapes=[vm(TPD, 4, TILE), dma((TPD,)), dma((3, TPD))],
    )(made)


def solution(mesh):
    tiles = P("tiles", None, None)
    pair = P("tiles", None, None, None)
    return jax.shard_map(
        shards,
        mesh=mesh,
        in_specs=(tiles, pair, tiles, tiles, tiles, tiles, P(), P(), P()),
        out_specs=(tiles, pair, tiles),
        check_vma=False,
    )
```

```python
import functools
import math

import jax
import jax.numpy as jnp
from jax import lax
from jax.experimental import pallas as pl
from jax.experimental.pallas import tpu as pltpu
from jax.sharding import PartitionSpec as P

MESH = pl.DeviceIdType.MESH
TPD = 4
MOVE = 2
STEPS = 4
TILE = 128
BLOCKS = TILE // 8
GRAVITY = 9.81
ROOT_G = math.sqrt(GRAVITY)
SHALLOW = 0.1
COURANT = 0.45
STORAGE = 0.2
LOWEST = 2.0 * math.sqrt(GRAVITY * SHALLOW)
DEVICES = 128
F32 = jnp.float32


def peers(me):
    core = lax.rem(me, 2)
    y = lax.rem(me // 2, 4)
    z = lax.rem(me // 8, 4)
    x = me // 32
    xs = [lax.rem(x + d, 4) * 32 for d in range(4)]
    zs = [lax.rem(z + d, 4) * 8 for d in range(4)]
    ys = [lax.rem(y + d, 4) * 2 for d in range(4)]
    cs = [core, 1 - core]
    xz = [[a + b for b in zs] for a in xs]
    yc = [[a + b for b in cs] for a in ys]
    found = []
    for dx in range(4):
        for dz in range(4):
            for dy in range(4):
                for dc in range(2):
                    offset = ((dx * 4 + dz) * 4 + dy) * 2 + dc
                    if offset:
                        hops = sum(min(d, 4 - d) for d in (dx, dz, dy))
                        found.append((hops, offset, xz[dx][dz] + yc[dy][dc]))
    found.sort(key=lambda item: -item[0])
    return [(offset, target) for _, offset, target in found]


def derived(h, mx, my):
    s = jnp.maximum(h, SHALLOW)
    r = lax.rsqrt(s)
    inv = r * r
    c = (ROOT_G * s) * r
    return inv, c


def wave(h, n, inv, c):
    u = n * inv
    return u, jnp.abs(u) + c


def face(h1, n1, a1, h2, n2, a2):
    inv1, c1 = derived(h1, n1, a1)
    inv2, c2 = derived(h2, n2, a2)
    u1, w1 = wave(h1, n1, inv1, c1)
    u2, w2 = wave(h2, n2, inv2, c2)
    speed = jnp.maximum(w1, w2)
    half_g = 0.5 * GRAVITY
    mass = (n1 + n2) - speed * (h2 - h1)
    push = (n1 * u1 + half_g * h1 * h1 + n2 * u2 + half_g * h2 * h2) - speed * (n2 - n1)
    carry = (a1 * u1 + a2 * u2) - speed * (a2 - a1)
    return mass, push, carry


def flood_kernel(
    wet_ref, link_ref, dest_ref, depth_in, vel_in, head_in, terr_in, leak_in, diff_in,
    tiles_out,
    U, D, R, G, L, S, KX, KY, VEL, mbuf, mtop, ew_own, ew_got, ns_own, ns_got,
    movers, mover_ground, arrived_ground, slopes, DA, line_own, line_got, made,
    in_sem, mx_send, mx_recv, mt_sem, ew_send, ew_recv, ns_send, ns_recv, mv_send, mv_recv,
    mg_send, mg_recv, ln_send, ln_recv, out_sem,
):
    me = lax.axis_index("tiles")
    row = me // 4
    col = lax.rem(me, 4)
    odd = lax.rem(row, 2)
    place = col + odd * (3 - 2 * col)
    base = me * TPD

    def device_at(r, c):
        o = lax.rem(r, 2)
        return r * 4 + c + o * (3 - 2 * c)

    east = device_at(row, lax.rem(place + 1, 4))
    west = device_at(row, lax.rem(place + 3, 4))
    north = device_at(lax.rem(row + 1, 32), place)
    south = device_at(lax.rem(row + 31, 32), place)
    after = lax.rem(me + 1, DEVICES)
    before = lax.rem(me + DEVICES - 1, DEVICES)
    everyone = peers(me)
    slot = [p + odd * (3 - 2 * p) for p in range(TPD)]

    loads = []
    for n, (array, place_of) in enumerate((
        (depth_in, lambda p: U.at[p, 0]), (vel_in, lambda p: VEL.at[p]),
        (head_in, lambda p: U.at[p, 3]), (terr_in, lambda p: G.at[p]),
        (leak_in, lambda p: L.at[p]), (diff_in, lambda p: S.at[p]),
    )):
        for p in range(TPD):
            loads.append(pltpu.make_async_copy(array.at[slot[p]], place_of(p), in_sem.at[n, p]))
    early, late = loads[: 4 * TPD], loads[4 * TPD :]

    barrier = pltpu.get_barrier_semaphore()

    def announce(some):
        for _, target in some:
            pl.semaphore_signal(barrier, inc=1, device_id=(target,), device_id_type=MESH)

    for load in early:
        load.start()
    announce(everyone)
    for load in late:
        load.start()

    wet = [wet_ref[base + slot[p]] for p in range(TPD)]
    linked = [[link_ref[k, base + slot[p]] for k in range(4)] for p in range(TPD)]
    lane = lax.broadcasted_iota(jnp.int32, (8, TILE), 1)
    sub = lax.broadcasted_iota(jnp.int32, (8, TILE), 0)
    first_lane = lane == 0
    last_lane = lane == TILE - 1
    half_lane = lane // 2
    wall_lane = [jnp.where(linked[p][1] >= 0, -1, TILE - 1) for p in range(TPD - 1)]
    wall_back = [jnp.where(linked[p][0] >= 0, -1, 0) for p in range(TPD)]
    zero = jnp.zeros((8, TILE), F32)

    def rows_of(i):
        return pl.ds(i * 8 if isinstance(i, int) else pl.multiple_of(i * 8, 8), 8)

    def pack(i, q, value, acc, edge):
        lane_at = q * BLOCKS + i
        shift = (lane_at + (1 if edge else 0)) % TILE
        return jnp.where(lane == lane_at, pltpu.roll(value, shift, 1), acc)

    for load in early:
        load.wait()

    def ground_block(i, carry):
        acc_e, acc_w = carry
        blk = rows_of(i)
        acc_e = pack(i, 4, G[TPD - 1, blk, :], acc_e, True)
        acc_w = pack(i, 4, G[0, blk, :], acc_w, False)
        return acc_e, acc_w

    ground_e = ground_w = zero
    for i in range(BLOCKS):
        ground_e, ground_w = ground_block(i, (ground_e, ground_w))
    for s in range(STEPS):
        for p in range(TPD):
            ns_own[s, 0, 16 + p : 17 + p, :] = G[p, TILE - 1 : TILE, :]
            ns_own[s, 1, 16 + p : 17 + p, :] = G[p, 0:1, :]
        for k in range(2):
            ns_own[s, k, 20:24, :] = jnp.zeros((4, TILE), F32)

    def sweep(step, dt_of):
        def block(i, carry):
            acc_e, acc_w, top = carry
            blk = rows_of(i)
            top = list(top)
            for p in range(TPD):
                if dt_of is None:
                    h = U[p, 0, blk, :]
                    mx = h * VEL[p, 0, blk, :]
                    my = h * VEL[p, 1, blk, :]
                    hd = U[p, 3, blk, :]
                    U[p, 1, blk, :] = mx
                    U[p, 2, blk, :] = my
                else:
                    new = [U[p, q, blk, :] + dt_of[p] * R[p, q, blk, :] for q in range(4)]
                    for q in range(4):
                        U[p, q, blk, :] = new[q]
                    h, mx, my, hd = new
                inv, c = derived(h, mx, my)
                top[p] = jnp.maximum(top[p], (jnp.abs(mx) + jnp.abs(my)) * inv + 2.0 * c)
                if p == TPD - 1:
                    for q, value in enumerate((h, mx, my, hd)):
                        acc_e = pack(i, q, value, acc_e, True)
                if p == 0:
                    for q, value in enumerate((h, mx, my, hd)):
                        acc_w = pack(i, q, value, acc_w, False)
            return acc_e, acc_w, tuple(top)

        state = (ground_e, ground_w, (zero,) * TPD)
        for i in range(BLOCKS):
            state = block(i, state)
        acc_e, acc_w, top = state
        ew_own[step, 0] = acc_e
        ew_own[step, 1] = acc_w
        largest = jnp.full((8, TILE), LOWEST, F32)
        for p in range(TPD):
            largest = jnp.maximum(largest, jnp.where(wet[p] == 1, top[p], LOWEST))
        mbuf[step, 0:1, :] = jnp.max(largest, axis=0, keepdims=True)
        for q in range(4):
            for p in range(TPD):
                at = q * 4 + p
                ns_own[step, 0, at : at + 1, :] = U[p, q, TILE - 1 : TILE, :]
                ns_own[step, 1, at : at + 1, :] = U[p, q, 0:1, :]

    def halos(step):
        return [
            pltpu.make_async_remote_copy(
                ew_own.at[step, 0], ew_got.at[step, 1], ew_send.at[step, 0], ew_recv.at[step, 1],
                device_id=(east,), device_id_type=MESH),
            pltpu.make_async_remote_copy(
                ew_own.at[step, 1], ew_got.at[step, 0], ew_send.at[step, 1], ew_recv.at[step, 0],
                device_id=(west,), device_id_type=MESH),
            pltpu.make_async_remote_copy(
                ns_own.at[step, 0], ns_got.at[step, 1], ns_send.at[step, 0], ns_recv.at[step, 1],
                device_id=(north,), device_id_type=MESH),
            pltpu.make_async_remote_copy(
                ns_own.at[step, 1], ns_got.at[step, 0], ns_send.at[step, 1], ns_recv.at[step, 0],
                device_id=(south,), device_id_type=MESH),
        ]

    def send(step):
        for n, (offset, target) in enumerate(everyone):
            if n == 2:
                for copy in halos(step):
                    copy.start()
            pltpu.make_async_remote_copy(
                mbuf.at[step, 0:1], mbuf.at[step, offset : offset + 1],
                mx_send.at[step], mx_recv.at[step],
                device_id=(target,), device_id_type=MESH).start()

    def all_rows(step, sem, rows=DEVICES):
        rest = mbuf.at[step, 1:rows]
        return pltpu.make_async_copy(rest, rest, sem.at[step])

    near = [item for item in everyone if item[0] < 8]
    across = [(offset // 8, target) for offset, target in everyone if offset % 8 == 0]

    def send_near(step):
        for offset, target in near:
            pltpu.make_async_remote_copy(
                mbuf.at[step, 0:1], mbuf.at[step, offset : offset + 1],
                mx_send.at[step], mx_recv.at[step],
                device_id=(target,), device_id_type=MESH).start()

    def send_across(step):
        all_rows(step, mx_recv, 8).wait()
        mtop[0:1, :] = jnp.max(mbuf[step, 0:8, :], axis=0, keepdims=True)
        for group, target in across:
            pltpu.make_async_remote_copy(
                mtop.at[0:1], mtop.at[group : group + 1], mt_sem.at[0], mt_sem.at[1],
                device_id=(target,), device_id_type=MESH).start()

    def across_rows(which):
        rest = mtop.at[1:16]
        return pltpu.make_async_copy(rest, rest, mt_sem.at[which])

    def ground_slopes():
        def block(i, below):
            blk = rows_of(i)
            nxt = rows_of(jnp.minimum(i + 1, BLOCKS - 1))
            top_row = jnp.where(i == BLOCKS - 1, 7, -1)
            here = [G[p, blk, :] for p in range(TPD)]
            turned = [pltpu.roll(g, TILE - 1, 1) for g in here]
            back = zero
            new_below = []
            for p in range(TPD):
                g = here[p]
                if p < TPD - 1:
                    de = jnp.where(last_lane, turned[p + 1], turned[p]) - g
                    de = jnp.where(lane == wall_lane[p], 0.0, de)
                else:
                    de = jnp.where(last_lane, 0.0, turned[p] - g)
                round_de = pltpu.roll(de, 1, 1)
                dw = jnp.where(first_lane, back, round_de)
                back = round_de
                KX[p, blk, :] = (0.5 * GRAVITY) * (de + dw)
                up = jnp.where(sub == 7, pltpu.roll(G[p, nxt, :], 7, 0), pltpu.roll(g, 7, 0))
                dn = jnp.where(sub == top_row, 0.0, up - g)
                round_dn = pltpu.roll(dn, 1, 0)
                ds = jnp.where(sub == 0, below[p], round_dn)
                new_below.append(round_dn)
                KY[p, blk, :] = (0.5 * GRAVITY) * (dn + ds)
            return tuple(new_below)

        lax.fori_loop(0, BLOCKS, block, (zero,) * TPD)

    def right_sides():
        def derive(i, _):
            blk = rows_of(i)
            for p in range(TPD):
                h, mx, my = (U[p, q, blk, :] for q in range(3))
                inv, c = derived(h, mx, my)
                u, au = wave(h, mx, inv, c)
                v, av = wave(h, my, inv, c)
                still = (0.5 * GRAVITY) * h * h
                D[p, 0, blk, :] = au
                D[p, 1, blk, :] = av
                D[p, 2, blk, :] = mx * u + still
                D[p, 3, blk, :] = mx * v
                D[p, 4, blk, :] = my * v + still
            return 0

        lax.fori_loop(0, BLOCKS, derive, 0, unroll=4)

        def block(i, below):
            blk = rows_of(i)
            nxt = rows_of(jnp.minimum(i + 1, BLOCKS - 1))
            top_row = jnp.where(i == BLOCKS - 1, 7, -1)
            new_below = []
            after_turned = None
            east_faces = [None] * TPD
            sides = [None] * TPD
            for p in reversed(range(TPD)):
                h, mx, my, hd = (U[p, q, blk, :] for q in range(4))
                au, fxx, fxy = D[p, 0, blk, :], D[p, 2, blk, :], D[p, 3, blk, :]
                own = (h, mx, my, hd, au, fxx, fxy)
                turned = [pltpu.roll(value, TILE - 1, 1) for value in own]
                if after_turned is None:
                    he, me_, ye, de, ae, xe, ce = turned
                else:
                    he, me_, ye, de, ae, xe, ce = (
                        jnp.where(last_lane, b, a) for a, b in zip(turned, after_turned)
                    )
                after_turned = turned
                speed = jnp.maximum(au, ae)
                g0 = (mx + me_) - speed * (he - h)
                g1 = (fxx + xe) - speed * (me_ - mx)
                g2 = (fxy + ce) - speed * (ye - my)
                g3 = de - hd
                step_out = au * mx
                if p == TPD - 1:
                    wall, push = last_lane, 0.0
                else:
                    wall, push = lane == wall_lane[p], 2.0 * (fxx + step_out)
                g0 = jnp.where(wall, 0.0, g0)
                g1 = jnp.where(wall, push, g1)
                g2 = jnp.where(wall, 0.0, g2)
                g3 = jnp.where(wall, 0.0, g3)
                east_faces[p] = (g0, g1, g2, g3)
                sides[p] = 2.0 * (fxx - step_out)
            back = (zero,) * 4
            for p in range(TPD):
                rounds = [pltpu.roll(g, 1, 1) for g in east_faces[p]]
                west_faces = [jnp.where(first_lane, b, a) for a, b in zip(rounds, back)]
                if p > 0:
                    west_faces[1] = jnp.where(lane == wall_back[p], sides[p], west_faces[1])
                back = rounds
                x0, x1, x2, x3 = (e - w for e, w in zip(east_faces[p], west_faces))

                h, mx, my, hd = (U[p, q, blk, :] for q in range(4))
                av, fxy, fyy = D[p, 1, blk, :], D[p, 3, blk, :], D[p, 4, blk, :]
                own = (h, mx, my, hd, av, fxy, fyy)
                ups = (U[p, 0, nxt, :], U[p, 1, nxt, :], U[p, 2, nxt, :], U[p, 3, nxt, :],
                       D[p, 1, nxt, :], D[p, 3, nxt, :], D[p, 4, nxt, :])
                hn, xn, mn, dn, an, cn, yn = (
                    jnp.where(sub == 7, pltpu.roll(b, 7, 0), pltpu.roll(a, 7, 0))
                    for a, b in zip(own, ups)
                )
                speed = jnp.maximum(av, an)
                f0 = (my + mn) - speed * (hn - h)
                f1 = (fyy + yn) - speed * (mn - my)
                f2 = (fxy + cn) - speed * (xn - mx)
                f3 = dn - hd
                faces = [jnp.where(sub == top_row, 0.0, f) for f in (f0, f1, f2, f3)]
                rounds = [pltpu.roll(f, 1, 0) for f in faces]
                lower = [jnp.where(sub == 0, b, a) for a, b in zip(rounds, below[4 * p : 4 * p + 4])]
                new_below.extend(rounds)
                y0, y1, y2, y3 = (n - s for n, s in zip(faces, lower))

                seep = L[p, blk, :] * (h + G[p, blk, :] - hd)
                R[p, 0, blk, :] = -0.5 * (x0 + y0) - seep
                R[p, 1, blk, :] = -0.5 * (x1 + y2) - h * KX[p, blk, :]
                R[p, 2, blk, :] = -0.5 * (x2 + y1) - h * KY[p, blk, :]
                R[p, 3, blk, :] = S[p, blk, :] * (x3 + y3) + seep * (1.0 / STORAGE)
            return tuple(new_below)

        lax.fori_loop(0, BLOCKS, block, (zero,) * (4 * TPD), unroll=2)

    def column_terms(own, got, link, flip_east):
        ghost = jnp.where(link >= 0, got, jnp.where(lane // BLOCKS == 1, -own, own))
        part = lambda packed, q: packed if q == 0 else pltpu.roll(packed, TILE - q * BLOCKS, 1)
        h, n, a, hd, g = (part(own, q) for q in range(5))
        gh, gn, ga, ghd, gg = (part(ghost, q) for q in range(5))
        if flip_east:
            mass, push, carry = face(h, n, a, gh, gn, ga)
            sign = -0.5
        else:
            mass, push, carry = face(gh, gn, ga, h, n, a)
            sign = 0.5
        slope = (0.5 * GRAVITY) * h * ((gg - g) if flip_east else (g - gg))
        return sign * mass, sign * push - slope, sign * carry, ghd - hd

    def row_terms(own, got, k, is_north):
        rows = lax.broadcasted_iota(jnp.int32, (TPD, TILE), 0)
        link = jnp.full((TPD, TILE), linked[0][k], jnp.int32)
        for p in range(1, TPD):
            link = jnp.where(rows == p, linked[p][k], link)
        mine = [own[q * 4 : q * 4 + 4, :] for q in range(5)]
        signs = (1.0, 1.0, -1.0, 1.0, 1.0)
        ghost = [
            jnp.where(link >= 0, got[q * 4 : q * 4 + 4, :], signs[q] * mine[q]) for q in range(5)
        ]
        h, a, n, hd, g = mine
        gh, ga, gn, ghd, gg = ghost
        if is_north:
            mass, push, carry = face(h, n, a, gh, gn, ga)
            sign = -0.5
        else:
            mass, push, carry = face(gh, gn, ga, h, n, a)
            sign = 0.5
        slope = (0.5 * GRAVITY) * h * ((gg - g) if is_north else (g - gg))
        return sign * mass, sign * carry, sign * push - slope, ghd - hd

    def rims(step):
        for copy in halos(step):
            copy.wait_recv()
        for side, p, edge in ((0, TPD - 1, True), (1, 0, False)):
            terms = column_terms(
                ew_own[step, side], ew_got[step, side], linked[p][1 - side], edge
            )
            at_edge = last_lane if edge else first_lane

            for i in range(BLOCKS):
                blk = rows_of(i)
                shift = (TILE - 1 - i) if edge else (TILE - i) % TILE
                for q in range(4):
                    add = pltpu.roll(terms[q], shift, 1)
                    if q == 3:
                        add = add * S[p, blk, :]
                    R[p, q, blk, :] += jnp.where(at_edge, add, 0.0)
        for side, at in ((0, TILE - 1), (1, 0)):
            terms = row_terms(ns_own.at[step, side], ns_got.at[step, side], 3 - side, side == 0)
            for p in range(TPD):
                for q in range(4):
                    add = terms[q][p : p + 1, :]
                    if q == 3:
                        add = add * S[p, at : at + 1, :]
                    R[p, q, at : at + 1, :] += add

    def interval(step):
        if isinstance(step, int):
            across_rows(1).wait()
            tops = mtop[...]
        else:
            all_rows(step, mx_recv).wait()
            tops = mbuf[step]
        top = jnp.max(jnp.max(tops, axis=0, keepdims=True), axis=1, keepdims=True)
        dt = COURANT / jnp.broadcast_to(top, (8, TILE))
        return dt, [jnp.where(wet[p] == 1, dt, 0.0) for p in range(TPD)]

    sweep(0, None)
    pl.semaphore_wait(barrier, DEVICES - 1)

    def ranked(flags, values):
        count = jnp.int32(0)
        picks = [jnp.int32(0)] * MOVE
        for flag, value in zip(flags, values):
            for j in range(MOVE):
                picks[j] = jnp.where(jnp.logical_and(flag, count == j), value, picks[j])
            count = count + flag.astype(jnp.int32)
        return picks

    mine = [dest_ref[base + t] for t in range(TPD)]
    leaving = [
        ranked([d >= base + TPD for d in mine], slot),
        ranked([d < base for d in mine], slot),
    ]
    wanted = [jnp.int32(0)] * TPD
    wanted_wet = [jnp.int32(0)] * TPD

    def offer(flag, goes, tile, tile_wet):
        for k in range(TPD):
            here = jnp.logical_and(flag, goes == base + k)
            wanted[k] = jnp.where(here, tile, wanted[k])
            wanted_wet[k] = jnp.where(here, tile_wet, wanted_wet[k])

    for t in range(TPD):
        offer(mine[t] >= base, mine[t], slot[t], wet_ref[base + t])
    for first_slot, side, reach in ((before * TPD, 0, me > 0), (after * TPD, 1, me < DEVICES - 1)):
        rank = jnp.int32(0)
        for t in range(TPD):
            goes = dest_ref[first_slot + t]
            comes = goes >= base if side == 0 else goes < base + TPD
            comes = jnp.logical_and(reach, comes)
            tile = TPD + side * MOVE + jnp.minimum(rank, MOVE - 1)
            offer(comes, goes, tile, wet_ref[first_slot + t])
            rank = rank + comes.astype(jnp.int32)

    def grounds(kind):
        return [
            pltpu.make_async_remote_copy(
                mover_ground.at[side, kind], arrived_ground.at[side, kind],
                mg_send.at[side, kind], mg_recv.at[side, kind],
                device_id=(target,), device_id_type=MESH)
            for side, target in ((0, after), (1, before))
        ]

    PIECES = ((0, 0, TILE), (1, 0, 104), (1, 104, 24))

    def fields_of(piece):
        j, start, count = PIECES[piece]
        rows = pl.ds(start, count)
        return [
            pltpu.make_async_remote_copy(
                movers.at[side, j, :, rows, :], U.at[TPD + side * MOVE + j, :, rows, :],
                mv_send.at[side, piece], mv_recv.at[side, piece],
                device_id=(target,), device_id_type=MESH)
            for side, target in ((0, after), (1, before))
        ]

    def lines():
        return [
            pltpu.make_async_remote_copy(
                line_own.at[pl.ds(side * MOVE, MOVE)], line_got.at[pl.ds(side * MOVE, MOVE)], ln_send.at[side], ln_recv.at[side],
                device_id=(target,), device_id_type=MESH)
            for side, target in ((0, after), (1, before))
        ]

    def outer_lines():
        for side in range(2):
            for j in range(MOVE):
                tile = leaving[side][j]
                acc = zero
                for q in range(4):
                    line_own[side * MOVE + j, q : q + 1, :] = R[tile, q, TILE - 1 : TILE, :]
                    line_own[side * MOVE + j, 4 + q : 5 + q, :] = R[tile, q, 0:1, :]
                    for i in range(BLOCKS):
                        at = q * BLOCKS + i
                        pair = pltpu.roll(R[tile, q, rows_of(i), :], 2 * at + 1, 1)
                        acc = jnp.where(half_lane == at, pair, acc)
                line_own[side * MOVE + j, 8:16, :] = acc

    def arrived_slopes():
        def block(i, below):
            blk = rows_of(i)
            nxt = rows_of(jnp.minimum(i + 1, BLOCKS - 1))
            new_below = []
            for n in range(2 * MOVE):
                side, j = divmod(n, MOVE)
                g = arrived_ground[side, 0, j, blk, :]
                up = pltpu.roll(arrived_ground[side, 0, j, nxt, :], 7, 0)
                rise = jnp.where(sub == 7, up, pltpu.roll(g, 7, 0)) - g
                back = pltpu.roll(rise, 1, 0)
                new_below.append(back)
                across_x = pltpu.roll(g, TILE - 1, 1) - pltpu.roll(g, 1, 1)
                slopes[side, j, 0, blk, :] = (0.5 * GRAVITY) * across_x
                slopes[side, j, 1, blk, :] = (0.5 * GRAVITY) * (
                    rise + jnp.where(sub == 0, below[n], back)
                )
            return tuple(new_below)

        lax.fori_loop(0, BLOCKS, block, (zero,) * (2 * MOVE), unroll=2)

    def arrived_sides(j):
        def derive(i, _):
            blk = rows_of(i)
            for side in range(2):
                h, mx, my = (U[TPD + side * MOVE + j, q, blk, :] for q in range(3))
                inv, c = derived(h, mx, my)
                u, au = wave(h, mx, inv, c)
                v, av = wave(h, my, inv, c)
                still = (0.5 * GRAVITY) * h * h
                DA[side, 0, blk, :] = au
                DA[side, 1, blk, :] = av
                DA[side, 2, blk, :] = mx * u + still
                DA[side, 3, blk, :] = mx * v
                DA[side, 4, blk, :] = my * v + still
            return 0


        def block(i, below):
            blk = rows_of(i)
            nxt = rows_of(jnp.minimum(i + 1, BLOCKS - 1))
            new_below = []
            for side in range(2):
                old = below[4 * side : 4 * side + 4]
                h, mx, my, hd = (U[TPD + side * MOVE + j, q, blk, :] for q in range(4))
                g = arrived_ground[side, 0, j, blk, :]
                au, av, fxx, fxy, fyy = (DA[side, n, blk, :] for n in range(5))
                he, me_, ye, de, ae, xe, ce = (
                    pltpu.roll(value, TILE - 1, 1) for value in (h, mx, my, hd, au, fxx, fxy)
                )
                speed = jnp.maximum(au, ae)
                east_faces = (
                    (mx + me_) - speed * (he - h),
                    (fxx + xe) - speed * (me_ - mx),
                    (fxy + ce) - speed * (ye - my),
                    de - hd,
                )
                x0, x1, x2, x3 = (f - pltpu.roll(f, 1, 1) for f in east_faces)
                kx, ky = (slopes[side, j, n, blk, :] for n in range(2))
                ups = [U[TPD + side * MOVE + j, q, nxt, :] for q in range(4)]
                ups += [DA[side, n, nxt, :] for n in (1, 3, 4)]
                hn, xn, mn, dn, an, cn, yn = (
                    jnp.where(sub == 7, pltpu.roll(b, 7, 0), pltpu.roll(a, 7, 0))
                    for a, b in zip((h, mx, my, hd, av, fxy, fyy), ups)
                )
                speed = jnp.maximum(av, an)
                faces = (
                    (my + mn) - speed * (hn - h),
                    (fyy + yn) - speed * (mn - my),
                    (fxy + cn) - speed * (xn - mx),
                    dn - hd,
                )
                rounds = [pltpu.roll(f, 1, 0) for f in faces]
                lower = [jnp.where(sub == 0, b, a) for a, b in zip(rounds, old)]
                new_below.extend(rounds)
                y0, y1, y2, y3 = (n - s for n, s in zip(faces, lower))
                seep = arrived_ground[side, 1, j, blk, :] * (h + g - hd)
                R[TPD + side * MOVE + j, 0, blk, :] = -0.5 * (x0 + y0) - seep
                R[TPD + side * MOVE + j, 1, blk, :] = -0.5 * (x1 + y2) - h * kx
                R[TPD + side * MOVE + j, 2, blk, :] = -0.5 * (x2 + y1) - h * ky
                R[TPD + side * MOVE + j, 3, blk, :] = (
                    arrived_ground[side, 2, j, blk, :] * (x3 + y3) + seep * (1.0 / STORAGE)
                )
            return tuple(new_below)

        below = (zero,) * 8
        for piece, (tile, start, count) in enumerate(PIECES):
            if tile != j:
                continue
            for copy in fields_of(piece):
                copy.wait_recv()
            lo, hi = start // 8, (start + count) // 8
            whole = hi - (hi - lo) % 4
            lax.fori_loop(lo, whole, derive, 0, unroll=4)
            for i in range(whole, hi):
                derive(i, 0)
            first = lo - 1 if lo else 0
            last = hi - 1 if hi < BLOCKS else BLOCKS
            below = lax.fori_loop(first, last, block, below, unroll=4)

    def body(step, _):
        send(step)

        @pl.when(step == 0)
        def _():
            for load in late:
                load.wait()
            ground_slopes()
            for side in range(2):
                for j in range(MOVE):
                    for kind, array in enumerate((G, L, S)):
                        mover_ground[side, kind, j] = array[leaving[side][j]]

        for copy in grounds(step):
            copy.start()
        right_sides()
        rims(step)
        sweep(step + 1, interval(step)[1])
        return 0

    lax.fori_loop(0, STEPS - 1, body, 0)

    final = STEPS - 1
    for copy in halos(final):
        copy.start()
    send_near(final)

    def collect(j):
        for q in range(4):
            for i in range(BLOCKS):
                blk = rows_of(i)
                own = [U[p, q, blk, :] for p in range(TPD)]
                for side in range(2):
                    value = own[0]
                    for p in range(1, TPD):
                        value = jnp.where(leaving[side][j] == p, own[p], value)
                    movers[side, j, q, blk, :] = value

    def send_fields(j):
        for piece in range(len(PIECES)):
            if PIECES[piece][0] == j:
                for copy in fields_of(piece):
                    copy.start()

    collect(0)
    send_fields(0)
    collect(1)
    right_sides()
    send_across(final)
    send_fields(1)
    for kind in range(3):
        for copy in grounds(kind):
            copy.wait_recv()
    arrived_slopes()
    rims(final)
    outer_lines()
    for copy in lines():
        copy.start()
    for j in range(MOVE):
        arrived_sides(j)
    for copy in lines():
        copy.wait_recv()
    dt = interval(final)[0]
    keeps = []
    for k in range(TPD):
        tile = wanted[k]
        dt_k = jnp.where(wanted_wet[k] == 1, dt, 0.0)
        guest = tile >= TPD
        line = jnp.maximum(tile - TPD, 0)
        turned_lane = lax.rem(lane + 1, TILE)
        edge_lane = turned_lane < jnp.where(guest, 2, 0)
        south_row = sub == jnp.where(guest, 0, -1)
        north_row = sub == jnp.where(guest, 7, -1)
        cols = line_got[line, 8:16, :]
        rows = line_got[line, 0:8, :]
        for q in range(4):
            for i in range(BLOCKS):
                blk = rows_of(i)
                rate = R[tile, q, blk, :]
                at = q * BLOCKS + i
                rate = jnp.where(edge_lane, pltpu.roll(cols, TILE - 1 - 2 * at, 1), rate)
                if i == 0:
                    rate = jnp.where(south_row, rows[4 + q : 5 + q, :], rate)
                if i == BLOCKS - 1:
                    rate = jnp.where(north_row, rows[q : q + 1, :], rate)
                made[k, q, blk, :] = U[tile, q, blk, :] + dt_k * rate
        keep = pltpu.make_async_copy(made.at[k], tiles_out.at[k], out_sem.at[k])
        keep.start()
        keeps.append(keep)
    for step in range(STEPS):
        all_rows(step, mx_send, DEVICES if step < final else 8).wait()
        for copy in halos(step):
            copy.wait_send()
    across_rows(0).wait()
    for kind in range(3):
        for copy in grounds(kind):
            copy.wait_send()
    for piece in range(len(PIECES)):
        for copy in fields_of(piece):
            copy.wait_send()
    for copy in lines():
        copy.wait_send()
    for keep in keeps:
        keep.wait()


def split_kernel(tiles, depth_out, flow_out, head_out, held, in_sem, sem):
    fetches = [
        pltpu.make_async_copy(tiles.at[k], held.at[k], in_sem.at[k]) for k in range(TPD)
    ]
    for fetch in fetches:
        fetch.start()
    copies = []
    for k in range(TPD):
        fetches[k].wait()
        for n, (part, out) in enumerate(
            ((held.at[k, 0], depth_out), (held.at[k, 1:3], flow_out), (held.at[k, 3], head_out))
        ):
            copy = pltpu.make_async_copy(part, out.at[k], sem.at[n, k])
            copy.start()
            copies.append(copy)
    for copy in copies:
        copy.wait()


def shards(depth, velocity, head, terrain, leakance, diffusivity, tile_wet, neighbours, destination):
    hbm = pl.BlockSpec(memory_space=pltpu.HBM)
    smem = pl.BlockSpec(memory_space=pltpu.SMEM)
    vm = lambda *shape: pltpu.VMEM(shape + (TILE,), F32)
    dma = pltpu.SemaphoreType.DMA
    made = pl.pallas_call(
        flood_kernel,
        out_shape=jax.ShapeDtypeStruct((TPD, 4, TILE, TILE), F32),
        in_specs=[smem] * 3 + [hbm] * 6,
        out_specs=hbm,
        scratch_shapes=[
            vm(TPD + 2 * MOVE, 4, TILE), vm(TPD, 5, TILE), vm(TPD + 2 * MOVE, 4, TILE),
            vm(TPD, TILE), vm(TPD, TILE), vm(TPD, TILE), vm(TPD, TILE), vm(TPD, TILE),
            vm(TPD, 2, TILE), vm(STEPS, DEVICES), vm(16),
            vm(STEPS, 2, 8), vm(STEPS, 2, 8), vm(STEPS, 2, 24), vm(STEPS, 2, 24),
            vm(2, MOVE, 4, TILE), vm(2, 3, MOVE, TILE), vm(2, 3, MOVE, TILE), vm(2, MOVE, 2, TILE),
            vm(2, 5, TILE), vm(2 * MOVE, 16), vm(2 * MOVE, 16), vm(TPD, 4, TILE),
            dma((6, TPD)), dma((STEPS,)), dma((STEPS,)), dma((2,)),
            dma((STEPS, 2)), dma((STEPS, 2)), dma((STEPS, 2)), dma((STEPS, 2)),
            dma((2, 3)), dma((2, 3)), dma((2, 3)), dma((2, 3)), dma((2,)), dma((2,)),
            dma((TPD,)),
        ],
        compiler_params=pltpu.CompilerParams(
            collective_id=0, has_side_effects=True, vmem_limit_bytes=60 << 20
        ),
    )(tile_wet, neighbours.T, destination, depth, velocity, head, terrain, leakance, diffusivity)
    tile = jax.ShapeDtypeStruct((TPD, TILE, TILE), F32)
    return pl.pallas_call(
        split_kernel,
        out_shape=(tile, jax.ShapeDtypeStruct((TPD, 2, TILE, TILE), F32), tile),
        in_specs=[hbm],
        out_specs=(hbm,) * 3,
        scratch_shapes=[vm(TPD, 4, TILE), dma((TPD,)), dma((3, TPD))],
    )(made)


def solution(mesh):
    tiles = P("tiles", None, None)
    pair = P("tiles", None, None, None)
    return jax.shard_map(
        shards,
        mesh=mesh,
        in_specs=(tiles, pair, tiles, tiles, tiles, tiles, P(), P(), P()),
        out_specs=(tiles, pair, tiles),
        check_vma=False,
    )
```

```python
import functools
import math

import jax
import jax.numpy as jnp
from jax import lax
from jax.experimental import pallas as pl
from jax.experimental.pallas import tpu as pltpu
from jax.sharding import PartitionSpec as P

MESH = pl.DeviceIdType.MESH
TPD = 4
MOVE = 2
STEPS = 4
TILE = 128
BLOCKS = TILE // 8
GRAVITY = 9.81
ROOT_G = math.sqrt(GRAVITY)
SHALLOW = 0.1
COURANT = 0.45
STORAGE = 0.2
LOWEST = 2.0 * math.sqrt(GRAVITY * SHALLOW)
DEVICES = 128
F32 = jnp.float32


def peers(me):
    core = lax.rem(me, 2)
    y = lax.rem(me // 2, 4)
    z = lax.rem(me // 8, 4)
    x = me // 32
    xs = [lax.rem(x + d, 4) * 32 for d in range(4)]
    zs = [lax.rem(z + d, 4) * 8 for d in range(4)]
    ys = [lax.rem(y + d, 4) * 2 for d in range(4)]
    cs = [core, 1 - core]
    xz = [[a + b for b in zs] for a in xs]
    yc = [[a + b for b in cs] for a in ys]
    found = []
    for dx in range(4):
        for dz in range(4):
            for dy in range(4):
                for dc in range(2):
                    offset = ((dx * 4 + dz) * 4 + dy) * 2 + dc
                    if offset:
                        hops = sum(min(d, 4 - d) for d in (dx, dz, dy))
                        found.append((hops, offset, xz[dx][dz] + yc[dy][dc]))
    found.sort(key=lambda item: -item[0])
    return [(offset, target) for _, offset, target in found]


def derived(h, mx, my):
    s = jnp.maximum(h, SHALLOW)
    r = lax.rsqrt(s)
    inv = r * r
    c = (ROOT_G * s) * r
    return inv, c


def wave(h, n, inv, c):
    u = n * inv
    return u, jnp.abs(u) + c


def face(h1, n1, a1, h2, n2, a2):
    inv1, c1 = derived(h1, n1, a1)
    inv2, c2 = derived(h2, n2, a2)
    u1, w1 = wave(h1, n1, inv1, c1)
    u2, w2 = wave(h2, n2, inv2, c2)
    speed = jnp.maximum(w1, w2)
    half_g = 0.5 * GRAVITY
    mass = (n1 + n2) - speed * (h2 - h1)
    push = (n1 * u1 + half_g * h1 * h1 + n2 * u2 + half_g * h2 * h2) - speed * (n2 - n1)
    carry = (a1 * u1 + a2 * u2) - speed * (a2 - a1)
    return mass, push, carry


def flood_kernel(
    wet_ref, link_ref, dest_ref, depth_in, vel_in, head_in, terr_in, leak_in, diff_in,
    tiles_out,
    U, D, R, G, L, S, KX, KY, VEL, mbuf, mtop, ew_own, ew_got, ns_own, ns_got, ground_own, ground_got,
    movers, mover_ground, arrived_ground, slopes, DA, line_own, line_got, made,
    in_sem, mx_send, mx_recv, mt_sem, ew_send, ew_recv, ns_send, ns_recv, gr_send, gr_recv, mv_send, mv_recv,
    mg_send, mg_recv, ln_send, ln_recv, out_sem,
):
    me = lax.axis_index("tiles")
    row = me // 4
    col = lax.rem(me, 4)
    odd = lax.rem(row, 2)
    place = col + odd * (3 - 2 * col)
    base = me * TPD

    def device_at(r, c):
        o = lax.rem(r, 2)
        return r * 4 + c + o * (3 - 2 * c)

    east = device_at(row, lax.rem(place + 1, 4))
    west = device_at(row, lax.rem(place + 3, 4))
    north = device_at(lax.rem(row + 1, 32), place)
    south = device_at(lax.rem(row + 31, 32), place)
    after = lax.rem(me + 1, DEVICES)
    before = lax.rem(me + DEVICES - 1, DEVICES)
    everyone = peers(me)
    slot = [p + odd * (3 - 2 * p) for p in range(TPD)]

    loads = []
    for n, (array, place_of) in enumerate((
        (depth_in, lambda p: U.at[p, 0]), (vel_in, lambda p: VEL.at[p]),
        (head_in, lambda p: U.at[p, 3]), (terr_in, lambda p: G.at[p]),
        (leak_in, lambda p: L.at[p]), (diff_in, lambda p: S.at[p]),
    )):
        for p in range(TPD):
            loads.append(pltpu.make_async_copy(array.at[slot[p]], place_of(p), in_sem.at[n, p]))
    early, late = loads[: 4 * TPD], loads[4 * TPD :]

    barrier = pltpu.get_barrier_semaphore()

    def announce(some):
        for _, target in some:
            pl.semaphore_signal(barrier, inc=1, device_id=(target,), device_id_type=MESH)

    for load in early:
        load.start()
    announce(everyone)
    for load in late:
        load.start()

    wet = [wet_ref[base + slot[p]] for p in range(TPD)]
    linked = [[link_ref[k, base + slot[p]] for k in range(4)] for p in range(TPD)]
    lane = lax.broadcasted_iota(jnp.int32, (8, TILE), 1)
    sub = lax.broadcasted_iota(jnp.int32, (8, TILE), 0)
    first_lane = lane == 0
    last_lane = lane == TILE - 1
    half_lane = lane // 2
    wall_lane = [jnp.where(linked[p][1] >= 0, -1, TILE - 1) for p in range(TPD - 1)]
    wall_back = [jnp.where(linked[p][0] >= 0, -1, 0) for p in range(TPD)]
    zero = jnp.zeros((8, TILE), F32)

    def rows_of(i):
        return pl.ds(i * 8 if isinstance(i, int) else pl.multiple_of(i * 8, 8), 8)

    def pack(i, q, value, acc, edge):
        lane_at = q * BLOCKS + i
        shift = (lane_at + (1 if edge else 0)) % TILE
        return jnp.where(lane == lane_at, pltpu.roll(value, shift, 1), acc)

    for load in early:
        load.wait()

    def ground_block(i, carry):
        acc_e, acc_w = carry
        blk = rows_of(i)
        acc_e = pack(i, 4, G[TPD - 1, blk, :], acc_e, True)
        acc_w = pack(i, 4, G[0, blk, :], acc_w, False)
        return acc_e, acc_w

    ground_e = ground_w = zero
    for i in range(BLOCKS):
        ground_e, ground_w = ground_block(i, (ground_e, ground_w))
    ground_own[...] = jnp.zeros((2, 8, TILE), F32)
    for p in range(TPD):
        ground_own[0, p : p + 1, :] = G[p, TILE - 1 : TILE, :]
        ground_own[1, p : p + 1, :] = G[p, 0:1, :]

    def sweep(step, dt_of):
        def block(i, carry):
            acc_e, acc_w, top = carry
            blk = rows_of(i)
            top = list(top)
            for p in range(TPD):
                if dt_of is None:
                    h = U[p, 0, blk, :]
                    mx = h * VEL[p, 0, blk, :]
                    my = h * VEL[p, 1, blk, :]
                    hd = U[p, 3, blk, :]
                    U[p, 1, blk, :] = mx
                    U[p, 2, blk, :] = my
                else:
                    new = [U[p, q, blk, :] + dt_of[p] * R[p, q, blk, :] for q in range(4)]
                    for q in range(4):
                        U[p, q, blk, :] = new[q]
                    h, mx, my, hd = new
                inv, c = derived(h, mx, my)
                top[p] = jnp.maximum(top[p], (jnp.abs(mx) + jnp.abs(my)) * inv + 2.0 * c)
                if p == TPD - 1:
                    for q, value in enumerate((h, mx, my, hd)):
                        acc_e = pack(i, q, value, acc_e, True)
                if p == 0:
                    for q, value in enumerate((h, mx, my, hd)):
                        acc_w = pack(i, q, value, acc_w, False)
            return acc_e, acc_w, tuple(top)

        state = (ground_e, ground_w, (zero,) * TPD)
        for i in range(BLOCKS):
            state = block(i, state)
        acc_e, acc_w, top = state
        ew_own[step, 0] = acc_e
        ew_own[step, 1] = acc_w
        largest = jnp.full((8, TILE), LOWEST, F32)
        for p in range(TPD):
            largest = jnp.maximum(largest, jnp.where(wet[p] == 1, top[p], LOWEST))
        mbuf[step, 0:1, :] = jnp.max(largest, axis=0, keepdims=True)
        for q in range(4):
            for p in range(TPD):
                at = q * 4 + p
                ns_own[step, 0, at : at + 1, :] = U[p, q, TILE - 1 : TILE, :]
                ns_own[step, 1, at : at + 1, :] = U[p, q, 0:1, :]

    def halos(step):
        return [
            pltpu.make_async_remote_copy(
                ew_own.at[step, 0], ew_got.at[step, 1], ew_send.at[step, 0], ew_recv.at[step, 1],
                device_id=(east,), device_id_type=MESH),
            pltpu.make_async_remote_copy(
                ew_own.at[step, 1], ew_got.at[step, 0], ew_send.at[step, 1], ew_recv.at[step, 0],
                device_id=(west,), device_id_type=MESH),
            pltpu.make_async_remote_copy(
                ns_own.at[step, 0], ns_got.at[step, 1], ns_send.at[step, 0], ns_recv.at[step, 1],
                device_id=(north,), device_id_type=MESH),
            pltpu.make_async_remote_copy(
                ns_own.at[step, 1], ns_got.at[step, 0], ns_send.at[step, 1], ns_recv.at[step, 0],
                device_id=(south,), device_id_type=MESH),
        ]

    def ground_halos():
        return [
            pltpu.make_async_remote_copy(
                ground_own.at[0], ground_got.at[1], gr_send.at[0], gr_recv.at[1],
                device_id=(north,), device_id_type=MESH),
            pltpu.make_async_remote_copy(
                ground_own.at[1], ground_got.at[0], gr_send.at[1], gr_recv.at[0],
                device_id=(south,), device_id_type=MESH),
        ]

    def send(step):
        for n, (offset, target) in enumerate(everyone):
            if n == 2:
                for copy in halos(step):
                    copy.start()
            pltpu.make_async_remote_copy(
                mbuf.at[step, 0:1], mbuf.at[step, offset : offset + 1],
                mx_send.at[step], mx_recv.at[step],
                device_id=(target,), device_id_type=MESH).start()

    def all_rows(step, sem, rows=DEVICES):
        rest = mbuf.at[step, 1:rows]
        return pltpu.make_async_copy(rest, rest, sem.at[step])

    near = [item for item in everyone if item[0] < 8]
    across = [(offset // 8, target) for offset, target in everyone if offset % 8 == 0]

    def send_near(step):
        for offset, target in near:
            pltpu.make_async_remote_copy(
                mbuf.at[step, 0:1], mbuf.at[step, offset : offset + 1],
                mx_send.at[step], mx_recv.at[step],
                device_id=(target,), device_id_type=MESH).start()

    def send_across(step):
        all_rows(step, mx_recv, 8).wait()
        mtop[0:1, :] = jnp.max(mbuf[step, 0:8, :], axis=0, keepdims=True)
        for group, target in across:
            pltpu.make_async_remote_copy(
                mtop.at[0:1], mtop.at[group : group + 1], mt_sem.at[0], mt_sem.at[1],
                device_id=(target,), device_id_type=MESH).start()

    def across_rows(which):
        rest = mtop.at[1:16]
        return pltpu.make_async_copy(rest, rest, mt_sem.at[which])

    def ground_slopes():
        def block(i, below):
            blk = rows_of(i)
            nxt = rows_of(jnp.minimum(i + 1, BLOCKS - 1))
            top_row = jnp.where(i == BLOCKS - 1, 7, -1)
            here = [G[p, blk, :] for p in range(TPD)]
            turned = [pltpu.roll(g, TILE - 1, 1) for g in here]
            back = zero
            new_below = []
            for p in range(TPD):
                g = here[p]
                if p < TPD - 1:
                    de = jnp.where(last_lane, turned[p + 1], turned[p]) - g
                    de = jnp.where(lane == wall_lane[p], 0.0, de)
                else:
                    de = jnp.where(last_lane, 0.0, turned[p] - g)
                round_de = pltpu.roll(de, 1, 1)
                dw = jnp.where(first_lane, back, round_de)
                back = round_de
                KX[p, blk, :] = (0.5 * GRAVITY) * (de + dw)
                up = jnp.where(sub == 7, pltpu.roll(G[p, nxt, :], 7, 0), pltpu.roll(g, 7, 0))
                dn = jnp.where(sub == top_row, 0.0, up - g)
                round_dn = pltpu.roll(dn, 1, 0)
                ds = jnp.where(sub == 0, below[p], round_dn)
                new_below.append(round_dn)
                KY[p, blk, :] = (0.5 * GRAVITY) * (dn + ds)
            return tuple(new_below)

        lax.fori_loop(0, BLOCKS, block, (zero,) * TPD)

    def right_sides():
        def derive(i, _):
            blk = rows_of(i)
            for p in range(TPD):
                h, mx, my = (U[p, q, blk, :] for q in range(3))
                inv, c = derived(h, mx, my)
                u, au = wave(h, mx, inv, c)
                v, av = wave(h, my, inv, c)
                still = (0.5 * GRAVITY) * h * h
                D[p, 0, blk, :] = au
                D[p, 1, blk, :] = av
                D[p, 2, blk, :] = mx * u + still
                D[p, 3, blk, :] = mx * v
                D[p, 4, blk, :] = my * v + still
            return 0

        lax.fori_loop(0, BLOCKS, derive, 0, unroll=4)

        def block(i, below):
            blk = rows_of(i)
            nxt = rows_of(jnp.minimum(i + 1, BLOCKS - 1))
            top_row = jnp.where(i == BLOCKS - 1, 7, -1)
            new_below = []
            after_turned = None
            east_faces = [None] * TPD
            sides = [None] * TPD
            for p in reversed(range(TPD)):
                h, mx, my, hd = (U[p, q, blk, :] for q in range(4))
                au, fxx, fxy = D[p, 0, blk, :], D[p, 2, blk, :], D[p, 3, blk, :]
                own = (h, mx, my, hd, au, fxx, fxy)
                turned = [pltpu.roll(value, TILE - 1, 1) for value in own]
                if after_turned is None:
                    he, me_, ye, de, ae, xe, ce = turned
                else:
                    he, me_, ye, de, ae, xe, ce = (
                        jnp.where(last_lane, b, a) for a, b in zip(turned, after_turned)
                    )
                after_turned = turned
                speed = jnp.maximum(au, ae)
                g0 = (mx + me_) - speed * (he - h)
                g1 = (fxx + xe) - speed * (me_ - mx)
                g2 = (fxy + ce) - speed * (ye - my)
                g3 = de - hd
                step_out = au * mx
                if p == TPD - 1:
                    wall, push = last_lane, 0.0
                else:
                    wall, push = lane == wall_lane[p], 2.0 * (fxx + step_out)
                g0 = jnp.where(wall, 0.0, g0)
                g1 = jnp.where(wall, push, g1)
                g2 = jnp.where(wall, 0.0, g2)
                g3 = jnp.where(wall, 0.0, g3)
                east_faces[p] = (g0, g1, g2, g3)
                sides[p] = 2.0 * (fxx - step_out)
            back = (zero,) * 4
            for p in range(TPD):
                rounds = [pltpu.roll(g, 1, 1) for g in east_faces[p]]
                west_faces = [jnp.where(first_lane, b, a) for a, b in zip(rounds, back)]
                if p > 0:
                    west_faces[1] = jnp.where(lane == wall_back[p], sides[p], west_faces[1])
                back = rounds
                x0, x1, x2, x3 = (e - w for e, w in zip(east_faces[p], west_faces))

                h, mx, my, hd = (U[p, q, blk, :] for q in range(4))
                av, fxy, fyy = D[p, 1, blk, :], D[p, 3, blk, :], D[p, 4, blk, :]
                own = (h, mx, my, hd, av, fxy, fyy)
                ups = (U[p, 0, nxt, :], U[p, 1, nxt, :], U[p, 2, nxt, :], U[p, 3, nxt, :],
                       D[p, 1, nxt, :], D[p, 3, nxt, :], D[p, 4, nxt, :])
                hn, xn, mn, dn, an, cn, yn = (
                    jnp.where(sub == 7, pltpu.roll(b, 7, 0), pltpu.roll(a, 7, 0))
                    for a, b in zip(own, ups)
                )
                speed = jnp.maximum(av, an)
                f0 = (my + mn) - speed * (hn - h)
                f1 = (fyy + yn) - speed * (mn - my)
                f2 = (fxy + cn) - speed * (xn - mx)
                f3 = dn - hd
                faces = [jnp.where(sub == top_row, 0.0, f) for f in (f0, f1, f2, f3)]
                rounds = [pltpu.roll(f, 1, 0) for f in faces]
                lower = [jnp.where(sub == 0, b, a) for a, b in zip(rounds, below[4 * p : 4 * p + 4])]
                new_below.extend(rounds)
                y0, y1, y2, y3 = (n - s for n, s in zip(faces, lower))

                seep = L[p, blk, :] * (h + G[p, blk, :] - hd)
                R[p, 0, blk, :] = -0.5 * (x0 + y0) - seep
                R[p, 1, blk, :] = -0.5 * (x1 + y2) - h * KX[p, blk, :]
                R[p, 2, blk, :] = -0.5 * (x2 + y1) - h * KY[p, blk, :]
                R[p, 3, blk, :] = S[p, blk, :] * (x3 + y3) + seep * (1.0 / STORAGE)
            return tuple(new_below)

        lax.fori_loop(0, BLOCKS, block, (zero,) * (4 * TPD), unroll=2)

    def column_terms(own, got, link, flip_east):
        ghost = jnp.where(link >= 0, got, jnp.where(lane // BLOCKS == 1, -own, own))
        part = lambda packed, q: packed if q == 0 else pltpu.roll(packed, TILE - q * BLOCKS, 1)
        h, n, a, hd, g = (part(own, q) for q in range(5))
        gh, gn, ga, ghd, gg = (part(ghost, q) for q in range(5))
        if flip_east:
            mass, push, carry = face(h, n, a, gh, gn, ga)
            sign = -0.5
        else:
            mass, push, carry = face(gh, gn, ga, h, n, a)
            sign = 0.5
        slope = (0.5 * GRAVITY) * h * ((gg - g) if flip_east else (g - gg))
        return sign * mass, sign * push - slope, sign * carry, ghd - hd

    def row_terms(own, got, own_ground, got_ground, k, is_north):
        rows = lax.broadcasted_iota(jnp.int32, (TPD, TILE), 0)
        link = jnp.full((TPD, TILE), linked[0][k], jnp.int32)
        for p in range(1, TPD):
            link = jnp.where(rows == p, linked[p][k], link)
        mine = [own[q * 4 : q * 4 + 4, :] for q in range(4)] + [own_ground]
        theirs = [got[q * 4 : q * 4 + 4, :] for q in range(4)] + [got_ground]
        signs = (1.0, 1.0, -1.0, 1.0, 1.0)
        ghost = [jnp.where(link >= 0, theirs[q], signs[q] * mine[q]) for q in range(5)]
        h, a, n, hd, g = mine
        gh, ga, gn, ghd, gg = ghost
        if is_north:
            mass, push, carry = face(h, n, a, gh, gn, ga)
            sign = -0.5
        else:
            mass, push, carry = face(gh, gn, ga, h, n, a)
            sign = 0.5
        slope = (0.5 * GRAVITY) * h * ((gg - g) if is_north else (g - gg))
        return sign * mass, sign * carry, sign * push - slope, ghd - hd

    def rims(step):
        for copy in halos(step):
            copy.wait_recv()
        for side, p, edge in ((0, TPD - 1, True), (1, 0, False)):
            terms = column_terms(
                ew_own[step, side], ew_got[step, side], linked[p][1 - side], edge
            )
            at_edge = last_lane if edge else first_lane

            for i in range(BLOCKS):
                blk = rows_of(i)
                shift = (TILE - 1 - i) if edge else (TILE - i) % TILE
                for q in range(4):
                    add = pltpu.roll(terms[q], shift, 1)
                    if q == 3:
                        add = add * S[p, blk, :]
                    R[p, q, blk, :] += jnp.where(at_edge, add, 0.0)
        for side, at in ((0, TILE - 1), (1, 0)):
            terms = row_terms(
                ns_own.at[step, side], ns_got.at[step, side],
                ground_own[side, 0:TPD, :], ground_got[side, 0:TPD, :], 3 - side, side == 0,
            )
            for p in range(TPD):
                for q in range(4):
                    add = terms[q][p : p + 1, :]
                    if q == 3:
                        add = add * S[p, at : at + 1, :]
                    R[p, q, at : at + 1, :] += add

    def interval(step):
        if isinstance(step, int):
            across_rows(1).wait()
            tops = mtop[...]
        else:
            all_rows(step, mx_recv).wait()
            tops = mbuf[step]
        top = jnp.max(jnp.max(tops, axis=0, keepdims=True), axis=1, keepdims=True)
        dt = COURANT / jnp.broadcast_to(top, (8, TILE))
        return dt, [jnp.where(wet[p] == 1, dt, 0.0) for p in range(TPD)]

    sweep(0, None)
    pl.semaphore_wait(barrier, DEVICES - 1)
    for copy in ground_halos():
        copy.start()

    def ranked(flags, values):
        count = jnp.int32(0)
        picks = [jnp.int32(0)] * MOVE
        for flag, value in zip(flags, values):
            for j in range(MOVE):
                picks[j] = jnp.where(jnp.logical_and(flag, count == j), value, picks[j])
            count = count + flag.astype(jnp.int32)
        return picks

    mine = [dest_ref[base + t] for t in range(TPD)]
    leaving = [
        ranked([d >= base + TPD for d in mine], slot),
        ranked([d < base for d in mine], slot),
    ]
    wanted = [jnp.int32(0)] * TPD
    wanted_wet = [jnp.int32(0)] * TPD

    def offer(flag, goes, tile, tile_wet):
        for k in range(TPD):
            here = jnp.logical_and(flag, goes == base + k)
            wanted[k] = jnp.where(here, tile, wanted[k])
            wanted_wet[k] = jnp.where(here, tile_wet, wanted_wet[k])

    for t in range(TPD):
        offer(mine[t] >= base, mine[t], slot[t], wet_ref[base + t])
    for first_slot, side, reach in ((before * TPD, 0, me > 0), (after * TPD, 1, me < DEVICES - 1)):
        rank = jnp.int32(0)
        for t in range(TPD):
            goes = dest_ref[first_slot + t]
            comes = goes >= base if side == 0 else goes < base + TPD
            comes = jnp.logical_and(reach, comes)
            tile = TPD + side * MOVE + jnp.minimum(rank, MOVE - 1)
            offer(comes, goes, tile, wet_ref[first_slot + t])
            rank = rank + comes.astype(jnp.int32)

    def grounds(kind):
        return [
            pltpu.make_async_remote_copy(
                mover_ground.at[side, kind], arrived_ground.at[side, kind],
                mg_send.at[side, kind], mg_recv.at[side, kind],
                device_id=(target,), device_id_type=MESH)
            for side, target in ((0, after), (1, before))
        ]

    PIECES = ((0, 0, TILE), (1, 0, 104), (1, 104, 24))

    def fields_of(piece):
        j, start, count = PIECES[piece]
        rows = pl.ds(start, count)
        return [
            pltpu.make_async_remote_copy(
                movers.at[side, j, :, rows, :], U.at[TPD + side * MOVE + j, :, rows, :],
                mv_send.at[side, piece], mv_recv.at[side, piece],
                device_id=(target,), device_id_type=MESH)
            for side, target in ((0, after), (1, before))
        ]

    def lines():
        return [
            pltpu.make_async_remote_copy(
                line_own.at[pl.ds(side * MOVE, MOVE)], line_got.at[pl.ds(side * MOVE, MOVE)], ln_send.at[side], ln_recv.at[side],
                device_id=(target,), device_id_type=MESH)
            for side, target in ((0, after), (1, before))
        ]

    def outer_lines():
        for side in range(2):
            for j in range(MOVE):
                tile = leaving[side][j]
                acc = zero
                for q in range(4):
                    line_own[side * MOVE + j, q : q + 1, :] = R[tile, q, TILE - 1 : TILE, :]
                    line_own[side * MOVE + j, 4 + q : 5 + q, :] = R[tile, q, 0:1, :]
                    for i in range(BLOCKS):
                        at = q * BLOCKS + i
                        pair = pltpu.roll(R[tile, q, rows_of(i), :], 2 * at + 1, 1)
                        acc = jnp.where(half_lane == at, pair, acc)
                line_own[side * MOVE + j, 8:16, :] = acc

    def arrived_slopes():
        def block(i, below):
            blk = rows_of(i)
            nxt = rows_of(jnp.minimum(i + 1, BLOCKS - 1))
            new_below = []
            for n in range(2 * MOVE):
                side, j = divmod(n, MOVE)
                g = arrived_ground[side, 0, j, blk, :]
                up = pltpu.roll(arrived_ground[side, 0, j, nxt, :], 7, 0)
                rise = jnp.where(sub == 7, up, pltpu.roll(g, 7, 0)) - g
                back = pltpu.roll(rise, 1, 0)
                new_below.append(back)
                across_x = pltpu.roll(g, TILE - 1, 1) - pltpu.roll(g, 1, 1)
                slopes[side, j, 0, blk, :] = (0.5 * GRAVITY) * across_x
                slopes[side, j, 1, blk, :] = (0.5 * GRAVITY) * (
                    rise + jnp.where(sub == 0, below[n], back)
                )
            return tuple(new_below)

        lax.fori_loop(0, BLOCKS, block, (zero,) * (2 * MOVE), unroll=2)

    def arrived_sides(j):
        def derive(i, _):
            blk = rows_of(i)
            for side in range(2):
                h, mx, my = (U[TPD + side * MOVE + j, q, blk, :] for q in range(3))
                inv, c = derived(h, mx, my)
                u, au = wave(h, mx, inv, c)
                v, av = wave(h, my, inv, c)
                still = (0.5 * GRAVITY) * h * h
                DA[side, 0, blk, :] = au
                DA[side, 1, blk, :] = av
                DA[side, 2, blk, :] = mx * u + still
                DA[side, 3, blk, :] = mx * v
                DA[side, 4, blk, :] = my * v + still
            return 0


        def block(i, below):
            blk = rows_of(i)
            nxt = rows_of(jnp.minimum(i + 1, BLOCKS - 1))
            new_below = []
            for side in range(2):
                old = below[4 * side : 4 * side + 4]
                h, mx, my, hd = (U[TPD + side * MOVE + j, q, blk, :] for q in range(4))
                g = arrived_ground[side, 0, j, blk, :]
                au, av, fxx, fxy, fyy = (DA[side, n, blk, :] for n in range(5))
                he, me_, ye, de, ae, xe, ce = (
                    pltpu.roll(value, TILE - 1, 1) for value in (h, mx, my, hd, au, fxx, fxy)
                )
                speed = jnp.maximum(au, ae)
                east_faces = (
                    (mx + me_) - speed * (he - h),
                    (fxx + xe) - speed * (me_ - mx),
                    (fxy + ce) - speed * (ye - my),
                    de - hd,
                )
                x0, x1, x2, x3 = (f - pltpu.roll(f, 1, 1) for f in east_faces)
                kx, ky = (slopes[side, j, n, blk, :] for n in range(2))
                ups = [U[TPD + side * MOVE + j, q, nxt, :] for q in range(4)]
                ups += [DA[side, n, nxt, :] for n in (1, 3, 4)]
                hn, xn, mn, dn, an, cn, yn = (
                    jnp.where(sub == 7, pltpu.roll(b, 7, 0), pltpu.roll(a, 7, 0))
                    for a, b in zip((h, mx, my, hd, av, fxy, fyy), ups)
                )
                speed = jnp.maximum(av, an)
                faces = (
                    (my + mn) - speed * (hn - h),
                    (fyy + yn) - speed * (mn - my),
                    (fxy + cn) - speed * (xn - mx),
                    dn - hd,
                )
                rounds = [pltpu.roll(f, 1, 0) for f in faces]
                lower = [jnp.where(sub == 0, b, a) for a, b in zip(rounds, old)]
                new_below.extend(rounds)
                y0, y1, y2, y3 = (n - s for n, s in zip(faces, lower))
                seep = arrived_ground[side, 1, j, blk, :] * (h + g - hd)
                R[TPD + side * MOVE + j, 0, blk, :] = -0.5 * (x0 + y0) - seep
                R[TPD + side * MOVE + j, 1, blk, :] = -0.5 * (x1 + y2) - h * kx
                R[TPD + side * MOVE + j, 2, blk, :] = -0.5 * (x2 + y1) - h * ky
                R[TPD + side * MOVE + j, 3, blk, :] = (
                    arrived_ground[side, 2, j, blk, :] * (x3 + y3) + seep * (1.0 / STORAGE)
                )
            return tuple(new_below)

        below = (zero,) * 8
        for piece, (tile, start, count) in enumerate(PIECES):
            if tile != j:
                continue
            for copy in fields_of(piece):
                copy.wait_recv()
            lo, hi = start // 8, (start + count) // 8
            whole = hi - (hi - lo) % 4
            lax.fori_loop(lo, whole, derive, 0, unroll=4)
            for i in range(whole, hi):
                derive(i, 0)
            first = lo - 1 if lo else 0
            last = hi - 1 if hi < BLOCKS else BLOCKS
            below = lax.fori_loop(first, last, block, below, unroll=4)

    def body(step, _):
        send(step)

        @pl.when(step == 0)
        def _():
            for load in late:
                load.wait()
            for side in range(2):
                for j in range(MOVE):
                    for kind, array in enumerate((G, L, S)):
                        mover_ground[side, kind, j] = array[leaving[side][j]]

        for copy in grounds(step):
            copy.start()

        @pl.when(step == 0)
        def _():
            ground_slopes()

        right_sides()

        @pl.when(step == 0)
        def _():
            for copy in ground_halos():
                copy.wait_recv()

        rims(step)
        sweep(step + 1, interval(step)[1])
        return 0

    lax.fori_loop(0, STEPS - 1, body, 0)

    final = STEPS - 1
    send_near(final)
    for copy in halos(final):
        copy.start()

    def collect(j):
        for q in range(4):
            for i in range(BLOCKS):
                blk = rows_of(i)
                own = [U[p, q, blk, :] for p in range(TPD)]
                for side in range(2):
                    value = own[0]
                    for p in range(1, TPD):
                        value = jnp.where(leaving[side][j] == p, own[p], value)
                    movers[side, j, q, blk, :] = value

    def send_fields(j):
        for piece in range(len(PIECES)):
            if PIECES[piece][0] == j:
                for copy in fields_of(piece):
                    copy.start()

    collect(0)
    send_fields(0)
    collect(1)
    right_sides()
    send_across(final)
    send_fields(1)
    for kind in range(3):
        for copy in grounds(kind):
            copy.wait_recv()
    arrived_slopes()
    rims(final)
    outer_lines()
    for copy in lines():
        copy.start()
    for j in range(MOVE):
        arrived_sides(j)
    for copy in lines():
        copy.wait_recv()
    dt = interval(final)[0]
    keeps = []
    for k in range(TPD):
        tile = wanted[k]
        dt_k = jnp.where(wanted_wet[k] == 1, dt, 0.0)
        guest = tile >= TPD
        line = jnp.maximum(tile - TPD, 0)
        turned_lane = lax.rem(lane + 1, TILE)
        edge_lane = turned_lane < jnp.where(guest, 2, 0)
        south_row = sub == jnp.where(guest, 0, -1)
        north_row = sub == jnp.where(guest, 7, -1)
        cols = line_got[line, 8:16, :]
        rows = line_got[line, 0:8, :]
        for q in range(4):
            for i in range(BLOCKS):
                blk = rows_of(i)
                rate = R[tile, q, blk, :]
                at = q * BLOCKS + i
                rate = jnp.where(edge_lane, pltpu.roll(cols, TILE - 1 - 2 * at, 1), rate)
                if i == 0:
                    rate = jnp.where(south_row, rows[4 + q : 5 + q, :], rate)
                if i == BLOCKS - 1:
                    rate = jnp.where(north_row, rows[q : q + 1, :], rate)
                made[k, q, blk, :] = U[tile, q, blk, :] + dt_k * rate
        keep = pltpu.make_async_copy(made.at[k], tiles_out.at[k], out_sem.at[k])
        keep.start()
        keeps.append(keep)
    for step in range(STEPS):
        all_rows(step, mx_send, DEVICES if step < final else 8).wait()
        for copy in halos(step):
            copy.wait_send()
    across_rows(0).wait()
    for copy in ground_halos():
        copy.wait_send()
    for kind in range(3):
        for copy in grounds(kind):
            copy.wait_send()
    for piece in range(len(PIECES)):
        for copy in fields_of(piece):
            copy.wait_send()
    for copy in lines():
        copy.wait_send()
    for keep in keeps:
        keep.wait()


def split_kernel(tiles, depth_out, flow_out, head_out, held, in_sem, sem):
    fetches = [
        pltpu.make_async_copy(tiles.at[k], held.at[k], in_sem.at[k]) for k in range(TPD)
    ]
    for fetch in fetches:
        fetch.start()
    copies = []
    for k in range(TPD):
        fetches[k].wait()
        for n, (part, out) in enumerate(
            ((held.at[k, 0], depth_out), (held.at[k, 1:3], flow_out), (held.at[k, 3], head_out))
        ):
            copy = pltpu.make_async_copy(part, out.at[k], sem.at[n, k])
            copy.start()
            copies.append(copy)
    for copy in copies:
        copy.wait()


def shards(depth, velocity, head, terrain, leakance, diffusivity, tile_wet, neighbours, destination):
    hbm = pl.BlockSpec(memory_space=pltpu.HBM)
    smem = pl.BlockSpec(memory_space=pltpu.SMEM)
    vm = lambda *shape: pltpu.VMEM(shape + (TILE,), F32)
    dma = pltpu.SemaphoreType.DMA
    made = pl.pallas_call(
        flood_kernel,
        out_shape=jax.ShapeDtypeStruct((TPD, 4, TILE, TILE), F32),
        in_specs=[smem] * 3 + [hbm] * 6,
        out_specs=hbm,
        scratch_shapes=[
            vm(TPD + 2 * MOVE, 4, TILE), vm(TPD, 5, TILE), vm(TPD + 2 * MOVE, 4, TILE),
            vm(TPD, TILE), vm(TPD, TILE), vm(TPD, TILE), vm(TPD, TILE), vm(TPD, TILE),
            vm(TPD, 2, TILE), vm(STEPS, DEVICES), vm(16),
            vm(STEPS, 2, 8), vm(STEPS, 2, 8), vm(STEPS, 2, 16), vm(STEPS, 2, 16), vm(2, 8), vm(2, 8),
            vm(2, MOVE, 4, TILE), vm(2, 3, MOVE, TILE), vm(2, 3, MOVE, TILE), vm(2, MOVE, 2, TILE),
            vm(2, 5, TILE), vm(2 * MOVE, 16), vm(2 * MOVE, 16), vm(TPD, 4, TILE),
            dma((6, TPD)), dma((STEPS,)), dma((STEPS,)), dma((2,)),
            dma((STEPS, 2)), dma((STEPS, 2)), dma((STEPS, 2)), dma((STEPS, 2)), dma((2,)), dma((2,)),
            dma((2, 3)), dma((2, 3)), dma((2, 3)), dma((2, 3)), dma((2,)), dma((2,)),
            dma((TPD,)),
        ],
        compiler_params=pltpu.CompilerParams(
            collective_id=0, has_side_effects=True, vmem_limit_bytes=60 << 20
        ),
    )(tile_wet, neighbours.T, destination, depth, velocity, head, terrain, leakance, diffusivity)
    tile = jax.ShapeDtypeStruct((TPD, TILE, TILE), F32)
    return pl.pallas_call(
        split_kernel,
        out_shape=(tile, jax.ShapeDtypeStruct((TPD, 2, TILE, TILE), F32), tile),
        in_specs=[hbm],
        out_specs=(hbm,) * 3,
        scratch_shapes=[vm(TPD, 4, TILE), dma((TPD,)), dma((3, TPD))],
    )(made)


def solution(mesh):
    tiles = P("tiles", None, None)
    pair = P("tiles", None, None, None)
    return jax.shard_map(
        shards,
        mesh=mesh,
        in_specs=(tiles, pair, tiles, tiles, tiles, tiles, P(), P(), P()),
        out_specs=(tiles, pair, tiles),
        check_vma=False,
    )
```

```python
import functools
import math

import jax
import jax.numpy as jnp
from jax import lax
from jax.experimental import pallas as pl
from jax.experimental.pallas import tpu as pltpu
from jax.sharding import PartitionSpec as P

MESH = pl.DeviceIdType.MESH
TPD = 4
MOVE = 2
STEPS = 4
TILE = 128
BLOCKS = TILE // 8
GRAVITY = 9.81
ROOT_G = math.sqrt(GRAVITY)
SHALLOW = 0.1
COURANT = 0.45
STORAGE = 0.2
LOWEST = 2.0 * math.sqrt(GRAVITY * SHALLOW)
DEVICES = 128
F32 = jnp.float32


def peers(me):
    core = lax.rem(me, 2)
    y = lax.rem(me // 2, 4)
    z = lax.rem(me // 8, 4)
    x = me // 32
    xs = [lax.rem(x + d, 4) * 32 for d in range(4)]
    zs = [lax.rem(z + d, 4) * 8 for d in range(4)]
    ys = [lax.rem(y + d, 4) * 2 for d in range(4)]
    cs = [core, 1 - core]
    xz = [[a + b for b in zs] for a in xs]
    yc = [[a + b for b in cs] for a in ys]
    found = []
    for dx in range(4):
        for dz in range(4):
            for dy in range(4):
                for dc in range(2):
                    offset = ((dx * 4 + dz) * 4 + dy) * 2 + dc
                    if offset:
                        hops = sum(min(d, 4 - d) for d in (dx, dz, dy))
                        found.append((hops, offset, xz[dx][dz] + yc[dy][dc]))
    found.sort(key=lambda item: -item[0])
    return [(offset, target) for _, offset, target in found]


def derived(h, mx, my):
    s = jnp.maximum(h, SHALLOW)
    r = lax.rsqrt(s)
    inv = r * r
    c = (ROOT_G * s) * r
    return inv, c


def wave(h, n, inv, c):
    u = n * inv
    return u, jnp.abs(u) + c


def face(h1, n1, a1, h2, n2, a2):
    inv1, c1 = derived(h1, n1, a1)
    inv2, c2 = derived(h2, n2, a2)
    u1, w1 = wave(h1, n1, inv1, c1)
    u2, w2 = wave(h2, n2, inv2, c2)
    speed = jnp.maximum(w1, w2)
    half_g = 0.5 * GRAVITY
    mass = (n1 + n2) - speed * (h2 - h1)
    push = (n1 * u1 + half_g * h1 * h1 + n2 * u2 + half_g * h2 * h2) - speed * (n2 - n1)
    carry = (a1 * u1 + a2 * u2) - speed * (a2 - a1)
    return mass, push, carry


def flood_kernel(
    wet_ref, link_ref, dest_ref, depth_in, vel_in, head_in, terr_in, leak_in, diff_in,
    tiles_out,
    U, D, R, G, L, S, KX, KY, VEL, mbuf, mtop, ew_own, ew_got, ns_own, ns_got, ground_own, ground_got,
    movers, mover_ground, arrived_ground, slopes, DA, line_own, line_got, made,
    in_sem, mx_send, mx_recv, mt_sem, ew_send, ew_recv, ns_send, ns_recv, gr_send, gr_recv, mv_send, mv_recv,
    mg_send, mg_recv, ln_send, ln_recv, out_sem,
):
    me = lax.axis_index("tiles")
    row = me // 4
    col = lax.rem(me, 4)
    odd = lax.rem(row, 2)
    place = col + odd * (3 - 2 * col)
    base = me * TPD

    def device_at(r, c):
        o = lax.rem(r, 2)
        return r * 4 + c + o * (3 - 2 * c)

    east = device_at(row, lax.rem(place + 1, 4))
    west = device_at(row, lax.rem(place + 3, 4))
    north = device_at(lax.rem(row + 1, 32), place)
    south = device_at(lax.rem(row + 31, 32), place)
    after = lax.rem(me + 1, DEVICES)
    before = lax.rem(me + DEVICES - 1, DEVICES)
    everyone = peers(me)
    slot = [p + odd * (3 - 2 * p) for p in range(TPD)]

    loads = []
    for n, (array, place_of) in enumerate((
        (depth_in, lambda p: U.at[p, 0]), (vel_in, lambda p: VEL.at[p]),
        (head_in, lambda p: U.at[p, 3]), (terr_in, lambda p: G.at[p]),
        (leak_in, lambda p: L.at[p]), (diff_in, lambda p: S.at[p]),
    )):
        for p in range(TPD):
            loads.append(pltpu.make_async_copy(array.at[slot[p]], place_of(p), in_sem.at[n, p]))
    early, late = loads[: 4 * TPD], loads[4 * TPD :]

    barrier = pltpu.get_barrier_semaphore()

    def announce(some):
        for _, target in some:
            pl.semaphore_signal(barrier, inc=1, device_id=(target,), device_id_type=MESH)

    for load in early:
        load.start()
    announce(everyone)
    for load in late:
        load.start()

    wet = [wet_ref[base + slot[p]] for p in range(TPD)]
    linked = [[link_ref[k, base + slot[p]] for k in range(4)] for p in range(TPD)]
    lane = lax.broadcasted_iota(jnp.int32, (8, TILE), 1)
    sub = lax.broadcasted_iota(jnp.int32, (8, TILE), 0)
    first_lane = lane == 0
    last_lane = lane == TILE - 1
    half_lane = lane // 2
    wall_lane = [jnp.where(linked[p][1] >= 0, -1, TILE - 1) for p in range(TPD - 1)]
    wall_back = [jnp.where(linked[p][0] >= 0, -1, 0) for p in range(TPD)]
    zero = jnp.zeros((8, TILE), F32)

    def rows_of(i):
        return pl.ds(i * 8 if isinstance(i, int) else pl.multiple_of(i * 8, 8), 8)

    def pack(i, q, value, acc, edge):
        lane_at = q * BLOCKS + i
        shift = (lane_at + (1 if edge else 0)) % TILE
        return jnp.where(lane == lane_at, pltpu.roll(value, shift, 1), acc)

    for load in early:
        load.wait()

    def ground_block(i, carry):
        acc_e, acc_w = carry
        blk = rows_of(i)
        acc_e = pack(i, 4, G[TPD - 1, blk, :], acc_e, True)
        acc_w = pack(i, 4, G[0, blk, :], acc_w, False)
        return acc_e, acc_w

    ground_e = ground_w = zero
    for i in range(BLOCKS):
        ground_e, ground_w = ground_block(i, (ground_e, ground_w))
    ground_own[...] = jnp.zeros((2, 8, TILE), F32)
    for p in range(TPD):
        ground_own[0, p : p + 1, :] = G[p, TILE - 1 : TILE, :]
        ground_own[1, p : p + 1, :] = G[p, 0:1, :]

    def sweep(step, dt_of):
        def block(i, carry):
            acc_e, acc_w, top = carry
            blk = rows_of(i)
            top = list(top)
            for p in range(TPD):
                if dt_of is None:
                    h = U[p, 0, blk, :]
                    mx = h * VEL[p, 0, blk, :]
                    my = h * VEL[p, 1, blk, :]
                    hd = U[p, 3, blk, :]
                    U[p, 1, blk, :] = mx
                    U[p, 2, blk, :] = my
                else:
                    new = [U[p, q, blk, :] + dt_of[p] * R[p, q, blk, :] for q in range(4)]
                    for q in range(4):
                        U[p, q, blk, :] = new[q]
                    h, mx, my, hd = new
                inv, c = derived(h, mx, my)
                top[p] = jnp.maximum(top[p], (jnp.abs(mx) + jnp.abs(my)) * inv + 2.0 * c)
                if p == TPD - 1:
                    for q, value in enumerate((h, mx, my, hd)):
                        acc_e = pack(i, q, value, acc_e, True)
                if p == 0:
                    for q, value in enumerate((h, mx, my, hd)):
                        acc_w = pack(i, q, value, acc_w, False)
            return acc_e, acc_w, tuple(top)

        state = (ground_e, ground_w, (zero,) * TPD)
        for i in range(BLOCKS):
            state = block(i, state)
        acc_e, acc_w, top = state
        ew_own[step, 0] = acc_e
        ew_own[step, 1] = acc_w
        largest = jnp.full((8, TILE), LOWEST, F32)
        for p in range(TPD):
            largest = jnp.maximum(largest, jnp.where(wet[p] == 1, top[p], LOWEST))
        mbuf[step, 0:1, :] = jnp.max(largest, axis=0, keepdims=True)
        for q in range(4):
            for p in range(TPD):
                at = q * 4 + p
                ns_own[step, 0, at : at + 1, :] = U[p, q, TILE - 1 : TILE, :]
                ns_own[step, 1, at : at + 1, :] = U[p, q, 0:1, :]

    def halos(step):
        return [
            pltpu.make_async_remote_copy(
                ew_own.at[step, 0], ew_got.at[step, 1], ew_send.at[step, 0], ew_recv.at[step, 1],
                device_id=(east,), device_id_type=MESH),
            pltpu.make_async_remote_copy(
                ew_own.at[step, 1], ew_got.at[step, 0], ew_send.at[step, 1], ew_recv.at[step, 0],
                device_id=(west,), device_id_type=MESH),
            pltpu.make_async_remote_copy(
                ns_own.at[step, 0], ns_got.at[step, 1], ns_send.at[step, 0], ns_recv.at[step, 1],
                device_id=(north,), device_id_type=MESH),
            pltpu.make_async_remote_copy(
                ns_own.at[step, 1], ns_got.at[step, 0], ns_send.at[step, 1], ns_recv.at[step, 0],
                device_id=(south,), device_id_type=MESH),
        ]

    def ground_halos():
        return [
            pltpu.make_async_remote_copy(
                ground_own.at[0], ground_got.at[1], gr_send.at[0], gr_recv.at[1],
                device_id=(north,), device_id_type=MESH),
            pltpu.make_async_remote_copy(
                ground_own.at[1], ground_got.at[0], gr_send.at[1], gr_recv.at[0],
                device_id=(south,), device_id_type=MESH),
        ]

    def send(step):
        for n, (offset, target) in enumerate(everyone):
            if n == 2:
                for copy in halos(step):
                    copy.start()
            pltpu.make_async_remote_copy(
                mbuf.at[step, 0:1], mbuf.at[step, offset : offset + 1],
                mx_send.at[step], mx_recv.at[step],
                device_id=(target,), device_id_type=MESH).start()

    def all_rows(step, sem, rows=DEVICES):
        rest = mbuf.at[step, 1:rows]
        return pltpu.make_async_copy(rest, rest, sem.at[step])

    near = [item for item in everyone if item[0] < 8]
    across = [(offset // 8, target) for offset, target in everyone if offset % 8 == 0]

    def send_near(step):
        for offset, target in near:
            pltpu.make_async_remote_copy(
                mbuf.at[step, 0:1], mbuf.at[step, offset : offset + 1],
                mx_send.at[step], mx_recv.at[step],
                device_id=(target,), device_id_type=MESH).start()

    def send_across(step):
        all_rows(step, mx_recv, 8).wait()
        mtop[0:1, :] = jnp.max(mbuf[step, 0:8, :], axis=0, keepdims=True)
        for group, target in across:
            pltpu.make_async_remote_copy(
                mtop.at[0:1], mtop.at[group : group + 1], mt_sem.at[0], mt_sem.at[1],
                device_id=(target,), device_id_type=MESH).start()

    def across_rows(which):
        rest = mtop.at[1:16]
        return pltpu.make_async_copy(rest, rest, mt_sem.at[which])

    def ground_slopes():
        def block(i, below):
            blk = rows_of(i)
            nxt = rows_of(jnp.minimum(i + 1, BLOCKS - 1))
            top_row = jnp.where(i == BLOCKS - 1, 7, -1)
            here = [G[p, blk, :] for p in range(TPD)]
            turned = [pltpu.roll(g, TILE - 1, 1) for g in here]
            back = zero
            new_below = []
            for p in range(TPD):
                g = here[p]
                if p < TPD - 1:
                    de = jnp.where(last_lane, turned[p + 1], turned[p]) - g
                    de = jnp.where(lane == wall_lane[p], 0.0, de)
                else:
                    de = jnp.where(last_lane, 0.0, turned[p] - g)
                round_de = pltpu.roll(de, 1, 1)
                dw = jnp.where(first_lane, back, round_de)
                back = round_de
                KX[p, blk, :] = (0.5 * GRAVITY) * (de + dw)
                up = jnp.where(sub == 7, pltpu.roll(G[p, nxt, :], 7, 0), pltpu.roll(g, 7, 0))
                dn = jnp.where(sub == top_row, 0.0, up - g)
                round_dn = pltpu.roll(dn, 1, 0)
                ds = jnp.where(sub == 0, below[p], round_dn)
                new_below.append(round_dn)
                KY[p, blk, :] = (0.5 * GRAVITY) * (dn + ds)
            return tuple(new_below)

        lax.fori_loop(0, BLOCKS, block, (zero,) * TPD)

    def right_sides():
        def derive(i, _):
            blk = rows_of(i)
            for p in range(TPD):
                h, mx, my = (U[p, q, blk, :] for q in range(3))
                inv, c = derived(h, mx, my)
                u, au = wave(h, mx, inv, c)
                v, av = wave(h, my, inv, c)
                still = (0.5 * GRAVITY) * h * h
                D[p, 0, blk, :] = au
                D[p, 1, blk, :] = av
                D[p, 2, blk, :] = mx * u + still
                D[p, 3, blk, :] = mx * v
                D[p, 4, blk, :] = my * v + still
            return 0

        lax.fori_loop(0, BLOCKS, derive, 0, unroll=4)

        def block(i, below):
            blk = rows_of(i)
            nxt = rows_of(jnp.minimum(i + 1, BLOCKS - 1))
            top_row = jnp.where(i == BLOCKS - 1, 7, -1)
            new_below = []
            after_turned = None
            east_faces = [None] * TPD
            sides = [None] * TPD
            for p in reversed(range(TPD)):
                h, mx, my, hd = (U[p, q, blk, :] for q in range(4))
                au, fxx, fxy = D[p, 0, blk, :], D[p, 2, blk, :], D[p, 3, blk, :]
                own = (h, mx, my, hd, au, fxx, fxy)
                turned = [pltpu.roll(value, TILE - 1, 1) for value in own]
                if after_turned is None:
                    he, me_, ye, de, ae, xe, ce = turned
                else:
                    he, me_, ye, de, ae, xe, ce = (
                        jnp.where(last_lane, b, a) for a, b in zip(turned, after_turned)
                    )
                after_turned = turned
                speed = jnp.maximum(au, ae)
                g0 = (mx + me_) - speed * (he - h)
                g1 = (fxx + xe) - speed * (me_ - mx)
                g2 = (fxy + ce) - speed * (ye - my)
                g3 = de - hd
                step_out = au * mx
                if p == TPD - 1:
                    wall, push = last_lane, 0.0
                else:
                    wall, push = lane == wall_lane[p], 2.0 * (fxx + step_out)
                g0 = jnp.where(wall, 0.0, g0)
                g1 = jnp.where(wall, push, g1)
                g2 = jnp.where(wall, 0.0, g2)
                g3 = jnp.where(wall, 0.0, g3)
                east_faces[p] = (g0, g1, g2, g3)
                sides[p] = 2.0 * (fxx - step_out)
            back = (zero,) * 4
            for p in range(TPD):
                rounds = [pltpu.roll(g, 1, 1) for g in east_faces[p]]
                west_faces = [jnp.where(first_lane, b, a) for a, b in zip(rounds, back)]
                if p > 0:
                    west_faces[1] = jnp.where(lane == wall_back[p], sides[p], west_faces[1])
                back = rounds
                x0, x1, x2, x3 = (e - w for e, w in zip(east_faces[p], west_faces))

                h, mx, my, hd = (U[p, q, blk, :] for q in range(4))
                av, fxy, fyy = D[p, 1, blk, :], D[p, 3, blk, :], D[p, 4, blk, :]
                own = (h, mx, my, hd, av, fxy, fyy)
                ups = (U[p, 0, nxt, :], U[p, 1, nxt, :], U[p, 2, nxt, :], U[p, 3, nxt, :],
                       D[p, 1, nxt, :], D[p, 3, nxt, :], D[p, 4, nxt, :])
                hn, xn, mn, dn, an, cn, yn = (
                    jnp.where(sub == 7, pltpu.roll(b, 7, 0), pltpu.roll(a, 7, 0))
                    for a, b in zip(own, ups)
                )
                speed = jnp.maximum(av, an)
                f0 = (my + mn) - speed * (hn - h)
                f1 = (fyy + yn) - speed * (mn - my)
                f2 = (fxy + cn) - speed * (xn - mx)
                f3 = dn - hd
                faces = [jnp.where(sub == top_row, 0.0, f) for f in (f0, f1, f2, f3)]
                rounds = [pltpu.roll(f, 1, 0) for f in faces]
                lower = [jnp.where(sub == 0, b, a) for a, b in zip(rounds, below[4 * p : 4 * p + 4])]
                new_below.extend(rounds)
                y0, y1, y2, y3 = (n - s for n, s in zip(faces, lower))

                seep = L[p, blk, :] * (h + G[p, blk, :] - hd)
                R[p, 0, blk, :] = -0.5 * (x0 + y0) - seep
                R[p, 1, blk, :] = -0.5 * (x1 + y2) - h * KX[p, blk, :]
                R[p, 2, blk, :] = -0.5 * (x2 + y1) - h * KY[p, blk, :]
                R[p, 3, blk, :] = S[p, blk, :] * (x3 + y3) + seep * (1.0 / STORAGE)
            return tuple(new_below)

        lax.fori_loop(0, BLOCKS, block, (zero,) * (4 * TPD), unroll=4)

    def column_terms(own, got, link, flip_east):
        ghost = jnp.where(link >= 0, got, jnp.where(lane // BLOCKS == 1, -own, own))
        part = lambda packed, q: packed if q == 0 else pltpu.roll(packed, TILE - q * BLOCKS, 1)
        h, n, a, hd, g = (part(own, q) for q in range(5))
        gh, gn, ga, ghd, gg = (part(ghost, q) for q in range(5))
        if flip_east:
            mass, push, carry = face(h, n, a, gh, gn, ga)
            sign = -0.5
        else:
            mass, push, carry = face(gh, gn, ga, h, n, a)
            sign = 0.5
        slope = (0.5 * GRAVITY) * h * ((gg - g) if flip_east else (g - gg))
        return sign * mass, sign * push - slope, sign * carry, ghd - hd

    def row_terms(own, got, own_ground, got_ground, k, is_north):
        rows = lax.broadcasted_iota(jnp.int32, (TPD, TILE), 0)
        link = jnp.full((TPD, TILE), linked[0][k], jnp.int32)
        for p in range(1, TPD):
            link = jnp.where(rows == p, linked[p][k], link)
        mine = [own[q * 4 : q * 4 + 4, :] for q in range(4)] + [own_ground]
        theirs = [got[q * 4 : q * 4 + 4, :] for q in range(4)] + [got_ground]
        signs = (1.0, 1.0, -1.0, 1.0, 1.0)
        ghost = [jnp.where(link >= 0, theirs[q], signs[q] * mine[q]) for q in range(5)]
        h, a, n, hd, g = mine
        gh, ga, gn, ghd, gg = ghost
        if is_north:
            mass, push, carry = face(h, n, a, gh, gn, ga)
            sign = -0.5
        else:
            mass, push, carry = face(gh, gn, ga, h, n, a)
            sign = 0.5
        slope = (0.5 * GRAVITY) * h * ((gg - g) if is_north else (g - gg))
        return sign * mass, sign * carry, sign * push - slope, ghd - hd

    def rims(step):
        for copy in halos(step):
            copy.wait_recv()
        for side, p, edge in ((0, TPD - 1, True), (1, 0, False)):
            terms = column_terms(
                ew_own[step, side], ew_got[step, side], linked[p][1 - side], edge
            )
            at_edge = last_lane if edge else first_lane

            for i in range(BLOCKS):
                blk = rows_of(i)
                shift = (TILE - 1 - i) if edge else (TILE - i) % TILE
                for q in range(4):
                    add = pltpu.roll(terms[q], shift, 1)
                    if q == 3:
                        add = add * S[p, blk, :]
                    R[p, q, blk, :] += jnp.where(at_edge, add, 0.0)
        for side, at in ((0, TILE - 1), (1, 0)):
            terms = row_terms(
                ns_own.at[step, side], ns_got.at[step, side],
                ground_own[side, 0:TPD, :], ground_got[side, 0:TPD, :], 3 - side, side == 0,
            )
            for p in range(TPD):
                for q in range(4):
                    add = terms[q][p : p + 1, :]
                    if q == 3:
                        add = add * S[p, at : at + 1, :]
                    R[p, q, at : at + 1, :] += add

    def interval(step):
        if isinstance(step, int):
            across_rows(1).wait()
            tops = mtop[...]
        else:
            all_rows(step, mx_recv).wait()
            tops = mbuf[step]
        top = jnp.max(jnp.max(tops, axis=0, keepdims=True), axis=1, keepdims=True)
        dt = COURANT / jnp.broadcast_to(top, (8, TILE))
        return dt, [jnp.where(wet[p] == 1, dt, 0.0) for p in range(TPD)]

    sweep(0, None)
    pl.semaphore_wait(barrier, DEVICES - 1)
    for copy in ground_halos():
        copy.start()

    def ranked(flags, values):
        count = jnp.int32(0)
        picks = [jnp.int32(0)] * MOVE
        for flag, value in zip(flags, values):
            for j in range(MOVE):
                picks[j] = jnp.where(jnp.logical_and(flag, count == j), value, picks[j])
            count = count + flag.astype(jnp.int32)
        return picks

    mine = [dest_ref[base + t] for t in range(TPD)]
    leaving = [
        ranked([d >= base + TPD for d in mine], slot),
        ranked([d < base for d in mine], slot),
    ]
    wanted = [jnp.int32(0)] * TPD
    wanted_wet = [jnp.int32(0)] * TPD

    def offer(flag, goes, tile, tile_wet):
        for k in range(TPD):
            here = jnp.logical_and(flag, goes == base + k)
            wanted[k] = jnp.where(here, tile, wanted[k])
            wanted_wet[k] = jnp.where(here, tile_wet, wanted_wet[k])

    for t in range(TPD):
        offer(mine[t] >= base, mine[t], slot[t], wet_ref[base + t])
    for first_slot, side, reach in ((before * TPD, 0, me > 0), (after * TPD, 1, me < DEVICES - 1)):
        rank = jnp.int32(0)
        for t in range(TPD):
            goes = dest_ref[first_slot + t]
            comes = goes >= base if side == 0 else goes < base + TPD
            comes = jnp.logical_and(reach, comes)
            tile = TPD + side * MOVE + jnp.minimum(rank, MOVE - 1)
            offer(comes, goes, tile, wet_ref[first_slot + t])
            rank = rank + comes.astype(jnp.int32)

    def grounds(kind):
        return [
            pltpu.make_async_remote_copy(
                mover_ground.at[side, kind], arrived_ground.at[side, kind],
                mg_send.at[side, kind], mg_recv.at[side, kind],
                device_id=(target,), device_id_type=MESH)
            for side, target in ((0, after), (1, before))
        ]

    PIECES = ((0, 0, TILE), (1, 0, 104), (1, 104, 24))

    def fields_of(piece):
        j, start, count = PIECES[piece]
        rows = pl.ds(start, count)
        return [
            pltpu.make_async_remote_copy(
                movers.at[side, j, :, rows, :], U.at[TPD + side * MOVE + j, :, rows, :],
                mv_send.at[side, piece], mv_recv.at[side, piece],
                device_id=(target,), device_id_type=MESH)
            for side, target in ((0, after), (1, before))
        ]

    def lines():
        return [
            pltpu.make_async_remote_copy(
                line_own.at[pl.ds(side * MOVE, MOVE)], line_got.at[pl.ds(side * MOVE, MOVE)], ln_send.at[side], ln_recv.at[side],
                device_id=(target,), device_id_type=MESH)
            for side, target in ((0, after), (1, before))
        ]

    def outer_lines():
        for side in range(2):
            for j in range(MOVE):
                tile = leaving[side][j]
                acc = zero
                for q in range(4):
                    line_own[side * MOVE + j, q : q + 1, :] = R[tile, q, TILE - 1 : TILE, :]
                    line_own[side * MOVE + j, 4 + q : 5 + q, :] = R[tile, q, 0:1, :]
                    for i in range(BLOCKS):
                        at = q * BLOCKS + i
                        pair = pltpu.roll(R[tile, q, rows_of(i), :], 2 * at + 1, 1)
                        acc = jnp.where(half_lane == at, pair, acc)
                line_own[side * MOVE + j, 8:16, :] = acc

    def arrived_slopes():
        def block(i, below):
            blk = rows_of(i)
            nxt = rows_of(jnp.minimum(i + 1, BLOCKS - 1))
            new_below = []
            for n in range(2 * MOVE):
                side, j = divmod(n, MOVE)
                g = arrived_ground[side, 0, j, blk, :]
                up = pltpu.roll(arrived_ground[side, 0, j, nxt, :], 7, 0)
                rise = jnp.where(sub == 7, up, pltpu.roll(g, 7, 0)) - g
                back = pltpu.roll(rise, 1, 0)
                new_below.append(back)
                across_x = pltpu.roll(g, TILE - 1, 1) - pltpu.roll(g, 1, 1)
                slopes[side, j, 0, blk, :] = (0.5 * GRAVITY) * across_x
                slopes[side, j, 1, blk, :] = (0.5 * GRAVITY) * (
                    rise + jnp.where(sub == 0, below[n], back)
                )
            return tuple(new_below)

        lax.fori_loop(0, BLOCKS, block, (zero,) * (2 * MOVE), unroll=2)

    def arrived_sides(j):
        def derive(i, _):
            blk = rows_of(i)
            for side in range(2):
                h, mx, my = (U[TPD + side * MOVE + j, q, blk, :] for q in range(3))
                inv, c = derived(h, mx, my)
                u, au = wave(h, mx, inv, c)
                v, av = wave(h, my, inv, c)
                still = (0.5 * GRAVITY) * h * h
                DA[side, 0, blk, :] = au
                DA[side, 1, blk, :] = av
                DA[side, 2, blk, :] = mx * u + still
                DA[side, 3, blk, :] = mx * v
                DA[side, 4, blk, :] = my * v + still
            return 0


        def block(i, below):
            blk = rows_of(i)
            nxt = rows_of(jnp.minimum(i + 1, BLOCKS - 1))
            new_below = []
            for side in range(2):
                old = below[4 * side : 4 * side + 4]
                h, mx, my, hd = (U[TPD + side * MOVE + j, q, blk, :] for q in range(4))
                g = arrived_ground[side, 0, j, blk, :]
                au, av, fxx, fxy, fyy = (DA[side, n, blk, :] for n in range(5))
                he, me_, ye, de, ae, xe, ce = (
                    pltpu.roll(value, TILE - 1, 1) for value in (h, mx, my, hd, au, fxx, fxy)
                )
                speed = jnp.maximum(au, ae)
                east_faces = (
                    (mx + me_) - speed * (he - h),
                    (fxx + xe) - speed * (me_ - mx),
                    (fxy + ce) - speed * (ye - my),
                    de - hd,
                )
                x0, x1, x2, x3 = (f - pltpu.roll(f, 1, 1) for f in east_faces)
                kx, ky = (slopes[side, j, n, blk, :] for n in range(2))
                ups = [U[TPD + side * MOVE + j, q, nxt, :] for q in range(4)]
                ups += [DA[side, n, nxt, :] for n in (1, 3, 4)]
                hn, xn, mn, dn, an, cn, yn = (
                    jnp.where(sub == 7, pltpu.roll(b, 7, 0), pltpu.roll(a, 7, 0))
                    for a, b in zip((h, mx, my, hd, av, fxy, fyy), ups)
                )
                speed = jnp.maximum(av, an)
                faces = (
                    (my + mn) - speed * (hn - h),
                    (fyy + yn) - speed * (mn - my),
                    (fxy + cn) - speed * (xn - mx),
                    dn - hd,
                )
                rounds = [pltpu.roll(f, 1, 0) for f in faces]
                lower = [jnp.where(sub == 0, b, a) for a, b in zip(rounds, old)]
                new_below.extend(rounds)
                y0, y1, y2, y3 = (n - s for n, s in zip(faces, lower))
                seep = arrived_ground[side, 1, j, blk, :] * (h + g - hd)
                R[TPD + side * MOVE + j, 0, blk, :] = -0.5 * (x0 + y0) - seep
                R[TPD + side * MOVE + j, 1, blk, :] = -0.5 * (x1 + y2) - h * kx
                R[TPD + side * MOVE + j, 2, blk, :] = -0.5 * (x2 + y1) - h * ky
                R[TPD + side * MOVE + j, 3, blk, :] = (
                    arrived_ground[side, 2, j, blk, :] * (x3 + y3) + seep * (1.0 / STORAGE)
                )
            return tuple(new_below)

        below = (zero,) * 8
        for piece, (tile, start, count) in enumerate(PIECES):
            if tile != j:
                continue
            for copy in fields_of(piece):
                copy.wait_recv()
            lo, hi = start // 8, (start + count) // 8
            whole = hi - (hi - lo) % 4
            lax.fori_loop(lo, whole, derive, 0, unroll=4)
            for i in range(whole, hi):
                derive(i, 0)
            first = lo - 1 if lo else 0
            last = hi - 1 if hi < BLOCKS else BLOCKS
            below = lax.fori_loop(first, last, block, below, unroll=4)

    def body(step, _):
        send(step)

        @pl.when(step == 0)
        def _():
            for load in late:
                load.wait()
            for side in range(2):
                for j in range(MOVE):
                    for kind, array in enumerate((G, L, S)):
                        mover_ground[side, kind, j] = array[leaving[side][j]]

        for copy in grounds(step):
            copy.start()

        @pl.when(step == 0)
        def _():
            ground_slopes()

        right_sides()

        @pl.when(step == 0)
        def _():
            for copy in ground_halos():
                copy.wait_recv()

        rims(step)
        sweep(step + 1, interval(step)[1])
        return 0

    lax.fori_loop(0, STEPS - 1, body, 0)

    final = STEPS - 1
    send_near(final)
    for copy in halos(final):
        copy.start()

    def collect(j):
        for q in range(4):
            for i in range(BLOCKS):
                blk = rows_of(i)
                own = [U[p, q, blk, :] for p in range(TPD)]
                for side in range(2):
                    value = own[0]
                    for p in range(1, TPD):
                        value = jnp.where(leaving[side][j] == p, own[p], value)
                    movers[side, j, q, blk, :] = value

    def send_fields(j):
        for piece in range(len(PIECES)):
            if PIECES[piece][0] == j:
                for copy in fields_of(piece):
                    copy.start()

    collect(0)
    send_fields(0)
    collect(1)
    right_sides()
    send_across(final)
    send_fields(1)
    for kind in range(3):
        for copy in grounds(kind):
            copy.wait_recv()
    arrived_slopes()
    rims(final)
    outer_lines()
    for copy in lines():
        copy.start()
    for j in range(MOVE):
        arrived_sides(j)
    for copy in lines():
        copy.wait_recv()
    dt = interval(final)[0]
    keeps = []
    for k in range(TPD):
        tile = wanted[k]
        dt_k = jnp.where(wanted_wet[k] == 1, dt, 0.0)
        guest = tile >= TPD
        line = jnp.maximum(tile - TPD, 0)
        turned_lane = lax.rem(lane + 1, TILE)
        edge_lane = turned_lane < jnp.where(guest, 2, 0)
        south_row = sub == jnp.where(guest, 0, -1)
        north_row = sub == jnp.where(guest, 7, -1)
        cols = line_got[line, 8:16, :]
        rows = line_got[line, 0:8, :]
        for q in range(4):
            for i in range(BLOCKS):
                blk = rows_of(i)
                rate = R[tile, q, blk, :]
                at = q * BLOCKS + i
                rate = jnp.where(edge_lane, pltpu.roll(cols, TILE - 1 - 2 * at, 1), rate)
                if i == 0:
                    rate = jnp.where(south_row, rows[4 + q : 5 + q, :], rate)
                if i == BLOCKS - 1:
                    rate = jnp.where(north_row, rows[q : q + 1, :], rate)
                made[k, q, blk, :] = U[tile, q, blk, :] + dt_k * rate
        keep = pltpu.make_async_copy(made.at[k], tiles_out.at[k], out_sem.at[k])
        keep.start()
        keeps.append(keep)
    for step in range(STEPS):
        all_rows(step, mx_send, DEVICES if step < final else 8).wait()
        for copy in halos(step):
            copy.wait_send()
    across_rows(0).wait()
    for copy in ground_halos():
        copy.wait_send()
    for kind in range(3):
        for copy in grounds(kind):
            copy.wait_send()
    for piece in range(len(PIECES)):
        for copy in fields_of(piece):
            copy.wait_send()
    for copy in lines():
        copy.wait_send()
    for keep in keeps:
        keep.wait()


def split_kernel(tiles, depth_out, flow_out, head_out, held, in_sem, sem):
    fetches = [
        pltpu.make_async_copy(tiles.at[k], held.at[k], in_sem.at[k]) for k in range(TPD)
    ]
    for fetch in fetches:
        fetch.start()
    copies = []
    for k in range(TPD):
        fetches[k].wait()
        for n, (part, out) in enumerate(
            ((held.at[k, 0], depth_out), (held.at[k, 1:3], flow_out), (held.at[k, 3], head_out))
        ):
            copy = pltpu.make_async_copy(part, out.at[k], sem.at[n, k])
            copy.start()
            copies.append(copy)
    for copy in copies:
        copy.wait()


def shards(depth, velocity, head, terrain, leakance, diffusivity, tile_wet, neighbours, destination):
    hbm = pl.BlockSpec(memory_space=pltpu.HBM)
    smem = pl.BlockSpec(memory_space=pltpu.SMEM)
    vm = lambda *shape: pltpu.VMEM(shape + (TILE,), F32)
    dma = pltpu.SemaphoreType.DMA
    made = pl.pallas_call(
        flood_kernel,
        out_shape=jax.ShapeDtypeStruct((TPD, 4, TILE, TILE), F32),
        in_specs=[smem] * 3 + [hbm] * 6,
        out_specs=hbm,
        scratch_shapes=[
            vm(TPD + 2 * MOVE, 4, TILE), vm(TPD, 5, TILE), vm(TPD + 2 * MOVE, 4, TILE),
            vm(TPD, TILE), vm(TPD, TILE), vm(TPD, TILE), vm(TPD, TILE), vm(TPD, TILE),
            vm(TPD, 2, TILE), vm(STEPS, DEVICES), vm(16),
            vm(STEPS, 2, 8), vm(STEPS, 2, 8), vm(STEPS, 2, 16), vm(STEPS, 2, 16), vm(2, 8), vm(2, 8),
            vm(2, MOVE, 4, TILE), vm(2, 3, MOVE, TILE), vm(2, 3, MOVE, TILE), vm(2, MOVE, 2, TILE),
            vm(2, 5, TILE), vm(2 * MOVE, 16), vm(2 * MOVE, 16), vm(TPD, 4, TILE),
            dma((6, TPD)), dma((STEPS,)), dma((STEPS,)), dma((2,)),
            dma((STEPS, 2)), dma((STEPS, 2)), dma((STEPS, 2)), dma((STEPS, 2)), dma((2,)), dma((2,)),
            dma((2, 3)), dma((2, 3)), dma((2, 3)), dma((2, 3)), dma((2,)), dma((2,)),
            dma((TPD,)),
        ],
        compiler_params=pltpu.CompilerParams(
            collective_id=0, has_side_effects=True, vmem_limit_bytes=60 << 20
        ),
    )(tile_wet, neighbours.T, destination, depth, velocity, head, terrain, leakance, diffusivity)
    tile = jax.ShapeDtypeStruct((TPD, TILE, TILE), F32)
    return pl.pallas_call(
        split_kernel,
        out_shape=(tile, jax.ShapeDtypeStruct((TPD, 2, TILE, TILE), F32), tile),
        in_specs=[hbm],
        out_specs=(hbm,) * 3,
        scratch_shapes=[vm(TPD, 4, TILE), dma((TPD,)), dma((3, TPD))],
    )(made)


def solution(mesh):
    tiles = P("tiles", None, None)
    pair = P("tiles", None, None, None)
    return jax.shard_map(
        shards,
        mesh=mesh,
        in_specs=(tiles, pair, tiles, tiles, tiles, tiles, P(), P(), P()),
        out_specs=(tiles, pair, tiles),
        check_vma=False,
    )
```
